32 devices in a mesh: rep: 2 (over y), tp: 16 (over z, x, core).
Axes of the slice: x: 2, y: 2, z: 4, core: 2. Of those that a mesh axis runs over, the one named last changes fastest.
Arguments:
- tokens: bfloat16 [64, 8192], P('rep', 'tp'), parts along dimension 0, may hold values from -6 to 6
- attention_gain: bfloat16 [8192], replicated, may hold values from 0.5 to 1.5
- forward_gain: bfloat16 [8192], replicated, may hold values from 0.5 to 1.5
- query_weight: bfloat16 [8192, 8192], P(None, 'tp'), may hold values from -0.0625 to 0.0625
- key_matrix: bfloat16 [8192, 1024], P(None, 'tp'), may hold values from -0.0625 to 0.0625
- value_matrix: bfloat16 [8192, 1024], P(None, 'tp'), may hold values from -0.0625 to 0.0625
- output_weight: bfloat16 [8192, 8192], P('tp'), may hold values from -0.0625 to 0.0625
- gate_weight: bfloat16 [8192, 16384], P(None, 'tp'), may hold values from -0.0625 to 0.0625
- up_weight: bfloat16 [8192, 16384], P(None, 'tp'), may hold values from -0.0625 to 0.0625
- down_weight: bfloat16 [16384, 8192], P('tp'), may hold values from -0.046875 to 0.046875
- adapter_inputs: bfloat16 [32, 8192, 32], P(('rep', 'tp')), parts along dimension 0, may hold values from -0.0625 to 0.0625
- adapter_query: bfloat16 [32, 16, 8192], P('rep', None, 'tp'), parts along dimension 0, may hold values from -0.8984375 to 0.8984375
- adapter_upper: bfloat16 [32, 16, 16384], P('rep', None, 'tp'), parts along dimension 0, may hold values from -0.8984375 to 0.8984375
- adapter_place: int32 [32], P('rep'), parts along dimension 0, may hold values from 0 to 15, each once
- request_adapter: int32 [2], P('rep'), parts along dimension 0, may hold values from 0 to 15
- tree_parents: int32 [2, 32], P('rep'), parts along dimension 0, may hold values from 0 to 30, as said below
Outputs:
- layer_output: bfloat16 [64, 8192], P('rep', 'tp'), parts along dimension 0
The draws below stay inside these ranges and needn't reach their ends.
There are 2 independent parts, one for each index of `rep`. The reference program is written for one: setup_inputs(seed, part) draws one part's arguments, and reference() takes and returns one part's arrays. A program takes and returns all parts, laid end to end along the dimension named above; an argument that names none is the same for every part. Nothing has to cross between parts.
Inputs may be any that keep to these rules, and one draw needn't show every extreme that they name: tree_parents[r, 0] = 0 and tree_parents[r, i] < i for i >= 1: each request's tokens form one tree rooted at its first token; in request 0 the last token's parent is token 30. `adapter_place`: a permutation of the pool rows. `request_adapter`: an adapter number for each request.
All inputs are finite; a program needn't handle non-finite values.
Results may differ from the reference program's by a relative error of at most 0.013.
Values may be sent and summed in bfloat16 or wider, within the bound.
No kernel may reach another device: no remote copies, remote signals or barrier semaphores. Data moves between devices by JAX's collectives and lax.ppermute only.
A program may use at most 192 MiB of HBM per device.

```python
import math
import jax
import jax.numpy as jnp
import numpy as np
from jax import lax

MODEL_WIDTH = 8192
QUERY_HEADS = 64
KEY_VALUE_HEADS = 8
HEAD_SIZE = 128
FF = 16384
R = 16
TREE = 32
REQS = 1
TOKENS = 32
ADAPTERS = 16


def draw_tree_parents(key, part):
    key = jax.random.fold_in(key, 7)
    places = jnp.arange(TREE, dtype=jnp.int32)
    limit = jnp.maximum(places, 1)
    picks = jax.random.randint(key, (REQS, TREE), 0, limit[None, :])
    picks = jnp.where(places[None, :] == 0, 0, picks)
    request_rows = jnp.arange(REQS, dtype=jnp.int32)[:, None]
    fixed_last = (request_rows == 0) & (places[None, :] == TREE - 1)
    return jnp.where(fixed_last, TREE - 2, picks).astype(jnp.int32)


def levels(key, shape, pieces, low, high):
    def one(dim, blocks):
        heights = jax.random.uniform(jax.random.fold_in(jax.random.fold_in(key, 6), dim), (blocks,), jnp.float32, low / len(pieces), high / len(pieces))
        return jnp.repeat(jnp.exp(heights), shape[dim] // blocks).reshape((-1,) + (1,) * (len(shape) - dim - 1))

    loudness = one(*pieces[0])
    for cut in pieces[1:]:
        loudness = loudness * one(*cut)
    return loudness


def cumulative_ranks(count, lean):
    portions = [(1 << 20) // math.isqrt(grade ** lean) + 1 for grade in range(1, count + 1)]
    deviation = 1 + sum(portions) // (1 << 30)
    return np.cumsum(np.array([max(1, weight // deviation) for weight in portions]))


def ranked_ids(rng, extent, count, lean):
    grid = cumulative_ranks(count, lean)
    pick = jax.random.randint(jax.random.fold_in(rng, 1), extent, 0, int(grid[count - 1]))
    grade = jnp.searchsorted(jnp.asarray(grid, jnp.int32), pick, side="right")
    return jax.random.permutation(jax.random.fold_in(rng, 2), count)[grade].astype(jnp.int32)


def gaussian(key, shape, spread, bound, shards=(), kind=jnp.bfloat16):
    entries = spread * jax.random.normal(key, shape, jnp.float32)
    if shards:
        entries = entries * levels(key, shape, shards, -0.22, 0.18)
    return jnp.clip(entries, -bound, bound).astype(kind)


def setup_inputs(seed: int = 0, part: int = 0) -> dict:
    streams_of = jax.random.split(jax.random.key(seed), 17)
    part_keys = jax.random.split(jax.random.fold_in(streams_of[16], part), 17)
    tokens = gaussian(part_keys[0], (TOKENS, MODEL_WIDTH), 1.0, 6.0, ((1, 16),))
    attention_gain = jnp.clip(1.0 + 0.1 * jax.random.normal(streams_of[1], (MODEL_WIDTH,), jnp.float32), 0.5, 1.5).astype(jnp.bfloat16)
    forward_gain = jnp.clip(1.0 + 0.1 * jax.random.normal(streams_of[2], (MODEL_WIDTH,), jnp.float32), 0.5, 1.5).astype(jnp.bfloat16)
    query_weight = gaussian(streams_of[3], (MODEL_WIDTH, QUERY_HEADS * HEAD_SIZE), MODEL_WIDTH ** -0.5, 0.0625, ((1, 16),))
    key_matrix = gaussian(streams_of[4], (MODEL_WIDTH, KEY_VALUE_HEADS * HEAD_SIZE), MODEL_WIDTH ** -0.5, 0.0625, ((1, 16),))
    value_matrix = gaussian(streams_of[5], (MODEL_WIDTH, KEY_VALUE_HEADS * HEAD_SIZE), MODEL_WIDTH ** -0.5, 0.0625, ((1, 16),))
    output_weight = gaussian(streams_of[6], (QUERY_HEADS * HEAD_SIZE, MODEL_WIDTH), (QUERY_HEADS * HEAD_SIZE) ** -0.5, 0.0625, ((0, 16),))
    gate_weight = gaussian(streams_of[7], (MODEL_WIDTH, FF), MODEL_WIDTH ** -0.5, 0.0625, ((1, 16),))
    up_weight = gaussian(streams_of[8], (MODEL_WIDTH, FF), MODEL_WIDTH ** -0.5, 0.0625, ((1, 16),))
    down_weight = gaussian(streams_of[9], (FF, MODEL_WIDTH), FF ** -0.5, 0.046875, ((0, 16),))
    adapter_inputs = gaussian(part_keys[10], (ADAPTERS, MODEL_WIDTH, 2 * R), MODEL_WIDTH ** -0.5, 0.0625, ((0, 16),))
    adapter_query = gaussian(part_keys[11], (ADAPTERS, R, QUERY_HEADS * HEAD_SIZE), 0.15, 0.8984375, ((2, 16),))
    adapter_upper = gaussian(part_keys[12], (ADAPTERS, R, FF), 0.15, 0.8984375, ((2, 16),))
    adapter_place = jax.random.permutation(part_keys[13], ADAPTERS).astype(jnp.int32)
    request_adapter = ranked_ids(part_keys[14], (REQS,), ADAPTERS, 2)
    tree_parents = draw_tree_parents(jax.random.fold_in(jax.random.fold_in(streams_of[16], part), 71), part)
    return {"tokens": tokens, "attention_gain": attention_gain, "forward_gain": forward_gain, "query_weight": query_weight, "key_matrix": key_matrix, "value_matrix": value_matrix, "output_weight": output_weight, "gate_weight": gate_weight, "up_weight": up_weight, "down_weight": down_weight, "adapter_inputs": adapter_inputs, "adapter_query": adapter_query, "adapter_upper": adapter_upper, "adapter_place": adapter_place, "request_adapter": request_adapter, "tree_parents": tree_parents}


EPS = 1e-05
ROPE_BASE = 500000.0

def rms_scale(rows, gain):
    wide = rows.astype(jnp.float32)
    mean_sq = lax.optimization_barrier(jnp.mean(wide * wide, axis=-1, keepdims=True))
    return (wide * lax.rsqrt(mean_sq + EPS) * gain.astype(jnp.float32)).astype(jnp.bfloat16)

def ancestry(parents):
    tree_width = parents.shape[-1]
    places = jnp.arange(tree_width, dtype=jnp.int32)
    links = (parents[:, :, None] == places[None, None, :]).astype(jnp.float32)
    reach = jnp.maximum(links, jnp.eye(tree_width, dtype=jnp.float32)[None])
    for step in range(int(tree_width).bit_length()):
        reach = jnp.minimum(jnp.einsum('rij,rjk->rik', reach, reach, precision=lax.Precision.HIGHEST), 1.0)
    tree_depth = lax.optimization_barrier(jnp.sum(reach, axis=-1)) - 1.0
    return (reach, tree_depth)

def apply_rotary(heads, tree_depth):
    half = heads.shape[-1] // 2
    freq = ROPE_BASE ** (-jnp.arange(half, dtype=jnp.float32) * 2.0 / heads.shape[-1])
    angle = tree_depth[:, :, None] * freq[None, None, :]
    cosine = jnp.cos(angle)[:, :, None, :]
    sine = jnp.sin(angle)[:, :, None, :]
    wide = heads.astype(jnp.float32)
    first = wide[..., :half]
    second = wide[..., half:]
    return jnp.concatenate([first * cosine - second * sine, second * cosine + first * sine], axis=-1).astype(jnp.bfloat16)

def reference(tokens, attention_gain, forward_gain, query_weight, key_matrix, value_matrix, output_weight, gate_weight, up_weight, down_weight, adapter_inputs, adapter_query, adapter_upper, adapter_place, request_adapter, tree_parents):
    rows = tokens.shape[0]
    request_list = request_adapter.shape[0]
    tree_width = rows // request_list
    rank = adapter_query.shape[1]
    normed = rms_scale(tokens, attention_gain)
    slots = adapter_place[request_adapter]
    factors = adapter_inputs[slots].astype(jnp.float32)
    grouped = normed.reshape(request_list, tree_width, -1).astype(jnp.float32)
    low_query = jnp.einsum('rtd,rdk->rtk', grouped, factors[:, :, :rank]).astype(jnp.bfloat16)
    lift = jnp.einsum('rtk,rkc->rtc', low_query.astype(jnp.float32), adapter_query[request_adapter].astype(jnp.float32))
    query = (jnp.dot(normed, query_weight, preferred_element_type=jnp.float32) + lift.reshape(rows, -1)).astype(jnp.bfloat16)
    key_rows = jnp.dot(normed, key_matrix, preferred_element_type=jnp.float32).astype(jnp.bfloat16)
    value_rows = jnp.dot(normed, value_matrix, preferred_element_type=jnp.float32).astype(jnp.bfloat16)
    reach, tree_depth = ancestry(tree_parents)
    query_rotated = apply_rotary(query.reshape(request_list, tree_width, QUERY_HEADS, HEAD_SIZE), tree_depth)
    key_rotated = apply_rotary(key_rows.reshape(request_list, tree_width, KEY_VALUE_HEADS, HEAD_SIZE), tree_depth)
    query_grouped = query_rotated.reshape(request_list, tree_width, KEY_VALUE_HEADS, QUERY_HEADS // KEY_VALUE_HEADS, HEAD_SIZE).astype(jnp.float32)
    scores = jnp.einsum('rqgmd,rkgd->rgmqk', query_grouped, key_rotated.astype(jnp.float32)) * HEAD_SIZE ** (-0.5)
    weights = jnp.exp(scores) * reach[:, None, None, :, :]
    probs = (weights / lax.optimization_barrier(jnp.sum(weights, axis=-1, keepdims=True))).astype(jnp.bfloat16)
    heads_value = value_rows.reshape(request_list, tree_width, KEY_VALUE_HEADS, HEAD_SIZE).astype(jnp.float32)
    mixed = jnp.einsum('rgmqk,rkgd->rqgmd', probs.astype(jnp.float32), heads_value).astype(jnp.bfloat16)
    mixed = mixed.reshape(rows, QUERY_HEADS * HEAD_SIZE)
    attended = jnp.dot(mixed, output_weight, preferred_element_type=jnp.float32)
    hidden = (tokens.astype(jnp.float32) + attended).astype(jnp.bfloat16)
    normed_two = rms_scale(hidden, forward_gain)
    grouped_two = normed_two.reshape(request_list, tree_width, -1).astype(jnp.float32)
    low_up = jnp.einsum('rtd,rdk->rtk', grouped_two, factors[:, :, rank:]).astype(jnp.bfloat16)
    lift_up = jnp.einsum('rtk,rkc->rtc', low_up.astype(jnp.float32), adapter_upper[request_adapter].astype(jnp.float32))
    gate = jnp.dot(normed_two, gate_weight, preferred_element_type=jnp.float32)
    upper = jnp.dot(normed_two, up_weight, preferred_element_type=jnp.float32) + lift_up.reshape(rows, -1)
    active = (jax.nn.silu(gate) * upper).astype(jnp.bfloat16)
    forward = jnp.dot(active, down_weight, preferred_element_type=jnp.float32)
    return (hidden.astype(jnp.float32) + forward).astype(jnp.bfloat16)
```

```python
import jax
import jax.numpy as jnp
from jax import lax
from jax.sharding import PartitionSpec as P

HEAD_SIZE = 128


EPS = 1e-05
ROPE_BASE = 500000.0


def core_groups(axis):
    count = lax.axis_size(axis)
    return [list(range(core, count, 2)) for core in range(2)]


def exchange(blocks, axis):
    return lax.all_to_all(
        blocks, axis, 0, 0, axis_index_groups=core_groups(axis), tiled=True
    )


def by_core(mine, theirs, core):
    even = jnp.where(core == 0, mine, theirs)
    odd = jnp.where(core == 0, theirs, mine)
    return jnp.stack([even, odd], axis=1)


def gather_features(part, axis):
    chips = lax.axis_size(axis) // 2
    core = lax.axis_index(axis) & 1
    mine = exchange(jnp.broadcast_to(part[None], (chips,) + part.shape), axis)
    theirs = partner_2(mine, axis, 0)
    both = by_core(mine, theirs, core).reshape((2 * chips,) + part.shape)
    return jnp.moveaxis(both, 0, 1).reshape(part.shape[0], -1)


def sum_features(partial, axis):
    count = lax.axis_size(axis)
    core = lax.axis_index(axis) & 1
    rows = partial.shape[0]
    split = partial.reshape(rows, count // 2, 2, -1)
    even = split[:, :, 0]
    odd = split[:, :, 1]
    mine = jnp.where(core == 0, even, odd)
    theirs = jnp.where(core == 0, odd, even).astype(jnp.bfloat16)
    pair = (mine + partner_2(theirs, axis, 0).astype(jnp.float32)).astype(jnp.bfloat16)
    got = exchange(jnp.moveaxis(pair, 1, 0), axis)
    return jnp.sum(got.astype(jnp.float32), axis=0)


def from_owner(mine, owner, axis):
    core = lax.axis_index(axis) & 1
    held = jnp.where(lax.axis_index(axis) == owner, mine, jnp.zeros_like(mine))
    held = held + partner_2(held, axis, 0)
    chips = lax.axis_size(axis) // 2
    got = exchange(jnp.broadcast_to(held[None], (chips,) + held.shape), axis)
    return lax.dynamic_index_in_dim(got, owner >> 1, 0, keepdims=False)


def partner_2(block, axis, distance):
    count = lax.axis_size(axis)
    route = []
    for low in range(count):
        high = low | 1 << distance
        if high != low and high < count:
            route += [(low, high), (high, low)]
    return lax.ppermute(block, axis, route)


def rms_scale(rows, gain):
    wide = rows.astype(jnp.float32)
    mean_sq = jnp.mean(wide * wide, axis=-1, keepdims=True)
    return (wide * lax.rsqrt(mean_sq + EPS) * gain.astype(jnp.float32)).astype(jnp.bfloat16)


def ancestry(parents):
    tree_width = parents.shape[-1]
    places = jnp.arange(tree_width, dtype=jnp.int32)
    links = (parents[:, :, None] == places[None, None, :]).astype(jnp.float32)
    reach = jnp.maximum(links, jnp.eye(tree_width, dtype=jnp.float32)[None])
    for step in range(int(tree_width).bit_length()):
        reach = jnp.minimum(
            jnp.einsum("rij,rjk->rik", reach, reach, precision=lax.Precision.HIGHEST), 1.0
        )
    tree_depth = jnp.sum(reach, axis=-1) - 1.0
    return (reach, tree_depth)


def apply_rotary(heads, tree_depth):
    half = heads.shape[-1] // 2
    freq = ROPE_BASE ** (-jnp.arange(half, dtype=jnp.float32) * 2.0 / heads.shape[-1])
    angle = tree_depth[:, :, None] * freq[None, None, :]
    cosine = jnp.cos(angle)[:, :, None, :]
    sine = jnp.sin(angle)[:, :, None, :]
    wide = heads.astype(jnp.float32)
    first = wide[..., :half]
    second = wide[..., half:]
    return jnp.concatenate(
        [first * cosine - second * sine, second * cosine + first * sine], axis=-1
    ).astype(jnp.bfloat16)


def join_pair(mine, theirs, flag):
    lower = jnp.concatenate([mine, theirs], axis=1)
    upper = jnp.concatenate([theirs, mine], axis=1)
    return jnp.where(flag == 1, upper, lower)


def body(
    tokens,
    attention_gain,
    forward_gain,
    query_weight,
    key_matrix,
    value_matrix,
    output_weight,
    gate_weight,
    up_weight,
    down_weight,
    adapter_inputs,
    adapter_query,
    adapter_upper,
    adapter_place,
    request_adapter,
    tree_parents,
):
    device = lax.axis_index("tp")
    rows = tokens.shape[0]
    request_list = request_adapter.shape[0]
    tree_width = rows // request_list
    rank = adapter_query.shape[1]
    pool_local = adapter_inputs.shape[0]
    head = HEAD_SIZE
    full_tokens = gather_features(tokens, "tp")
    normed = rms_scale(full_tokens, attention_gain)
    slots = adapter_place[request_adapter]
    owner = slots[0] // pool_local
    factors = lax.dynamic_index_in_dim(adapter_inputs, slots[0] % pool_local, 0, keepdims=False)
    low_held = jnp.dot(normed, factors[:, :rank], preferred_element_type=jnp.float32).astype(
        jnp.bfloat16
    )
    low_query = from_owner(low_held, owner, "tp")[None]
    lift = jnp.einsum(
        "rtk,rkc->rtc",
        low_query,
        adapter_query[request_adapter],
        preferred_element_type=jnp.float32,
    )
    query_local = (
        jnp.dot(normed, query_weight, preferred_element_type=jnp.float32) + lift.reshape(rows, -1)
    ).astype(jnp.bfloat16)
    key_local = jnp.dot(normed, key_matrix, preferred_element_type=jnp.float32).astype(jnp.bfloat16)
    value_local = jnp.dot(normed, value_matrix, preferred_element_type=jnp.float32).astype(
        jnp.bfloat16
    )
    query_cols = query_weight.shape[1]
    query_steps = max(0, (head // query_cols).bit_length() - 1)
    key_steps = (head // key_matrix.shape[1]).bit_length() - 1
    for bit in range(key_steps):
        flag = device >> bit & 1
        key_width = key_local.shape[1]
        with_query = bit < query_steps
        if with_query:
            query_width = query_local.shape[1]
            packed = jnp.concatenate([query_local, key_local, value_local], axis=1)
        else:
            query_width = 0
            packed = jnp.concatenate([key_local, value_local], axis=1)
        partner = partner_2(packed, "tp", bit)
        if with_query:
            query_local = join_pair(query_local, partner[:, :query_width], flag)
        key_other = partner[:, query_width : query_width + key_width]
        value_other = partner[:, query_width + key_width :]
        key_local = join_pair(key_local, key_other, flag)
        value_local = join_pair(value_local, value_other, flag)
    reach, tree_depth = ancestry(tree_parents)
    local_heads = query_local.shape[1] // head
    query_rotated = apply_rotary(
        query_local.reshape(request_list, tree_width, local_heads, head), tree_depth
    )
    key_rotated = apply_rotary(key_local.reshape(request_list, tree_width, 1, head), tree_depth)[
        :, :, 0, :
    ]
    heads_value = value_local.reshape(request_list, tree_width, head)
    scores = jnp.einsum(
        "rqhd,rkd->rhqk", query_rotated, key_rotated, preferred_element_type=jnp.float32
    ) * head ** (-0.5)
    weights = jnp.exp(scores) * reach[:, None, :, :]
    probs = (weights / jnp.sum(weights, axis=-1, keepdims=True)).astype(jnp.bfloat16)
    mixed = jnp.einsum(
        "rhqk,rkd->rqhd", probs, heads_value, preferred_element_type=jnp.float32
    ).astype(jnp.bfloat16)
    mixed = mixed.reshape(rows, local_heads * head)
    offset = (device & (1 << query_steps) - 1) * query_cols
    own_mixed = lax.dynamic_slice_in_dim(mixed, offset, query_cols, 1)
    partial_out = jnp.dot(own_mixed, output_weight, preferred_element_type=jnp.float32)
    summed = sum_features(partial_out, "tp")
    hidden = (tokens.astype(jnp.float32) + summed).astype(jnp.bfloat16)
    hidden_full = gather_features(hidden, "tp")
    normed_two = rms_scale(hidden_full, forward_gain)
    low_held_two = jnp.dot(normed_two, factors[:, rank:], preferred_element_type=jnp.float32).astype(
        jnp.bfloat16
    )
    low_up = from_owner(low_held_two, owner, "tp")[None]
    lift_up = jnp.einsum(
        "rtk,rkc->rtc", low_up, adapter_upper[request_adapter], preferred_element_type=jnp.float32
    )
    gate = jnp.dot(normed_two, gate_weight, preferred_element_type=jnp.float32)
    upper = jnp.dot(normed_two, up_weight, preferred_element_type=jnp.float32) + lift_up.reshape(
        rows, -1
    )
    active = (jax.nn.silu(gate) * upper).astype(jnp.bfloat16)
    forward = jnp.dot(active, down_weight, preferred_element_type=jnp.float32)
    forward_part = sum_features(forward, "tp")
    return (hidden.astype(jnp.float32) + forward_part).astype(jnp.bfloat16)


def solution(mesh):
    return jax.shard_map(
        body,
        mesh=mesh,
        in_specs=(
            P("rep", "tp"),
            P(),
            P(),
            P(None, "tp"),
            P(None, "tp"),
            P(None, "tp"),
            P("tp", None),
            P(None, "tp"),
            P(None, "tp"),
            P("tp", None),
            P(("rep", "tp"), None, None),
            P("rep", None, "tp"),
            P("rep", None, "tp"),
            P("rep"),
            P("rep"),
            P("rep", None),
        ),
        out_specs=P("rep", "tp"),
        check_vma=False,
    )
```

```python
import jax
import jax.numpy as jnp
import numpy as np
from jax import lax
from jax.experimental import pallas as pl
from jax.experimental.pallas import tpu as pltpu
from jax.sharding import PartitionSpec as P

HEAD_SIZE = 128


EPS = 1e-05
ROPE_BASE = 500000.0


def core_groups(axis):
    count = lax.axis_size(axis)
    return [list(range(core, count, 2)) for core in range(2)]


def exchange(blocks, axis):
    return lax.all_to_all(
        blocks, axis, 0, 0, axis_index_groups=core_groups(axis), tiled=True
    )


def by_core(mine, theirs, core):
    even = jnp.where(core == 0, mine, theirs)
    odd = jnp.where(core == 0, theirs, mine)
    return jnp.stack([even, odd], axis=1)


def gather_features(part, axis):
    chips = lax.axis_size(axis) // 2
    core = lax.axis_index(axis) & 1
    mine = exchange(jnp.broadcast_to(part[None], (chips,) + part.shape), axis)
    theirs = partner_2(mine, axis, 0)
    both = by_core(mine, theirs, core).reshape((2 * chips,) + part.shape)
    return jnp.moveaxis(both, 0, 1).reshape(part.shape[0], -1)


def sum_features(partial, axis):
    count = lax.axis_size(axis)
    core = lax.axis_index(axis) & 1
    rows = partial.shape[0]
    split = partial.reshape(rows, count // 2, 2, -1)
    even = split[:, :, 0]
    odd = split[:, :, 1]
    mine = jnp.where(core == 0, even, odd)
    theirs = jnp.where(core == 0, odd, even).astype(jnp.bfloat16)
    pair = (mine + partner_2(theirs, axis, 0).astype(jnp.float32)).astype(jnp.bfloat16)
    got = exchange(jnp.moveaxis(pair, 1, 0), axis)
    return jnp.sum(got.astype(jnp.float32), axis=0)


def from_owner(mine, owner, axis):
    core = lax.axis_index(axis) & 1
    held = jnp.where(lax.axis_index(axis) == owner, mine, jnp.zeros_like(mine))
    held = held + partner_2(held, axis, 0)
    chips = lax.axis_size(axis) // 2
    got = exchange(jnp.broadcast_to(held[None], (chips,) + held.shape), axis)
    return lax.dynamic_index_in_dim(got, owner >> 1, 0, keepdims=False)


def partner_2(block, axis, distance):
    count = lax.axis_size(axis)
    route = []
    for low in range(count):
        high = low | 1 << distance
        if high != low and high < count:
            route += [(low, high), (high, low)]
    return lax.ppermute(block, axis, route)


def rms_scale(rows, gain):
    wide = rows.astype(jnp.float32)
    mean_sq = jnp.mean(wide * wide, axis=-1, keepdims=True)
    return (wide * lax.rsqrt(mean_sq + EPS) * gain.astype(jnp.float32)).astype(jnp.bfloat16)


def ancestry(parents):
    tree_width = parents.shape[-1]
    places = jnp.arange(tree_width, dtype=jnp.int32)
    links = (parents[:, :, None] == places[None, None, :]).astype(jnp.float32)
    reach = jnp.maximum(links, jnp.eye(tree_width, dtype=jnp.float32)[None])
    for step in range(int(tree_width).bit_length()):
        reach = jnp.minimum(
            jnp.einsum("rij,rjk->rik", reach, reach, precision=lax.Precision.HIGHEST), 1.0
        )
    tree_depth = jnp.sum(reach, axis=-1) - 1.0
    return (reach, tree_depth)


def apply_rotary(heads, tree_depth):
    half = heads.shape[-1] // 2
    freq = ROPE_BASE ** (-jnp.arange(half, dtype=jnp.float32) * 2.0 / heads.shape[-1])
    angle = tree_depth[:, :, None] * freq[None, None, :]
    cosine = jnp.cos(angle)[:, :, None, :]
    sine = jnp.sin(angle)[:, :, None, :]
    wide = heads.astype(jnp.float32)
    first = wide[..., :half]
    second = wide[..., half:]
    return jnp.concatenate(
        [first * cosine - second * sine, second * cosine + first * sine], axis=-1
    ).astype(jnp.bfloat16)


def join_pair(mine, theirs, flag):
    lower = jnp.concatenate([mine, theirs], axis=1)
    upper = jnp.concatenate([theirs, mine], axis=1)
    return jnp.where(flag == 1, upper, lower)


def general_body(
    tokens,
    attention_gain,
    forward_gain,
    query_weight,
    key_matrix,
    value_matrix,
    output_weight,
    gate_weight,
    up_weight,
    down_weight,
    adapter_inputs,
    adapter_query,
    adapter_upper,
    adapter_place,
    request_adapter,
    tree_parents,
):
    device = lax.axis_index("tp")
    rows = tokens.shape[0]
    request_list = request_adapter.shape[0]
    tree_width = rows // request_list
    rank = adapter_query.shape[1]
    pool_local = adapter_inputs.shape[0]
    head = HEAD_SIZE
    full_tokens = gather_features(tokens, "tp")
    normed = rms_scale(full_tokens, attention_gain)
    slots = adapter_place[request_adapter]
    owner = slots[0] // pool_local
    factors = lax.dynamic_index_in_dim(adapter_inputs, slots[0] % pool_local, 0, keepdims=False)
    low_held = jnp.dot(normed, factors[:, :rank], preferred_element_type=jnp.float32).astype(
        jnp.bfloat16
    )
    low_query = from_owner(low_held, owner, "tp")[None]
    lift = jnp.einsum(
        "rtk,rkc->rtc",
        low_query,
        adapter_query[request_adapter],
        preferred_element_type=jnp.float32,
    )
    query_local = (
        jnp.dot(normed, query_weight, preferred_element_type=jnp.float32) + lift.reshape(rows, -1)
    ).astype(jnp.bfloat16)
    key_local = jnp.dot(normed, key_matrix, preferred_element_type=jnp.float32).astype(jnp.bfloat16)
    value_local = jnp.dot(normed, value_matrix, preferred_element_type=jnp.float32).astype(
        jnp.bfloat16
    )
    query_cols = query_weight.shape[1]
    query_steps = max(0, (head // query_cols).bit_length() - 1)
    key_steps = (head // key_matrix.shape[1]).bit_length() - 1
    for bit in range(key_steps):
        flag = device >> bit & 1
        key_width = key_local.shape[1]
        with_query = bit < query_steps
        if with_query:
            query_width = query_local.shape[1]
            packed = jnp.concatenate([query_local, key_local, value_local], axis=1)
        else:
            query_width = 0
            packed = jnp.concatenate([key_local, value_local], axis=1)
        partner = partner_2(packed, "tp", bit)
        if with_query:
            query_local = join_pair(query_local, partner[:, :query_width], flag)
        key_other = partner[:, query_width : query_width + key_width]
        value_other = partner[:, query_width + key_width :]
        key_local = join_pair(key_local, key_other, flag)
        value_local = join_pair(value_local, value_other, flag)
    reach, tree_depth = ancestry(tree_parents)
    local_heads = query_local.shape[1] // head
    query_rotated = apply_rotary(
        query_local.reshape(request_list, tree_width, local_heads, head), tree_depth
    )
    key_rotated = apply_rotary(key_local.reshape(request_list, tree_width, 1, head), tree_depth)[
        :, :, 0, :
    ]
    heads_value = value_local.reshape(request_list, tree_width, head)
    scores = jnp.einsum(
        "rqhd,rkd->rhqk", query_rotated, key_rotated, preferred_element_type=jnp.float32
    ) * head ** (-0.5)
    weights = jnp.exp(scores) * reach[:, None, :, :]
    probs = (weights / jnp.sum(weights, axis=-1, keepdims=True)).astype(jnp.bfloat16)
    mixed = jnp.einsum(
        "rhqk,rkd->rqhd", probs, heads_value, preferred_element_type=jnp.float32
    ).astype(jnp.bfloat16)
    mixed = mixed.reshape(rows, local_heads * head)
    offset = (device & (1 << query_steps) - 1) * query_cols
    own_mixed = lax.dynamic_slice_in_dim(mixed, offset, query_cols, 1)
    partial_out = jnp.dot(own_mixed, output_weight, preferred_element_type=jnp.float32)
    summed = sum_features(partial_out, "tp")
    hidden = (tokens.astype(jnp.float32) + summed).astype(jnp.bfloat16)
    hidden_full = gather_features(hidden, "tp")
    normed_two = rms_scale(hidden_full, forward_gain)
    low_held_two = jnp.dot(normed_two, factors[:, rank:], preferred_element_type=jnp.float32).astype(
        jnp.bfloat16
    )
    low_up = from_owner(low_held_two, owner, "tp")[None]
    lift_up = jnp.einsum(
        "rtk,rkc->rtc", low_up, adapter_upper[request_adapter], preferred_element_type=jnp.float32
    )
    gate = jnp.dot(normed_two, gate_weight, preferred_element_type=jnp.float32)
    upper = jnp.dot(normed_two, up_weight, preferred_element_type=jnp.float32) + lift_up.reshape(
        rows, -1
    )
    active = (jax.nn.silu(gate) * upper).astype(jnp.bfloat16)
    forward = jnp.dot(active, down_weight, preferred_element_type=jnp.float32)
    forward_part = sum_features(forward, "tp")
    return (hidden.astype(jnp.float32) + forward_part).astype(jnp.bfloat16)


VMEM = pltpu.VMEM
WHOLE = pl.BlockSpec(memory_space=pltpu.VMEM)
SCALAR = pl.BlockSpec(memory_space=pltpu.SMEM)
FAR = pl.BlockSpec(memory_space=pltpu.HBM)
ROW_DOT = (((1,), (1,)), ((), ()))
LANES = 128
CHUNK = 1024


def dot(a, b):
    return jnp.dot(a, b, preferred_element_type=jnp.float32)


def dot_rows(a, b):
    return lax.dot_general(a, b, ROW_DOT, preferred_element_type=jnp.float32)


def call(kernel, name, outs, args, weights=(), ahead=(), scratch=(), limit=6):
    outs = tuple(VMEM(o.shape, o.dtype) for o in outs)
    size = sum(w.size for w in weights)

    def run(*refs):
        kernel(*refs[: len(args) + len(weights)], *refs[len(args) + len(weights) + len(ahead) :])

    return pl.pallas_call(
        run,
        out_shape=outs,
        in_specs=[WHOLE] * (len(args) + len(weights)) + [FAR] * len(ahead),
        out_specs=(WHOLE,) * len(outs),
        scratch_shapes=list(scratch),
        name=name,
        cost_estimate=pl.CostEstimate(
            flops=64 * size, bytes_accessed=2 * size, transcendentals=0
        ),
        compiler_params=pltpu.CompilerParams(vmem_limit_bytes=limit << 20),
    )(
        *args,
        *[pltpu.with_memory_space_constraint(w, VMEM) for w in weights],
        *[pltpu.with_memory_space_constraint(w, pltpu.HBM) for w in ahead],
    )


def stage(tokens, gains, lifts, parents, place, request, ahead, chips):
    rows, cols = tokens.shape
    outs = (
        VMEM((chips, rows, cols), tokens.dtype),
        VMEM(tokens.shape, tokens.dtype),
        *[VMEM(g.shape, g.dtype) for g in gains],
        *[VMEM(a.shape[1:], a.dtype) for a in lifts],
        VMEM(parents.shape, parents.dtype),
        VMEM((8, LANES), jnp.int32),
    )
    count = len(outs) - 1 + chips - 1

    def kernel(place_ref, request_ref, *refs):
        ins, outs, sem = refs[:6], refs[6 + len(ahead) : -1], refs[-1]
        token_ref, parent_ref = ins[0], ins[5]
        pairs = [(token_ref, outs[0].at[chip]) for chip in range(chips)]
        pairs += [(token_ref, outs[1])]
        pairs += [(ins[1], outs[2]), (ins[2], outs[3])]
        pairs += [(ins[k].at[request_ref[0]], outs[k + 1]) for k in (3, 4)]
        pairs += [(parent_ref, outs[6])]
        copies = [
            pltpu.make_async_copy(src, dst, sem.at[k]) for k, (src, dst) in enumerate(pairs)
        ]
        for copy in copies:
            copy.start()
        outs[7][...] = jnp.full(outs[7].shape, place_ref[request_ref[0]], jnp.int32)
        for copy in copies:
            copy.wait()

    args = (tokens, *gains, *lifts, parents, *ahead)
    return pl.pallas_call(
        kernel,
        out_shape=outs,
        in_specs=[SCALAR] * 2 + [FAR] * len(args),
        out_specs=(WHOLE,) * len(outs),
        scratch_shapes=[pltpu.SemaphoreType.DMA((count + 1,))],
        name="stage",
        compiler_params=pltpu.CompilerParams(vmem_limit_bytes=2 << 20),
    )(place, request, *[pltpu.with_memory_space_constraint(a, pltpu.HBM) for a in args])


def dot_chunks(left, weight_ref):
    depth = weight_ref.shape[0]
    step = min(depth, CHUNK)
    total = dot(left[:, :step], weight_ref[:step, :])
    for at in range(step, depth, step):
        total = total + dot(left[:, at : at + step], weight_ref[at : at + step, :])
    return total


def gain_block(gain_ref, index, cols):
    count = cols // LANES
    lines = [gain_ref[index * count + j : index * count + j + 1, :] for j in range(count)]
    return jnp.concatenate([line.astype(jnp.float32) for line in lines], axis=1)


def core_index():
    return lax.axis_index("tp") & 1


def in_order(mine, theirs, flag):
    mine = mine.astype(jnp.float32)
    theirs = theirs.astype(jnp.float32)
    return jnp.where(flag, mine, theirs), jnp.where(flag, theirs, mine)


def norm_blocks(mine_ref, theirs_ref, gain_ref, scratch, cols):
    chips = mine_ref.shape[0]
    first = core_index() == 0
    squares = jnp.zeros((mine_ref.shape[1], cols), jnp.float32)
    for chip in range(chips):
        for ref in (mine_ref, theirs_ref):
            wide = ref[chip, :, :cols].astype(jnp.float32)
            squares = squares + wide * wide
    mean_sq = jnp.sum(squares, axis=-1, keepdims=True) / (2 * chips * cols)
    scale = lax.rsqrt(mean_sq + EPS)
    for chip in range(chips):
        pair = in_order(mine_ref[chip, :, :cols], theirs_ref[chip, :, :cols], first)
        for side in range(2):
            low = (2 * chip + side) * cols
            gain = gain_block(gain_ref, 2 * chip + side, cols)
            scratch[:, low : low + cols] = (pair[side] * scale * gain).astype(jnp.bfloat16)
    return scale


def project_kernel(
    mine_ref, theirs_ref, gain_ref, query_ref, key_ref, value_ref, factor_ref,
    query_out, pair_out, payload_out, scratch,
):
    chips, rows, cols = mine_ref.shape
    norm_blocks(mine_ref, theirs_ref, gain_ref, scratch, cols)
    normed = scratch[...]
    rank = factor_ref.shape[0] // 2
    low = dot_rows(normed, factor_ref[:rank, :])
    query_out[...] = dot_chunks(normed, query_ref)
    half = key_ref.shape[0]
    pair_out[:, :half] = dot_rows(normed, key_ref[...]).astype(jnp.bfloat16)
    pair_out[:, half:] = dot_rows(normed, value_ref[...]).astype(jnp.bfloat16)
    padded = jnp.concatenate([low, jnp.zeros((rows, LANES - rank), jnp.float32)], axis=1)
    padded = padded.astype(jnp.bfloat16)
    for chip in range(chips):
        for side in range(2):
            at = (2 * chip + side) * cols
            payload_out[chip, side * rank : (side + 1) * rank, :cols] = factor_ref[
                rank:, at : at + cols
            ]
        payload_out[chip, :, cols:] = padded


def pick_kernel(owner_ref, got_ref, out_ref):
    owner = owner_ref[:1, :1] - core_index()
    piece = jnp.zeros(out_ref.shape, jnp.float32)
    for chip in range(got_ref.shape[0]):
        piece = piece + jnp.where(owner == 2 * chip, got_ref[chip].astype(jnp.float32), 0.0)
    out_ref[...] = piece.astype(jnp.bfloat16)


def joined(mine_ref, theirs_ref):
    return mine_ref[...].astype(jnp.float32) + theirs_ref[...].astype(jnp.float32)


def split_product(left, weight_ref, mine_out, theirs_out):
    chips, _, cols = mine_out.shape
    core = core_index()
    for chip in range(chips):
        at = pl.multiple_of((2 * chip + 1 - core) * cols, cols)
        theirs_out[chip] = dot(left, weight_ref[:, pl.ds(at, cols)]).astype(jnp.bfloat16)
        at = pl.multiple_of((2 * chip + core) * cols, cols)
        mine_out[chip] = dot(left, weight_ref[:, pl.ds(at, cols)])


def attend_kernel(
    query_ref, pair_mine, pair_theirs, piece_mine, piece_theirs,
    lift_ref, parent_ref, freq_ref, output_ref, mine_out, theirs_out,
):
    rows, query_cols = query_ref.shape
    head = HEAD_SIZE
    heads = query_cols // head
    half = head // 2
    rank = lift_ref.shape[0]
    first = core_index() == 0
    own = lax.broadcasted_iota(jnp.int32, (rows, rows), 0)
    other = lax.broadcasted_iota(jnp.int32, (rows, rows), 1)
    eye = jnp.where(own == other, 1.0, 0.0)
    links = jnp.where(parent_ref[...] == own, 1.0, 0.0)
    reach = dot_rows(eye.astype(jnp.bfloat16), jnp.maximum(links, eye).astype(jnp.bfloat16))
    for _ in range((rows - 1).bit_length()):
        square = reach.astype(jnp.bfloat16)
        reach = jnp.minimum(dot(square, square), 1.0)
    angle = (jnp.sum(reach, axis=-1, keepdims=True) - 1.0) * freq_ref[...]
    lane = lax.broadcasted_iota(jnp.int32, (rows, head), 1)
    cosine = jnp.cos(angle)
    sine = jnp.sin(angle)
    sine = jnp.where(lane < half, -sine, sine)

    def rotate(wide):
        return (wide * cosine + pltpu.roll(wide, half, 1) * sine).astype(jnp.bfloat16)

    even, odd = in_order(pair_mine[...], pair_theirs[...], first)
    key = rotate(jnp.where(lane < half, even, pltpu.roll(odd, half, 1)))
    value = jnp.where(lane < half, pltpu.roll(even, half, 1), odd).astype(jnp.bfloat16)
    piece = joined(piece_mine, piece_theirs)
    cols = piece.shape[1] - LANES
    low = piece[:, cols : cols + rank].astype(jnp.bfloat16)
    query = query_ref[...] + dot(low, lift_ref[...])
    query = query.astype(jnp.bfloat16).astype(jnp.float32)
    stacked = jnp.concatenate(
        [rotate(query[:, h * head : (h + 1) * head]) for h in range(heads)], axis=0
    )
    scores = dot_rows(stacked, key) * head ** (-0.5)
    weights = jnp.exp(scores) * jnp.concatenate([reach] * heads, axis=0)
    probs = (weights / jnp.sum(weights, axis=-1, keepdims=True)).astype(jnp.bfloat16)
    mixed = dot(probs, value).astype(jnp.bfloat16)
    mixed = jnp.concatenate([mixed[h * rows : (h + 1) * rows] for h in range(heads)], axis=1)
    split_product(mixed, output_ref, mine_out, theirs_out)


def hidden_kernel(
    got_ref, token_ref, gain_ref, piece_mine, piece_theirs,
    hidden_out, payload_out,
):
    chips, rows, cols = got_ref.shape
    total = token_ref[...].astype(jnp.float32)
    added = got_ref[0].astype(jnp.float32)
    for chip in range(1, chips):
        added = added + got_ref[chip].astype(jnp.float32)
    hidden = (total + added).astype(jnp.bfloat16)
    hidden_out[...] = hidden
    piece = joined(piece_mine, piece_theirs)
    rank = piece.shape[0] // 2
    factor = jnp.where(core_index() == 0, piece[:rank, :cols], piece[rank:, :cols])
    device = lax.axis_index("tp")
    gain = gain_block(gain_ref, 0, cols)
    for index in range(1, 2 * chips):
        gain = jnp.where(device == index, gain_block(gain_ref, index, cols), gain)
    gained = hidden.astype(jnp.float32) * gain
    low = dot_rows(gained.astype(jnp.bfloat16), factor.astype(jnp.bfloat16))
    padded = jnp.concatenate([low, jnp.zeros((rows, LANES - rank), jnp.float32)], axis=1)
    padded = padded.astype(jnp.bfloat16)
    for chip in range(chips):
        payload_out[chip, :, :cols] = hidden
        payload_out[chip, :, cols:] = padded


def forward_kernel(
    mine_ref, theirs_ref, gain_ref, lift_ref, gate_ref, up_ref, active_out, scratch,
):
    cols = mine_ref.shape[2] - LANES
    rank = lift_ref.shape[0]
    scale = norm_blocks(mine_ref, theirs_ref, gain_ref, scratch, cols)
    low = jnp.zeros((mine_ref.shape[1], LANES), jnp.float32)
    for chip in range(mine_ref.shape[0]):
        for ref in (mine_ref, theirs_ref):
            low = low + ref[chip, :, cols:].astype(jnp.float32)
    low = (low * scale)[:, :rank].astype(jnp.bfloat16)
    normed = scratch[...]
    gate = dot_chunks(normed, gate_ref)
    upper = dot_chunks(normed, up_ref) + dot(low, lift_ref[...])
    active_out[...] = (gate * jax.nn.sigmoid(gate) * upper).astype(jnp.bfloat16)


def down_kernel(active_ref, down_ref, mine_out, theirs_out):
    split_product(active_ref[...], down_ref, mine_out, theirs_out)


def fast_body(
    tokens,
    attention_gain,
    forward_gain,
    query_weight,
    key_matrix,
    value_matrix,
    output_weight,
    gate_weight,
    up_weight,
    down_weight,
    adapter_inputs,
    adapter_query,
    adapter_upper,
    adapter_place,
    request_adapter,
    tree_parents,
):
    rows, cols = tokens.shape
    chips = lax.axis_size("tp") // 2
    width = query_weight.shape[0]
    half = HEAD_SIZE // 2
    freq = ROPE_BASE ** (-np.arange(half, dtype=np.float32) * np.float32(2.0 / HEAD_SIZE))
    freq = jnp.asarray(np.concatenate([freq, freq])[None].astype(np.float32))
    shape = jax.ShapeDtypeStruct
    bf16, f32 = jnp.bfloat16, jnp.float32
    attention_gain = attention_gain.reshape(-1, LANES)
    forward_gain = forward_gain.reshape(-1, LANES)
    wide = cols + LANES
    split_out = (shape((chips, rows, cols), f32), shape((chips, rows, cols), bf16))

    heavy = (gate_weight, up_weight, down_weight)
    spread, kept_tokens, gain_one, gain_two, query_lift, up_lift, parents, owner = stage(
        tokens,
        (attention_gain, forward_gain),
        (adapter_query, adapter_upper),
        tree_parents,
        adapter_place,
        request_adapter,
        heavy,
        chips,
    )
    mine = exchange(spread, "tp")
    theirs = partner_2(mine, "tp", 0)
    query, pair, payload = call(
        project_kernel,
        "project",
        (
            shape((rows, query_weight.shape[1]), f32),
            shape((rows, 2 * key_matrix.shape[1]), bf16),
            shape((chips, rows, wide), bf16),
        ),
        (mine, theirs, gain_one),
        (query_weight, key_matrix.T, value_matrix.T, adapter_inputs[0].T),
        heavy,
        [VMEM((rows, width), bf16)],
    )
    pair_theirs = partner_2(pair, "tp", 0)
    got = exchange(payload, "tp")
    (piece,) = call(pick_kernel, "pick", (shape((rows, wide), bf16),), (owner, got), (), heavy)
    piece_theirs = partner_2(piece, "tp", 0)
    kept, sent = call(
        attend_kernel,
        "attend",
        split_out,
        (query, pair, pair_theirs, piece, piece_theirs, query_lift, parents, freq),
        (output_weight,),
        heavy,
    )
    chip_sum = (kept + partner_2(sent, "tp", 0).astype(f32)).astype(bf16)
    hidden, payload = call(
        hidden_kernel,
        "hidden",
        (shape((rows, cols), bf16), shape((chips, rows, wide), bf16)),
        (exchange(chip_sum, "tp"), kept_tokens, gain_two, piece, piece_theirs),
        (),
        heavy,
    )
    mine = exchange(payload, "tp")
    theirs = partner_2(mine, "tp", 0)
    (active,) = call(
        forward_kernel,
        "forward",
        (shape((rows, gate_weight.shape[1]), bf16),),
        (mine, theirs, gain_two, up_lift),
        (gate_weight, up_weight),
        (query_weight, output_weight, down_weight),
        [VMEM((rows, width), bf16)],
    )
    kept, sent = call(down_kernel, "down", split_out, (active,), (down_weight,))
    chip_sum = (kept + partner_2(sent, "tp", 0).astype(f32)).astype(bf16)
    added = jnp.sum(exchange(chip_sum, "tp").astype(f32), axis=0)
    return (hidden.astype(f32) + added).astype(bf16)


def body(*args):
    tokens, key_matrix, query_weight = args[0], args[4], args[3]
    fits = (
        tokens.shape[1] % LANES == 0
        and query_weight.shape[1] % HEAD_SIZE == 0
        and key_matrix.shape[1] * 2 == HEAD_SIZE
        and args[10].shape[0] == 1
        and args[14].shape[0] == 1
        and args[10].shape[2] == tokens.shape[0]
    )
    return fast_body(*args) if fits else general_body(*args)


def solution(mesh):
    return jax.shard_map(
        body,
        mesh=mesh,
        in_specs=(
            P("rep", "tp"),
            P(),
            P(),
            P(None, "tp"),
            P(None, "tp"),
            P(None, "tp"),
            P("tp", None),
            P(None, "tp"),
            P(None, "tp"),
            P("tp", None),
            P(("rep", "tp"), None, None),
            P("rep", None, "tp"),
            P("rep", None, "tp"),
            P("rep"),
            P("rep"),
            P("rep", None),
        ),
        out_specs=P("rep", "tp"),
        check_vma=False,
    )
```

```python
import jax
import jax.numpy as jnp
import numpy as np
from jax import lax
from jax.experimental import pallas as pl
from jax.experimental.pallas import tpu as pltpu
from jax.sharding import PartitionSpec as P

HEAD_SIZE = 128


EPS = 1e-05
ROPE_BASE = 500000.0


def core_groups(axis):
    count = lax.axis_size(axis)
    return [list(range(core, count, 2)) for core in range(2)]


def exchange(blocks, axis):
    return lax.all_to_all(
        blocks, axis, 0, 0, axis_index_groups=core_groups(axis), tiled=True
    )


def by_core(mine, theirs, core):
    even = jnp.where(core == 0, mine, theirs)
    odd = jnp.where(core == 0, theirs, mine)
    return jnp.stack([even, odd], axis=1)


def gather_features(part, axis):
    chips = lax.axis_size(axis) // 2
    core = lax.axis_index(axis) & 1
    mine = exchange(jnp.broadcast_to(part[None], (chips,) + part.shape), axis)
    theirs = partner_2(mine, axis, 0)
    both = by_core(mine, theirs, core).reshape((2 * chips,) + part.shape)
    return jnp.moveaxis(both, 0, 1).reshape(part.shape[0], -1)


def sum_features(partial, axis):
    count = lax.axis_size(axis)
    core = lax.axis_index(axis) & 1
    rows = partial.shape[0]
    split = partial.reshape(rows, count // 2, 2, -1)
    even = split[:, :, 0]
    odd = split[:, :, 1]
    mine = jnp.where(core == 0, even, odd)
    theirs = jnp.where(core == 0, odd, even).astype(jnp.bfloat16)
    pair = (mine + partner_2(theirs, axis, 0).astype(jnp.float32)).astype(jnp.bfloat16)
    got = exchange(jnp.moveaxis(pair, 1, 0), axis)
    return jnp.sum(got.astype(jnp.float32), axis=0)


def from_owner(mine, owner, axis):
    core = lax.axis_index(axis) & 1
    held = jnp.where(lax.axis_index(axis) == owner, mine, jnp.zeros_like(mine))
    held = held + partner_2(held, axis, 0)
    chips = lax.axis_size(axis) // 2
    got = exchange(jnp.broadcast_to(held[None], (chips,) + held.shape), axis)
    return lax.dynamic_index_in_dim(got, owner >> 1, 0, keepdims=False)


def partner_2(block, axis, distance):
    count = lax.axis_size(axis)
    route = []
    for low in range(count):
        high = low | 1 << distance
        if high != low and high < count:
            route += [(low, high), (high, low)]
    return lax.ppermute(block, axis, route)


def rms_scale(rows, gain):
    wide = rows.astype(jnp.float32)
    mean_sq = jnp.mean(wide * wide, axis=-1, keepdims=True)
    return (wide * lax.rsqrt(mean_sq + EPS) * gain.astype(jnp.float32)).astype(jnp.bfloat16)


def ancestry(parents):
    tree_width = parents.shape[-1]
    places = jnp.arange(tree_width, dtype=jnp.int32)
    links = (parents[:, :, None] == places[None, None, :]).astype(jnp.float32)
    reach = jnp.maximum(links, jnp.eye(tree_width, dtype=jnp.float32)[None])
    for step in range(int(tree_width).bit_length()):
        reach = jnp.minimum(
            jnp.einsum("rij,rjk->rik", reach, reach, precision=lax.Precision.HIGHEST), 1.0
        )
    tree_depth = jnp.sum(reach, axis=-1) - 1.0
    return (reach, tree_depth)


def apply_rotary(heads, tree_depth):
    half = heads.shape[-1] // 2
    freq = ROPE_BASE ** (-jnp.arange(half, dtype=jnp.float32) * 2.0 / heads.shape[-1])
    angle = tree_depth[:, :, None] * freq[None, None, :]
    cosine = jnp.cos(angle)[:, :, None, :]
    sine = jnp.sin(angle)[:, :, None, :]
    wide = heads.astype(jnp.float32)
    first = wide[..., :half]
    second = wide[..., half:]
    return jnp.concatenate(
        [first * cosine - second * sine, second * cosine + first * sine], axis=-1
    ).astype(jnp.bfloat16)


def join_pair(mine, theirs, flag):
    lower = jnp.concatenate([mine, theirs], axis=1)
    upper = jnp.concatenate([theirs, mine], axis=1)
    return jnp.where(flag == 1, upper, lower)


def general_body(
    tokens,
    attention_gain,
    forward_gain,
    query_weight,
    key_matrix,
    value_matrix,
    output_weight,
    gate_weight,
    up_weight,
    down_weight,
    adapter_inputs,
    adapter_query,
    adapter_upper,
    adapter_place,
    request_adapter,
    tree_parents,
):
    device = lax.axis_index("tp")
    rows = tokens.shape[0]
    request_list = request_adapter.shape[0]
    tree_width = rows // request_list
    rank = adapter_query.shape[1]
    pool_local = adapter_inputs.shape[0]
    head = HEAD_SIZE
    full_tokens = gather_features(tokens, "tp")
    normed = rms_scale(full_tokens, attention_gain)
    slots = adapter_place[request_adapter]
    owner = slots[0] // pool_local
    factors = lax.dynamic_index_in_dim(adapter_inputs, slots[0] % pool_local, 0, keepdims=False)
    low_held = jnp.dot(normed, factors[:, :rank], preferred_element_type=jnp.float32).astype(
        jnp.bfloat16
    )
    low_query = from_owner(low_held, owner, "tp")[None]
    lift = jnp.einsum(
        "rtk,rkc->rtc",
        low_query,
        adapter_query[request_adapter],
        preferred_element_type=jnp.float32,
    )
    query_local = (
        jnp.dot(normed, query_weight, preferred_element_type=jnp.float32) + lift.reshape(rows, -1)
    ).astype(jnp.bfloat16)
    key_local = jnp.dot(normed, key_matrix, preferred_element_type=jnp.float32).astype(jnp.bfloat16)
    value_local = jnp.dot(normed, value_matrix, preferred_element_type=jnp.float32).astype(
        jnp.bfloat16
    )
    query_cols = query_weight.shape[1]
    query_steps = max(0, (head // query_cols).bit_length() - 1)
    key_steps = (head // key_matrix.shape[1]).bit_length() - 1
    for bit in range(key_steps):
        flag = device >> bit & 1
        key_width = key_local.shape[1]
        with_query = bit < query_steps
        if with_query:
            query_width = query_local.shape[1]
            packed = jnp.concatenate([query_local, key_local, value_local], axis=1)
        else:
            query_width = 0
            packed = jnp.concatenate([key_local, value_local], axis=1)
        partner = partner_2(packed, "tp", bit)
        if with_query:
            query_local = join_pair(query_local, partner[:, :query_width], flag)
        key_other = partner[:, query_width : query_width + key_width]
        value_other = partner[:, query_width + key_width :]
        key_local = join_pair(key_local, key_other, flag)
        value_local = join_pair(value_local, value_other, flag)
    reach, tree_depth = ancestry(tree_parents)
    local_heads = query_local.shape[1] // head
    query_rotated = apply_rotary(
        query_local.reshape(request_list, tree_width, local_heads, head), tree_depth
    )
    key_rotated = apply_rotary(key_local.reshape(request_list, tree_width, 1, head), tree_depth)[
        :, :, 0, :
    ]
    heads_value = value_local.reshape(request_list, tree_width, head)
    scores = jnp.einsum(
        "rqhd,rkd->rhqk", query_rotated, key_rotated, preferred_element_type=jnp.float32
    ) * head ** (-0.5)
    weights = jnp.exp(scores) * reach[:, None, :, :]
    probs = (weights / jnp.sum(weights, axis=-1, keepdims=True)).astype(jnp.bfloat16)
    mixed = jnp.einsum(
        "rhqk,rkd->rqhd", probs, heads_value, preferred_element_type=jnp.float32
    ).astype(jnp.bfloat16)
    mixed = mixed.reshape(rows, local_heads * head)
    offset = (device & (1 << query_steps) - 1) * query_cols
    own_mixed = lax.dynamic_slice_in_dim(mixed, offset, query_cols, 1)
    partial_out = jnp.dot(own_mixed, output_weight, preferred_element_type=jnp.float32)
    summed = sum_features(partial_out, "tp")
    hidden = (tokens.astype(jnp.float32) + summed).astype(jnp.bfloat16)
    hidden_full = gather_features(hidden, "tp")
    normed_two = rms_scale(hidden_full, forward_gain)
    low_held_two = jnp.dot(normed_two, factors[:, rank:], preferred_element_type=jnp.float32).astype(
        jnp.bfloat16
    )
    low_up = from_owner(low_held_two, owner, "tp")[None]
    lift_up = jnp.einsum(
        "rtk,rkc->rtc", low_up, adapter_upper[request_adapter], preferred_element_type=jnp.float32
    )
    gate = jnp.dot(normed_two, gate_weight, preferred_element_type=jnp.float32)
    upper = jnp.dot(normed_two, up_weight, preferred_element_type=jnp.float32) + lift_up.reshape(
        rows, -1
    )
    active = (jax.nn.silu(gate) * upper).astype(jnp.bfloat16)
    forward = jnp.dot(active, down_weight, preferred_element_type=jnp.float32)
    forward_part = sum_features(forward, "tp")
    return (hidden.astype(jnp.float32) + forward_part).astype(jnp.bfloat16)


VMEM = pltpu.VMEM
WHOLE = pl.BlockSpec(memory_space=pltpu.VMEM)
SCALAR = pl.BlockSpec(memory_space=pltpu.SMEM)
FAR = pl.BlockSpec(memory_space=pltpu.HBM)
ROW_DOT = (((1,), (1,)), ((), ()))
LANES = 128
CHUNK = 1024


def dot(a, b):
    return jnp.dot(a, b, preferred_element_type=jnp.float32)


def dot_rows(a, b):
    return lax.dot_general(a, b, ROW_DOT, preferred_element_type=jnp.float32)


def call(kernel, name, outs, args, weights=(), ahead=(), scratch=(), limit=6, far=()):
    outs = tuple(VMEM(o.shape, o.dtype) for o in outs)
    size = sum(w.size for w in weights + far)
    used = len(args) + len(weights) + len(far)

    def run(*refs):
        kernel(*refs[:used], *refs[used + len(ahead) :])

    return pl.pallas_call(
        run,
        out_shape=outs,
        in_specs=[WHOLE] * (len(args) + len(weights)) + [FAR] * len(far + ahead),
        out_specs=(WHOLE,) * len(outs),
        scratch_shapes=list(scratch),
        name=name,
        cost_estimate=pl.CostEstimate(
            flops=64 * size, bytes_accessed=2 * size, transcendentals=0
        ),
        compiler_params=pltpu.CompilerParams(vmem_limit_bytes=limit << 20),
    )(
        *[pltpu.with_memory_space_constraint(w, VMEM) for w in args + weights],
        *[pltpu.with_memory_space_constraint(w, pltpu.HBM) for w in far + ahead],
    )


def stage(tokens, gains, lifts, parents, place, request, ahead, chips):
    rows, cols = tokens.shape
    outs = (
        VMEM((chips, rows, cols), tokens.dtype),
        VMEM(tokens.shape, tokens.dtype),
        *[VMEM(g.shape, g.dtype) for g in gains],
        *[VMEM(a.shape[1:], a.dtype) for a in lifts],
        VMEM(parents.shape, parents.dtype),
        VMEM((8, LANES), jnp.int32),
    )
    count = len(outs) - 1 + chips - 1

    def kernel(place_ref, request_ref, *refs):
        ins, outs, sem = refs[:6], refs[6 + len(ahead) : -1], refs[-1]
        token_ref, parent_ref = ins[0], ins[5]
        pairs = [(token_ref, outs[0].at[chip]) for chip in range(chips)]
        pairs += [(token_ref, outs[1])]
        pairs += [(ins[1], outs[2]), (ins[2], outs[3])]
        pairs += [(ins[k].at[request_ref[0]], outs[k + 1]) for k in (3, 4)]
        pairs += [(parent_ref, outs[6])]
        copies = [
            pltpu.make_async_copy(src, dst, sem.at[k]) for k, (src, dst) in enumerate(pairs)
        ]
        for copy in copies:
            copy.start()
        outs[7][...] = jnp.full(outs[7].shape, place_ref[request_ref[0]], jnp.int32)
        for copy in copies:
            copy.wait()

    args = (tokens, *gains, *lifts, parents, *ahead)
    return pl.pallas_call(
        kernel,
        out_shape=outs,
        in_specs=[SCALAR] * 2 + [FAR] * len(args),
        out_specs=(WHOLE,) * len(outs),
        scratch_shapes=[pltpu.SemaphoreType.DMA((count + 1,))],
        name="stage",
        compiler_params=pltpu.CompilerParams(vmem_limit_bytes=2 << 20),
    )(place, request, *[pltpu.with_memory_space_constraint(a, pltpu.HBM) for a in args])


def dot_chunks(left, weight_ref):
    depth = weight_ref.shape[0]
    step = min(depth, CHUNK)
    total = dot(left[:, :step], weight_ref[:step, :])
    for at in range(step, depth, step):
        total = total + dot(left[:, at : at + step], weight_ref[at : at + step, :])
    return total


def gain_block(gain_ref, index, cols):
    count = cols // LANES
    lines = [gain_ref[index * count + j : index * count + j + 1, :] for j in range(count)]
    return jnp.concatenate([line.astype(jnp.float32) for line in lines], axis=1)


def core_index():
    return lax.axis_index("tp") & 1


def in_order(mine, theirs, flag):
    mine = mine.astype(jnp.float32)
    theirs = theirs.astype(jnp.float32)
    return jnp.where(flag, mine, theirs), jnp.where(flag, theirs, mine)


def norm_blocks(mine_ref, theirs_ref, gain_ref, scratch, cols):
    chips = mine_ref.shape[0]
    first = core_index() == 0
    squares = jnp.zeros((mine_ref.shape[1], cols), jnp.float32)
    for chip in range(chips):
        for ref in (mine_ref, theirs_ref):
            wide = ref[chip, :, :cols].astype(jnp.float32)
            squares = squares + wide * wide
    mean_sq = jnp.sum(squares, axis=-1, keepdims=True) / (2 * chips * cols)
    scale = lax.rsqrt(mean_sq + EPS)
    for chip in range(chips):
        pair = in_order(mine_ref[chip, :, :cols], theirs_ref[chip, :, :cols], first)
        for side in range(2):
            low = (2 * chip + side) * cols
            gain = gain_block(gain_ref, 2 * chip + side, cols)
            scratch[:, low : low + cols] = (pair[side] * scale * gain).astype(jnp.bfloat16)
    return scale


def project_kernel(
    mine_ref, theirs_ref, gain_ref, query_ref, key_ref, value_ref, factor_ref,
    query_out, pair_out, payload_out, scratch,
):
    chips, rows, cols = mine_ref.shape
    norm_blocks(mine_ref, theirs_ref, gain_ref, scratch, cols)
    normed = scratch[...]
    rank = factor_ref.shape[0] // 2
    low = dot_rows(normed, factor_ref[:rank, :])
    query_out[...] = dot_chunks(normed, query_ref)
    half = key_ref.shape[0]
    pair_out[:, :half] = dot_rows(normed, key_ref[...]).astype(jnp.bfloat16)
    pair_out[:, half:] = dot_rows(normed, value_ref[...]).astype(jnp.bfloat16)
    padded = jnp.concatenate([low, jnp.zeros((rows, LANES - rank), jnp.float32)], axis=1)
    padded = padded.astype(jnp.bfloat16)
    for chip in range(chips):
        for side in range(2):
            at = (2 * chip + side) * cols
            payload_out[chip, side * rank : (side + 1) * rank, :cols] = factor_ref[
                rank:, at : at + cols
            ]
        payload_out[chip, :, cols:] = padded


def pick_kernel(owner_ref, got_ref, out_ref):
    owner = owner_ref[:1, :1] - core_index()
    piece = jnp.zeros(out_ref.shape, jnp.float32)
    for chip in range(got_ref.shape[0]):
        piece = piece + jnp.where(owner == 2 * chip, got_ref[chip].astype(jnp.float32), 0.0)
    out_ref[...] = piece.astype(jnp.bfloat16)


def joined(mine_ref, theirs_ref):
    return mine_ref[...].astype(jnp.float32) + theirs_ref[...].astype(jnp.float32)


def split_product(left, weight_ref, mine_out, theirs_out):
    chips, _, cols = mine_out.shape
    core = core_index()
    for chip in range(chips):
        at = pl.multiple_of((2 * chip + 1 - core) * cols, cols)
        theirs_out[chip] = dot(left, weight_ref[:, pl.ds(at, cols)]).astype(jnp.bfloat16)
        at = pl.multiple_of((2 * chip + core) * cols, cols)
        mine_out[chip] = dot(left, weight_ref[:, pl.ds(at, cols)])


def attend_kernel(
    query_ref, pair_mine, pair_theirs, piece_mine, piece_theirs,
    lift_ref, parent_ref, freq_ref, output_ref, mine_out, theirs_out,
):
    rows, query_cols = query_ref.shape
    head = HEAD_SIZE
    heads = query_cols // head
    half = head // 2
    rank = lift_ref.shape[0]
    first = core_index() == 0
    own = lax.broadcasted_iota(jnp.int32, (rows, rows), 0)
    other = lax.broadcasted_iota(jnp.int32, (rows, rows), 1)
    eye = jnp.where(own == other, 1.0, 0.0)
    links = jnp.where(parent_ref[...] == own, 1.0, 0.0)
    reach = dot_rows(eye.astype(jnp.bfloat16), jnp.maximum(links, eye).astype(jnp.bfloat16))
    for _ in range((rows - 1).bit_length()):
        square = reach.astype(jnp.bfloat16)
        reach = jnp.minimum(dot(square, square), 1.0)
    angle = (jnp.sum(reach, axis=-1, keepdims=True) - 1.0) * freq_ref[...]
    lane = lax.broadcasted_iota(jnp.int32, (rows, head), 1)
    cosine = jnp.cos(angle)
    sine = jnp.sin(angle)
    sine = jnp.where(lane < half, -sine, sine)

    def rotate(wide):
        return (wide * cosine + pltpu.roll(wide, half, 1) * sine).astype(jnp.bfloat16)

    even, odd = in_order(pair_mine[...], pair_theirs[...], first)
    key = rotate(jnp.where(lane < half, even, pltpu.roll(odd, half, 1)))
    value = jnp.where(lane < half, pltpu.roll(even, half, 1), odd).astype(jnp.bfloat16)
    piece = joined(piece_mine, piece_theirs)
    cols = piece.shape[1] - LANES
    low = piece[:, cols : cols + rank].astype(jnp.bfloat16)
    query = query_ref[...] + dot(low, lift_ref[...])
    query = query.astype(jnp.bfloat16).astype(jnp.float32)
    stacked = jnp.concatenate(
        [rotate(query[:, h * head : (h + 1) * head]) for h in range(heads)], axis=0
    )
    scores = dot_rows(stacked, key) * head ** (-0.5)
    weights = jnp.exp(scores) * jnp.concatenate([reach] * heads, axis=0)
    probs = (weights / jnp.sum(weights, axis=-1, keepdims=True)).astype(jnp.bfloat16)
    mixed = dot(probs, value).astype(jnp.bfloat16)
    mixed = jnp.concatenate([mixed[h * rows : (h + 1) * rows] for h in range(heads)], axis=1)
    split_product(mixed, output_ref, mine_out, theirs_out)


def hidden_kernel(
    got_ref, token_ref, gain_ref, piece_mine, piece_theirs,
    hidden_out, payload_out,
):
    chips, rows, cols = got_ref.shape
    total = token_ref[...].astype(jnp.float32)
    added = got_ref[0].astype(jnp.float32)
    for chip in range(1, chips):
        added = added + got_ref[chip].astype(jnp.float32)
    hidden = (total + added).astype(jnp.bfloat16)
    hidden_out[...] = hidden
    piece = joined(piece_mine, piece_theirs)
    rank = piece.shape[0] // 2
    factor = jnp.where(core_index() == 0, piece[:rank, :cols], piece[rank:, :cols])
    device = lax.axis_index("tp")
    gain = gain_block(gain_ref, 0, cols)
    for index in range(1, 2 * chips):
        gain = jnp.where(device == index, gain_block(gain_ref, index, cols), gain)
    gained = hidden.astype(jnp.float32) * gain
    low = dot_rows(gained.astype(jnp.bfloat16), factor.astype(jnp.bfloat16))
    padded = jnp.concatenate([low, jnp.zeros((rows, LANES - rank), jnp.float32)], axis=1)
    padded = padded.astype(jnp.bfloat16)
    for chip in range(chips):
        payload_out[chip, :, :cols] = hidden
        payload_out[chip, :, cols:] = padded


def forward_kernel(
    mine_ref, theirs_ref, gain_ref, lift_ref, gate_ref, up_ref, down_ref,
    mine_out, theirs_out, scratch, active, held, sem,
):
    chips = mine_ref.shape[0]
    cols = mine_ref.shape[2] - LANES

    def down_copy(chip):
        part = pl.ds(pl.multiple_of(2 * cols * chip, 2 * cols), 2 * cols)
        return pltpu.make_async_copy(down_ref.at[:, part], held.at[:, part], sem.at[chip])

    @pl.loop(0, chips)
    def _(chip):
        down_copy(chip).start()

    rank = lift_ref.shape[0]
    scale = norm_blocks(mine_ref, theirs_ref, gain_ref, scratch, cols)
    low = jnp.zeros((mine_ref.shape[1], LANES), jnp.float32)
    for chip in range(mine_ref.shape[0]):
        for ref in (mine_ref, theirs_ref):
            low = low + ref[chip, :, cols:].astype(jnp.float32)
    low = (low * scale)[:, :rank].astype(jnp.bfloat16)
    normed = scratch[...]
    gate = dot_chunks(normed, gate_ref)
    upper = dot_chunks(normed, up_ref) + dot(low, lift_ref[...])
    active[...] = (gate * jax.nn.sigmoid(gate) * upper).astype(jnp.bfloat16)
    core = core_index()

    @pl.loop(0, chips)
    def _(chip):
        down_copy(chip).wait()
        for side, out in ((1 - core, theirs_out), (core, mine_out)):
            at = pl.multiple_of((2 * chip + side) * cols, cols)
            out[chip] = dot(active[...], held[:, pl.ds(at, cols)]).astype(out.dtype)


def fast_body(
    tokens,
    attention_gain,
    forward_gain,
    query_weight,
    key_matrix,
    value_matrix,
    output_weight,
    gate_weight,
    up_weight,
    down_weight,
    adapter_inputs,
    adapter_query,
    adapter_upper,
    adapter_place,
    request_adapter,
    tree_parents,
):
    rows, cols = tokens.shape
    chips = lax.axis_size("tp") // 2
    width = query_weight.shape[0]
    half = HEAD_SIZE // 2
    freq = ROPE_BASE ** (-np.arange(half, dtype=np.float32) * np.float32(2.0 / HEAD_SIZE))
    freq = jnp.asarray(np.concatenate([freq, freq])[None].astype(np.float32))
    shape = jax.ShapeDtypeStruct
    bf16, f32 = jnp.bfloat16, jnp.float32
    attention_gain = attention_gain.reshape(-1, LANES)
    forward_gain = forward_gain.reshape(-1, LANES)
    wide = cols + LANES
    split_out = (shape((chips, rows, cols), f32), shape((chips, rows, cols), bf16))

    heavy = (gate_weight, up_weight, down_weight)
    most = heavy + (query_weight, output_weight)
    spread, kept_tokens, gain_one, gain_two, query_lift, up_lift, parents, owner = stage(
        tokens,
        (attention_gain, forward_gain),
        (adapter_query, adapter_upper),
        tree_parents,
        adapter_place,
        request_adapter,
        heavy,
        chips,
    )
    mine = exchange(spread, "tp")
    theirs = partner_2(mine, "tp", 0)
    query, pair, payload = call(
        project_kernel,
        "project",
        (
            shape((rows, query_weight.shape[1]), f32),
            shape((rows, 2 * key_matrix.shape[1]), bf16),
            shape((chips, rows, wide), bf16),
        ),
        (mine, theirs, gain_one),
        (query_weight, key_matrix.T, value_matrix.T, adapter_inputs[0].T),
        heavy,
        [VMEM((rows, width), bf16)],
    )
    pair_theirs = partner_2(pair, "tp", 0)
    got = exchange(payload, "tp")
    (piece,) = call(pick_kernel, "pick", (shape((rows, wide), bf16),), (owner, got), (), most)
    piece_theirs = partner_2(piece, "tp", 0)
    kept, sent = call(
        attend_kernel,
        "attend",
        split_out,
        (query, pair, pair_theirs, piece, piece_theirs, query_lift, parents, freq),
        (output_weight,),
        heavy + (query_weight,),
    )
    chip_sum = (kept + partner_2(sent, "tp", 0).astype(f32)).astype(bf16)
    hidden, payload = call(
        hidden_kernel,
        "hidden",
        (shape((rows, cols), bf16), shape((chips, rows, wide), bf16)),
        (exchange(chip_sum, "tp"), kept_tokens, gain_two, piece, piece_theirs),
        (),
        most,
    )
    mine = exchange(payload, "tp")
    theirs = partner_2(mine, "tp", 0)
    kept, sent = call(
        forward_kernel,
        "forward",
        split_out,
        (mine, theirs, gain_two, up_lift),
        (gate_weight, up_weight),
        (query_weight, output_weight),
        [
            VMEM((rows, width), bf16),
            VMEM((rows, gate_weight.shape[1]), bf16),
            VMEM(down_weight.shape, bf16),
            pltpu.SemaphoreType.DMA((chips,)),
        ],
        far=(down_weight,),
        limit=18,
    )
    chip_sum = (kept + partner_2(sent, "tp", 0).astype(f32)).astype(bf16)
    added = jnp.sum(exchange(chip_sum, "tp").astype(f32), axis=0)
    return (hidden.astype(f32) + added).astype(bf16)


def body(*args):
    tokens, key_matrix, query_weight = args[0], args[4], args[3]
    fits = (
        tokens.shape[1] % LANES == 0
        and query_weight.shape[1] % HEAD_SIZE == 0
        and key_matrix.shape[1] * 2 == HEAD_SIZE
        and args[10].shape[0] == 1
        and args[14].shape[0] == 1
        and args[10].shape[2] == tokens.shape[0]
    )
    return fast_body(*args) if fits else general_body(*args)


def solution(mesh):
    return jax.shard_map(
        body,
        mesh=mesh,
        in_specs=(
            P("rep", "tp"),
            P(),
            P(),
            P(None, "tp"),
            P(None, "tp"),
            P(None, "tp"),
            P("tp", None),
            P(None, "tp"),
            P(None, "tp"),
            P("tp", None),
            P(("rep", "tp"), None, None),
            P("rep", None, "tp"),
            P("rep", None, "tp"),
            P("rep"),
            P("rep"),
            P("rep", None),
        ),
        out_specs=P("rep", "tp"),
        check_vma=False,
    )
```

```python
import jax
import jax.numpy as jnp
import numpy as np
from jax import lax
from jax.experimental import pallas as pl
from jax.experimental.pallas import tpu as pltpu
from jax.sharding import PartitionSpec as P

HEAD_SIZE = 128


EPS = 1e-05
ROPE_BASE = 500000.0


def core_groups(axis):
    count = lax.axis_size(axis)
    return [list(range(core, count, 2)) for core in range(2)]


def exchange(blocks, axis):
    return lax.all_to_all(
        blocks, axis, 0, 0, axis_index_groups=core_groups(axis), tiled=True
    )


def by_core(mine, theirs, core):
    even = jnp.where(core == 0, mine, theirs)
    odd = jnp.where(core == 0, theirs, mine)
    return jnp.stack([even, odd], axis=1)


def gather_features(part, axis):
    chips = lax.axis_size(axis) // 2
    core = lax.axis_index(axis) & 1
    mine = exchange(jnp.broadcast_to(part[None], (chips,) + part.shape), axis)
    theirs = partner_2(mine, axis, 0)
    both = by_core(mine, theirs, core).reshape((2 * chips,) + part.shape)
    return jnp.moveaxis(both, 0, 1).reshape(part.shape[0], -1)


def sum_features(partial, axis):
    count = lax.axis_size(axis)
    core = lax.axis_index(axis) & 1
    rows = partial.shape[0]
    split = partial.reshape(rows, count // 2, 2, -1)
    even = split[:, :, 0]
    odd = split[:, :, 1]
    mine = jnp.where(core == 0, even, odd)
    theirs = jnp.where(core == 0, odd, even).astype(jnp.bfloat16)
    pair = (mine + partner_2(theirs, axis, 0).astype(jnp.float32)).astype(jnp.bfloat16)
    got = exchange(jnp.moveaxis(pair, 1, 0), axis)
    return jnp.sum(got.astype(jnp.float32), axis=0)


def from_owner(mine, owner, axis):
    core = lax.axis_index(axis) & 1
    held = jnp.where(lax.axis_index(axis) == owner, mine, jnp.zeros_like(mine))
    held = held + partner_2(held, axis, 0)
    chips = lax.axis_size(axis) // 2
    got = exchange(jnp.broadcast_to(held[None], (chips,) + held.shape), axis)
    return lax.dynamic_index_in_dim(got, owner >> 1, 0, keepdims=False)


def partner_2(block, axis, distance):
    count = lax.axis_size(axis)
    route = []
    for low in range(count):
        high = low | 1 << distance
        if high != low and high < count:
            route += [(low, high), (high, low)]
    return lax.ppermute(block, axis, route)


def rms_scale(rows, gain):
    wide = rows.astype(jnp.float32)
    mean_sq = jnp.mean(wide * wide, axis=-1, keepdims=True)
    return (wide * lax.rsqrt(mean_sq + EPS) * gain.astype(jnp.float32)).astype(jnp.bfloat16)


def ancestry(parents):
    tree_width = parents.shape[-1]
    places = jnp.arange(tree_width, dtype=jnp.int32)
    links = (parents[:, :, None] == places[None, None, :]).astype(jnp.float32)
    reach = jnp.maximum(links, jnp.eye(tree_width, dtype=jnp.float32)[None])
    for step in range(int(tree_width).bit_length()):
        reach = jnp.minimum(
            jnp.einsum("rij,rjk->rik", reach, reach, precision=lax.Precision.HIGHEST), 1.0
        )
    tree_depth = jnp.sum(reach, axis=-1) - 1.0
    return (reach, tree_depth)


def apply_rotary(heads, tree_depth):
    half = heads.shape[-1] // 2
    freq = ROPE_BASE ** (-jnp.arange(half, dtype=jnp.float32) * 2.0 / heads.shape[-1])
    angle = tree_depth[:, :, None] * freq[None, None, :]
    cosine = jnp.cos(angle)[:, :, None, :]
    sine = jnp.sin(angle)[:, :, None, :]
    wide = heads.astype(jnp.float32)
    first = wide[..., :half]
    second = wide[..., half:]
    return jnp.concatenate(
        [first * cosine - second * sine, second * cosine + first * sine], axis=-1
    ).astype(jnp.bfloat16)


def join_pair(mine, theirs, flag):
    lower = jnp.concatenate([mine, theirs], axis=1)
    upper = jnp.concatenate([theirs, mine], axis=1)
    return jnp.where(flag == 1, upper, lower)


def general_body(
    tokens,
    attention_gain,
    forward_gain,
    query_weight,
    key_matrix,
    value_matrix,
    output_weight,
    gate_weight,
    up_weight,
    down_weight,
    adapter_inputs,
    adapter_query,
    adapter_upper,
    adapter_place,
    request_adapter,
    tree_parents,
):
    device = lax.axis_index("tp")
    rows = tokens.shape[0]
    request_list = request_adapter.shape[0]
    tree_width = rows // request_list
    rank = adapter_query.shape[1]
    pool_local = adapter_inputs.shape[0]
    head = HEAD_SIZE
    full_tokens = gather_features(tokens, "tp")
    normed = rms_scale(full_tokens, attention_gain)
    slots = adapter_place[request_adapter]
    owner = slots[0] // pool_local
    factors = lax.dynamic_index_in_dim(adapter_inputs, slots[0] % pool_local, 0, keepdims=False)
    low_held = jnp.dot(normed, factors[:, :rank], preferred_element_type=jnp.float32).astype(
        jnp.bfloat16
    )
    low_query = from_owner(low_held, owner, "tp")[None]
    lift = jnp.einsum(
        "rtk,rkc->rtc",
        low_query,
        adapter_query[request_adapter],
        preferred_element_type=jnp.float32,
    )
    query_local = (
        jnp.dot(normed, query_weight, preferred_element_type=jnp.float32) + lift.reshape(rows, -1)
    ).astype(jnp.bfloat16)
    key_local = jnp.dot(normed, key_matrix, preferred_element_type=jnp.float32).astype(jnp.bfloat16)
    value_local = jnp.dot(normed, value_matrix, preferred_element_type=jnp.float32).astype(
        jnp.bfloat16
    )
    query_cols = query_weight.shape[1]
    query_steps = max(0, (head // query_cols).bit_length() - 1)
    key_steps = (head // key_matrix.shape[1]).bit_length() - 1
    for bit in range(key_steps):
        flag = device >> bit & 1
        key_width = key_local.shape[1]
        with_query = bit < query_steps
        if with_query:
            query_width = query_local.shape[1]
            packed = jnp.concatenate([query_local, key_local, value_local], axis=1)
        else:
            query_width = 0
            packed = jnp.concatenate([key_local, value_local], axis=1)
        partner = partner_2(packed, "tp", bit)
        if with_query:
            query_local = join_pair(query_local, partner[:, :query_width], flag)
        key_other = partner[:, query_width : query_width + key_width]
        value_other = partner[:, query_width + key_width :]
        key_local = join_pair(key_local, key_other, flag)
        value_local = join_pair(value_local, value_other, flag)
    reach, tree_depth = ancestry(tree_parents)
    local_heads = query_local.shape[1] // head
    query_rotated = apply_rotary(
        query_local.reshape(request_list, tree_width, local_heads, head), tree_depth
    )
    key_rotated = apply_rotary(key_local.reshape(request_list, tree_width, 1, head), tree_depth)[
        :, :, 0, :
    ]
    heads_value = value_local.reshape(request_list, tree_width, head)
    scores = jnp.einsum(
        "rqhd,rkd->rhqk", query_rotated, key_rotated, preferred_element_type=jnp.float32
    ) * head ** (-0.5)
    weights = jnp.exp(scores) * reach[:, None, :, :]
    probs = (weights / jnp.sum(weights, axis=-1, keepdims=True)).astype(jnp.bfloat16)
    mixed = jnp.einsum(
        "rhqk,rkd->rqhd", probs, heads_value, preferred_element_type=jnp.float32
    ).astype(jnp.bfloat16)
    mixed = mixed.reshape(rows, local_heads * head)
    offset = (device & (1 << query_steps) - 1) * query_cols
    own_mixed = lax.dynamic_slice_in_dim(mixed, offset, query_cols, 1)
    partial_out = jnp.dot(own_mixed, output_weight, preferred_element_type=jnp.float32)
    summed = sum_features(partial_out, "tp")
    hidden = (tokens.astype(jnp.float32) + summed).astype(jnp.bfloat16)
    hidden_full = gather_features(hidden, "tp")
    normed_two = rms_scale(hidden_full, forward_gain)
    low_held_two = jnp.dot(normed_two, factors[:, rank:], preferred_element_type=jnp.float32).astype(
        jnp.bfloat16
    )
    low_up = from_owner(low_held_two, owner, "tp")[None]
    lift_up = jnp.einsum(
        "rtk,rkc->rtc", low_up, adapter_upper[request_adapter], preferred_element_type=jnp.float32
    )
    gate = jnp.dot(normed_two, gate_weight, preferred_element_type=jnp.float32)
    upper = jnp.dot(normed_two, up_weight, preferred_element_type=jnp.float32) + lift_up.reshape(
        rows, -1
    )
    active = (jax.nn.silu(gate) * upper).astype(jnp.bfloat16)
    forward = jnp.dot(active, down_weight, preferred_element_type=jnp.float32)
    forward_part = sum_features(forward, "tp")
    return (hidden.astype(jnp.float32) + forward_part).astype(jnp.bfloat16)


VMEM = pltpu.VMEM
WHOLE = pl.BlockSpec(memory_space=pltpu.VMEM)
SCALAR = pl.BlockSpec(memory_space=pltpu.SMEM)
FAR = pl.BlockSpec(memory_space=pltpu.HBM)
ROW_DOT = (((1,), (1,)), ((), ()))
LANES = 128
CHUNK = 1024


def dot(a, b):
    return jnp.dot(a, b, preferred_element_type=jnp.float32)


def dot_rows(a, b):
    return lax.dot_general(a, b, ROW_DOT, preferred_element_type=jnp.float32)


def call(kernel, name, outs, args, weights=(), ahead=(), scratch=(), limit=6, far=()):
    outs = tuple(VMEM(o.shape, o.dtype) for o in outs)
    size = sum(w.size for w in weights + far)
    used = len(args) + len(weights) + len(far)

    def run(*refs):
        kernel(*refs[:used], *refs[used + len(ahead) :])

    return pl.pallas_call(
        run,
        out_shape=outs,
        in_specs=[WHOLE] * (len(args) + len(weights)) + [FAR] * len(far + ahead),
        out_specs=(WHOLE,) * len(outs),
        scratch_shapes=list(scratch),
        name=name,
        cost_estimate=pl.CostEstimate(
            flops=64 * size, bytes_accessed=2 * size, transcendentals=0
        ),
        compiler_params=pltpu.CompilerParams(vmem_limit_bytes=limit << 20),
    )(
        *[pltpu.with_memory_space_constraint(w, VMEM) for w in args + weights],
        *[pltpu.with_memory_space_constraint(w, pltpu.HBM) for w in far + ahead],
    )


def near(x):
    return pltpu.with_memory_space_constraint(x, VMEM)


def distant(x):
    return pltpu.with_memory_space_constraint(x, pltpu.HBM)


def spread(tokens, kept, ahead, chips):
    outs = (VMEM((chips,) + tokens.shape, tokens.dtype),)
    outs += tuple(VMEM(a.shape, a.dtype) for a in (tokens, *kept))
    used = 1 + len(kept)

    def kernel(*refs):
        ins, outs, sem = refs[:used], refs[used + len(ahead) : -1], refs[-1]
        pairs = [(ins[0], outs[0].at[chip]) for chip in range(chips)]
        pairs += [(ins[k], outs[1 + k]) for k in range(used)]
        copies = [
            pltpu.make_async_copy(src, dst, sem.at[k]) for k, (src, dst) in enumerate(pairs)
        ]
        for copy in copies:
            copy.start()
        for copy in copies:
            copy.wait()

    return pl.pallas_call(
        kernel,
        out_shape=outs,
        in_specs=[FAR] * (used + len(ahead)),
        out_specs=(WHOLE,) * len(outs),
        scratch_shapes=[pltpu.SemaphoreType.DMA((chips + used,))],
        name="spread",
        compiler_params=pltpu.CompilerParams(vmem_limit_bytes=2 << 20),
    )(*[distant(a) for a in (tokens, *kept, *ahead)])


def table_kernel(
    request_ref, place_ref, query_ref, up_ref, parent_ref, after_ref,
    query_out, up_out, owner_out, cosine_out, sine_out, reach_out, place, sem,
):
    request = request_ref[0]
    copies = [
        pltpu.make_async_copy(place_ref, place, sem.at[0]),
        pltpu.make_async_copy(query_ref.at[request], query_out, sem.at[1]),
        pltpu.make_async_copy(up_ref.at[request], up_out, sem.at[2]),
    ]
    for copy in copies:
        copy.start()
    rows, head = cosine_out.shape
    half = head // 2
    own = lax.broadcasted_iota(jnp.int32, (rows, rows), 0)
    other = lax.broadcasted_iota(jnp.int32, (rows, rows), 1)
    eye = jnp.where(own == other, 1.0, 0.0)
    links = jnp.where(parent_ref[...] == own, 1.0, 0.0)
    reach = dot_rows(eye.astype(jnp.bfloat16), jnp.maximum(links, eye).astype(jnp.bfloat16))
    for _ in range((rows - 1).bit_length()):
        square = reach.astype(jnp.bfloat16)
        reach = jnp.minimum(dot(square, square), 1.0)
    reach_out[...] = reach
    lane = lax.broadcasted_iota(jnp.int32, (rows, head), 1)
    place_in_half = jnp.where(lane < half, lane, lane - half).astype(jnp.float32)
    freq = jnp.exp(place_in_half * np.float32(-2.0 / head * np.log(ROPE_BASE)))
    angle = (jnp.sum(reach, axis=-1, keepdims=True) - 1.0) * freq
    sine = jnp.sin(angle)
    cosine_out[...] = jnp.cos(angle)
    sine_out[...] = jnp.where(lane < half, -sine, sine)
    for copy in copies:
        copy.wait()
    owner_out[...] = jnp.full(owner_out.shape, place[request], jnp.int32)


def tables(request, place, lifts, parents, after):
    rows = parents.shape[1]
    shapes = [(a.shape[1:], a.dtype) for a in lifts]
    shapes += [((8, LANES), jnp.int32)]
    shapes += [((rows, HEAD_SIZE), jnp.float32)] * 2 + [((rows, rows), jnp.float32)]
    return pl.pallas_call(
        table_kernel,
        out_shape=tuple(VMEM(*a) for a in shapes),
        in_specs=[SCALAR] + [FAR] * 3 + [WHOLE] * 2,
        out_specs=(WHOLE,) * len(shapes),
        scratch_shapes=[
            pltpu.SMEM(place.shape, jnp.int32),
            pltpu.SemaphoreType.DMA((3,)),
        ],
        name="tables",
        compiler_params=pltpu.CompilerParams(vmem_limit_bytes=2 << 20),
    )(request, *[distant(a) for a in (place, *lifts)], near(parents), near(after))


def dot_chunks(left, weight_ref):
    depth = weight_ref.shape[0]
    step = min(depth, CHUNK)
    total = dot(left[:, :step], weight_ref[:step, :])
    for at in range(step, depth, step):
        total = total + dot(left[:, at : at + step], weight_ref[at : at + step, :])
    return total


def gain_block(gain_ref, index, cols):
    count = cols // LANES
    lines = [gain_ref[index * count + j : index * count + j + 1, :] for j in range(count)]
    return jnp.concatenate([line.astype(jnp.float32) for line in lines], axis=1)


def core_index():
    return lax.axis_index("tp") & 1


def in_order(mine, theirs, flag):
    mine = mine.astype(jnp.float32)
    theirs = theirs.astype(jnp.float32)
    return jnp.where(flag, mine, theirs), jnp.where(flag, theirs, mine)


def norm_blocks(mine_ref, theirs_ref, gain_ref, scratch, cols):
    chips = mine_ref.shape[0]
    first = core_index() == 0
    squares = jnp.zeros((mine_ref.shape[1], cols), jnp.float32)
    for chip in range(chips):
        for ref in (mine_ref, theirs_ref):
            wide = ref[chip, :, :cols].astype(jnp.float32)
            squares = squares + wide * wide
    mean_sq = jnp.sum(squares, axis=-1, keepdims=True) / (2 * chips * cols)
    scale = lax.rsqrt(mean_sq + EPS)
    for chip in range(chips):
        pair = in_order(mine_ref[chip, :, :cols], theirs_ref[chip, :, :cols], first)
        for side in range(2):
            low = (2 * chip + side) * cols
            gain = gain_block(gain_ref, 2 * chip + side, cols)
            scratch[:, low : low + cols] = (pair[side] * scale * gain).astype(jnp.bfloat16)
    return scale


def project_kernel(
    mine_ref, theirs_ref, gain_ref, owner_ref, other_ref, query_ref, key_ref, value_ref,
    factor_ref, query_out, pair_out, payload_out, scratch,
):
    chips, rows, cols = mine_ref.shape
    core = core_index()
    norm_blocks(mine_ref, theirs_ref, gain_ref, scratch, cols)
    normed = scratch[...]
    rank = factor_ref.shape[0] // 2
    here = (owner_ref[:1, :1] & 1) == core
    low = jnp.where(
        here, dot_rows(normed, factor_ref[:rank, :]), dot_rows(normed, other_ref[:rank, :])
    )
    query_out[...] = dot_chunks(normed, query_ref)
    half = key_ref.shape[0]
    pair_out[:, :half] = dot_rows(normed, key_ref[...]).astype(jnp.bfloat16)
    pair_out[:, half:] = dot_rows(normed, value_ref[...]).astype(jnp.bfloat16)
    parts = rows // rank
    padded = jnp.concatenate([low, jnp.zeros((rows, LANES - rank), jnp.float32)], axis=1)
    padded = padded.astype(jnp.bfloat16)
    for chip in range(chips):
        at = pl.multiple_of((2 * chip + core) * cols, cols)
        own = factor_ref[rank:, pl.ds(at, cols)].astype(jnp.float32)
        other = other_ref[rank:, pl.ds(at, cols)].astype(jnp.float32)
        payload_out[chip, :, :cols] = jnp.where(here, own, other).astype(jnp.bfloat16)
        for part in range(parts):
            lanes = slice(cols + part * LANES, cols + (part + 1) * LANES)
            payload_out[chip, :, lanes] = padded[part * rank : (part + 1) * rank]


def split_product(left, weight_ref, mine_out, theirs_out):
    chips, _, cols = mine_out.shape
    core = core_index()
    for chip in range(chips):
        at = pl.multiple_of((2 * chip + 1 - core) * cols, cols)
        theirs_out[chip] = dot(left, weight_ref[:, pl.ds(at, cols)]).astype(jnp.bfloat16)
        at = pl.multiple_of((2 * chip + core) * cols, cols)
        mine_out[chip] = dot(left, weight_ref[:, pl.ds(at, cols)])


def attend_kernel(
    query_ref, pair_mine, pair_theirs, owner_ref, got_ref, lift_ref, cosine_ref, sine_ref,
    reach_ref, output_ref, mine_out, theirs_out, piece_out,
):
    rows, query_cols = query_ref.shape
    chips, _, cols = mine_out.shape
    head = HEAD_SIZE
    heads = query_cols // head
    half = head // 2
    rank = lift_ref.shape[0]
    owner = owner_ref[:1, :1]
    piece = jnp.zeros(got_ref.shape[1:], jnp.float32)
    for chip in range(chips):
        sent = got_ref[chip].astype(jnp.float32)
        piece = piece + jnp.where((owner >> 1) == chip, sent, 0.0)
    piece_out[...] = piece.astype(jnp.bfloat16)
    low = jnp.concatenate(
        [piece[:, at : at + LANES] for at in range(cols, piece.shape[1], LANES)], axis=0
    )
    lane = lax.broadcasted_iota(jnp.int32, (rows, head), 1)
    cosine = cosine_ref[...]
    sine = sine_ref[...]

    def rotate(wide):
        return (wide * cosine + pltpu.roll(wide, half, 1) * sine).astype(jnp.bfloat16)

    first = core_index() == 0
    even, odd = in_order(pair_mine[...], pair_theirs[...], first)
    key = rotate(jnp.where(lane < half, even, pltpu.roll(odd, half, 1)))
    value = jnp.where(lane < half, pltpu.roll(even, half, 1), odd).astype(jnp.bfloat16)
    query = query_ref[...] + dot(low[:, :rank].astype(jnp.bfloat16), lift_ref[...])
    query = query.astype(jnp.bfloat16).astype(jnp.float32)
    stacked = jnp.concatenate(
        [rotate(query[:, h * head : (h + 1) * head]) for h in range(heads)], axis=0
    )
    scores = dot_rows(stacked, key) * head ** (-0.5)
    weights = jnp.exp(scores) * jnp.concatenate([reach_ref[...]] * heads, axis=0)
    probs = (weights / jnp.sum(weights, axis=-1, keepdims=True)).astype(jnp.bfloat16)
    mixed = dot(probs, value).astype(jnp.bfloat16)
    mixed = jnp.concatenate([mixed[h * rows : (h + 1) * rows] for h in range(heads)], axis=1)
    split_product(mixed, output_ref, mine_out, theirs_out)


def hidden_kernel(
    got_ref, token_ref, gain_ref, piece_ref,
    hidden_out, payload_out,
):
    chips, rows, cols = got_ref.shape
    total = token_ref[...].astype(jnp.float32)
    added = got_ref[0].astype(jnp.float32)
    for chip in range(1, chips):
        added = added + got_ref[chip].astype(jnp.float32)
    hidden = (total + added).astype(jnp.bfloat16)
    hidden_out[...] = hidden
    factor = piece_ref[:, :cols]
    rank = factor.shape[0]
    device = lax.axis_index("tp")
    gain = gain_block(gain_ref, 0, cols)
    for index in range(1, 2 * chips):
        gain = jnp.where(device == index, gain_block(gain_ref, index, cols), gain)
    gained = hidden.astype(jnp.float32) * gain
    low = dot_rows(gained.astype(jnp.bfloat16), factor)
    padded = jnp.concatenate([low, jnp.zeros((rows, LANES - rank), jnp.float32)], axis=1)
    padded = padded.astype(jnp.bfloat16)
    for chip in range(chips):
        payload_out[chip, :, :cols] = hidden
        payload_out[chip, :, cols:] = padded


def forward_kernel(
    mine_ref, theirs_ref, gain_ref, lift_ref, gate_ref, up_ref, down_ref,
    mine_out, theirs_out, scratch, active, held, sem,
):
    chips = mine_ref.shape[0]
    cols = mine_ref.shape[2] - LANES

    def down_copy(chip):
        part = pl.ds(pl.multiple_of(2 * cols * chip, 2 * cols), 2 * cols)
        return pltpu.make_async_copy(down_ref.at[:, part], held.at[:, part], sem.at[chip])

    @pl.loop(0, chips)
    def _(chip):
        down_copy(chip).start()

    rank = lift_ref.shape[0]
    scale = norm_blocks(mine_ref, theirs_ref, gain_ref, scratch, cols)
    low = jnp.zeros((mine_ref.shape[1], LANES), jnp.float32)
    for chip in range(mine_ref.shape[0]):
        for ref in (mine_ref, theirs_ref):
            low = low + ref[chip, :, cols:].astype(jnp.float32)
    low = (low * scale)[:, :rank].astype(jnp.bfloat16)
    normed = scratch[...]
    gate = dot_chunks(normed, gate_ref)
    upper = dot_chunks(normed, up_ref) + dot(low, lift_ref[...])
    active[...] = (gate * jax.nn.sigmoid(gate) * upper).astype(jnp.bfloat16)
    core = core_index()

    @pl.loop(0, chips)
    def _(chip):
        down_copy(chip).wait()
        for side, out in ((1 - core, theirs_out), (core, mine_out)):
            at = pl.multiple_of((2 * chip + side) * cols, cols)
            out[chip] = dot(active[...], held[:, pl.ds(at, cols)]).astype(out.dtype)


def fast_body(
    tokens,
    attention_gain,
    forward_gain,
    query_weight,
    key_matrix,
    value_matrix,
    output_weight,
    gate_weight,
    up_weight,
    down_weight,
    adapter_inputs,
    adapter_query,
    adapter_upper,
    adapter_place,
    request_adapter,
    tree_parents,
):
    rows, cols = tokens.shape
    chips = lax.axis_size("tp") // 2
    width = query_weight.shape[0]
    shape = jax.ShapeDtypeStruct
    bf16, f32 = jnp.bfloat16, jnp.float32
    wide = cols + LANES
    heavy = (gate_weight, up_weight, down_weight)
    most = heavy + (query_weight, output_weight)
    rank = adapter_query.shape[1]
    split_out = (shape((chips, rows, cols), f32), shape((chips, rows, cols), bf16))
    factors = adapter_inputs[0].T

    spread_tokens, kept_tokens, gain_one, gain_two, parents = spread(
        tokens,
        (attention_gain.reshape(-1, LANES), forward_gain.reshape(-1, LANES), tree_parents),
        heavy,
        chips,
    )
    mine = exchange(spread_tokens, "tp")
    mine, held = lax.optimization_barrier((mine, adapter_inputs))
    theirs = partner_2(mine, "tp", 0)
    factors_theirs = partner_2(held, "tp", 0)[0].T
    query_lift, up_lift, owner, cosine, sine, reach = tables(
        request_adapter, adapter_place, (adapter_query, adapter_upper), parents, mine
    )
    query, pair, payload = call(
        project_kernel,
        "project",
        (
            shape((rows, query_weight.shape[1]), f32),
            shape((rows, 2 * key_matrix.shape[1]), bf16),
            shape((chips, rank, cols + rows // rank * LANES), bf16),
        ),
        (mine, theirs, gain_one, owner, factors_theirs),
        (query_weight, key_matrix.T, value_matrix.T, factors),
        heavy,
        [VMEM((rows, width), bf16)],
    )
    pair_theirs, payload = lax.optimization_barrier((partner_2(pair, "tp", 0), payload))
    kept, sent, piece = call(
        attend_kernel,
        "attend",
        (*split_out, shape(payload.shape[1:], bf16)),
        (
            query, pair, pair_theirs, owner, exchange(payload, "tp"), query_lift, cosine,
            sine, reach,
        ),
        (output_weight,),
        heavy + (query_weight,),
    )
    chip_sum = (kept + partner_2(sent, "tp", 0).astype(f32)).astype(bf16)
    hidden, payload = call(
        hidden_kernel,
        "hidden",
        (shape((rows, cols), bf16), shape((chips, rows, wide), bf16)),
        (exchange(chip_sum, "tp"), kept_tokens, gain_two, piece),
        (),
        most,
    )
    mine = exchange(payload, "tp")
    theirs = partner_2(mine, "tp", 0)
    kept, sent = call(
        forward_kernel,
        "forward",
        split_out,
        (mine, theirs, gain_two, up_lift),
        (gate_weight, up_weight),
        (query_weight, output_weight),
        [
            VMEM((rows, width), bf16),
            VMEM((rows, gate_weight.shape[1]), bf16),
            VMEM(down_weight.shape, bf16),
            pltpu.SemaphoreType.DMA((chips,)),
        ],
        far=(down_weight,),
        limit=18,
    )
    chip_sum = (kept + partner_2(sent, "tp", 0).astype(f32)).astype(bf16)
    added = jnp.sum(exchange(chip_sum, "tp").astype(f32), axis=0)
    return (hidden.astype(f32) + added).astype(bf16)


def body(*args):
    tokens, key_matrix, query_weight = args[0], args[4], args[3]
    fits = (
        tokens.shape[1] % LANES == 0
        and query_weight.shape[1] % HEAD_SIZE == 0
        and key_matrix.shape[1] * 2 == HEAD_SIZE
        and args[10].shape[0] == 1
        and args[14].shape[0] == 1
        and args[10].shape[2] == tokens.shape[0]
    )
    return fast_body(*args) if fits else general_body(*args)


def solution(mesh):
    return jax.shard_map(
        body,
        mesh=mesh,
        in_specs=(
            P("rep", "tp"),
            P(),
            P(),
            P(None, "tp"),
            P(None, "tp"),
            P(None, "tp"),
            P("tp", None),
            P(None, "tp"),
            P(None, "tp"),
            P("tp", None),
            P(("rep", "tp"), None, None),
            P("rep", None, "tp"),
            P("rep", None, "tp"),
            P("rep"),
            P("rep"),
            P("rep", None),
        ),
        out_specs=P("rep", "tp"),
        check_vma=False,
    )
```

```python
import jax
import jax.numpy as jnp
import numpy as np
from jax import lax
from jax.experimental import pallas as pl
from jax.experimental.pallas import tpu as pltpu
from jax.sharding import PartitionSpec as P

HEAD_SIZE = 128


EPS = 1e-05
ROPE_BASE = 500000.0


def core_groups(axis):
    count = lax.axis_size(axis)
    return [list(range(core, count, 2)) for core in range(2)]


def exchange(blocks, axis):
    return lax.all_to_all(
        blocks, axis, 0, 0, axis_index_groups=core_groups(axis), tiled=True
    )


def by_core(mine, theirs, core):
    even = jnp.where(core == 0, mine, theirs)
    odd = jnp.where(core == 0, theirs, mine)
    return jnp.stack([even, odd], axis=1)


def gather_features(part, axis):
    chips = lax.axis_size(axis) // 2
    core = lax.axis_index(axis) & 1
    mine = exchange(jnp.broadcast_to(part[None], (chips,) + part.shape), axis)
    theirs = partner_2(mine, axis, 0)
    both = by_core(mine, theirs, core).reshape((2 * chips,) + part.shape)
    return jnp.moveaxis(both, 0, 1).reshape(part.shape[0], -1)


def sum_features(partial, axis):
    count = lax.axis_size(axis)
    core = lax.axis_index(axis) & 1
    rows = partial.shape[0]
    split = partial.reshape(rows, count // 2, 2, -1)
    even = split[:, :, 0]
    odd = split[:, :, 1]
    mine = jnp.where(core == 0, even, odd)
    theirs = jnp.where(core == 0, odd, even).astype(jnp.bfloat16)
    pair = (mine + partner_2(theirs, axis, 0).astype(jnp.float32)).astype(jnp.bfloat16)
    got = exchange(jnp.moveaxis(pair, 1, 0), axis)
    return jnp.sum(got.astype(jnp.float32), axis=0)


def from_owner(mine, owner, axis):
    core = lax.axis_index(axis) & 1
    held = jnp.where(lax.axis_index(axis) == owner, mine, jnp.zeros_like(mine))
    held = held + partner_2(held, axis, 0)
    chips = lax.axis_size(axis) // 2
    got = exchange(jnp.broadcast_to(held[None], (chips,) + held.shape), axis)
    return lax.dynamic_index_in_dim(got, owner >> 1, 0, keepdims=False)


def partner_2(block, axis, distance):
    count = lax.axis_size(axis)
    route = []
    for low in range(count):
        high = low | 1 << distance
        if high != low and high < count:
            route += [(low, high), (high, low)]
    return lax.ppermute(block, axis, route)


def rms_scale(rows, gain):
    wide = rows.astype(jnp.float32)
    mean_sq = jnp.mean(wide * wide, axis=-1, keepdims=True)
    return (wide * lax.rsqrt(mean_sq + EPS) * gain.astype(jnp.float32)).astype(jnp.bfloat16)


def ancestry(parents):
    tree_width = parents.shape[-1]
    places = jnp.arange(tree_width, dtype=jnp.int32)
    links = (parents[:, :, None] == places[None, None, :]).astype(jnp.float32)
    reach = jnp.maximum(links, jnp.eye(tree_width, dtype=jnp.float32)[None])
    for step in range(int(tree_width).bit_length()):
        reach = jnp.minimum(
            jnp.einsum("rij,rjk->rik", reach, reach, precision=lax.Precision.HIGHEST), 1.0
        )
    tree_depth = jnp.sum(reach, axis=-1) - 1.0
    return (reach, tree_depth)


def apply_rotary(heads, tree_depth):
    half = heads.shape[-1] // 2
    freq = ROPE_BASE ** (-jnp.arange(half, dtype=jnp.float32) * 2.0 / heads.shape[-1])
    angle = tree_depth[:, :, None] * freq[None, None, :]
    cosine = jnp.cos(angle)[:, :, None, :]
    sine = jnp.sin(angle)[:, :, None, :]
    wide = heads.astype(jnp.float32)
    first = wide[..., :half]
    second = wide[..., half:]
    return jnp.concatenate(
        [first * cosine - second * sine, second * cosine + first * sine], axis=-1
    ).astype(jnp.bfloat16)


def join_pair(mine, theirs, flag):
    lower = jnp.concatenate([mine, theirs], axis=1)
    upper = jnp.concatenate([theirs, mine], axis=1)
    return jnp.where(flag == 1, upper, lower)


def general_body(
    tokens,
    attention_gain,
    forward_gain,
    query_weight,
    key_matrix,
    value_matrix,
    output_weight,
    gate_weight,
    up_weight,
    down_weight,
    adapter_inputs,
    adapter_query,
    adapter_upper,
    adapter_place,
    request_adapter,
    tree_parents,
):
    device = lax.axis_index("tp")
    rows = tokens.shape[0]
    request_list = request_adapter.shape[0]
    tree_width = rows // request_list
    rank = adapter_query.shape[1]
    pool_local = adapter_inputs.shape[0]
    head = HEAD_SIZE
    full_tokens = gather_features(tokens, "tp")
    normed = rms_scale(full_tokens, attention_gain)
    slots = adapter_place[request_adapter]
    owner = slots[0] // pool_local
    factors = lax.dynamic_index_in_dim(adapter_inputs, slots[0] % pool_local, 0, keepdims=False)
    low_held = jnp.dot(normed, factors[:, :rank], preferred_element_type=jnp.float32).astype(
        jnp.bfloat16
    )
    low_query = from_owner(low_held, owner, "tp")[None]
    lift = jnp.einsum(
        "rtk,rkc->rtc",
        low_query,
        adapter_query[request_adapter],
        preferred_element_type=jnp.float32,
    )
    query_local = (
        jnp.dot(normed, query_weight, preferred_element_type=jnp.float32) + lift.reshape(rows, -1)
    ).astype(jnp.bfloat16)
    key_local = jnp.dot(normed, key_matrix, preferred_element_type=jnp.float32).astype(jnp.bfloat16)
    value_local = jnp.dot(normed, value_matrix, preferred_element_type=jnp.float32).astype(
        jnp.bfloat16
    )
    query_cols = query_weight.shape[1]
    query_steps = max(0, (head // query_cols).bit_length() - 1)
    key_steps = (head // key_matrix.shape[1]).bit_length() - 1
    for bit in range(key_steps):
        flag = device >> bit & 1
        key_width = key_local.shape[1]
        with_query = bit < query_steps
        if with_query:
            query_width = query_local.shape[1]
            packed = jnp.concatenate([query_local, key_local, value_local], axis=1)
        else:
            query_width = 0
            packed = jnp.concatenate([key_local, value_local], axis=1)
        partner = partner_2(packed, "tp", bit)
        if with_query:
            query_local = join_pair(query_local, partner[:, :query_width], flag)
        key_other = partner[:, query_width : query_width + key_width]
        value_other = partner[:, query_width + key_width :]
        key_local = join_pair(key_local, key_other, flag)
        value_local = join_pair(value_local, value_other, flag)
    reach, tree_depth = ancestry(tree_parents)
    local_heads = query_local.shape[1] // head
    query_rotated = apply_rotary(
        query_local.reshape(request_list, tree_width, local_heads, head), tree_depth
    )
    key_rotated = apply_rotary(key_local.reshape(request_list, tree_width, 1, head), tree_depth)[
        :, :, 0, :
    ]
    heads_value = value_local.reshape(request_list, tree_width, head)
    scores = jnp.einsum(
        "rqhd,rkd->rhqk", query_rotated, key_rotated, preferred_element_type=jnp.float32
    ) * head ** (-0.5)
    weights = jnp.exp(scores) * reach[:, None, :, :]
    probs = (weights / jnp.sum(weights, axis=-1, keepdims=True)).astype(jnp.bfloat16)
    mixed = jnp.einsum(
        "rhqk,rkd->rqhd", probs, heads_value, preferred_element_type=jnp.float32
    ).astype(jnp.bfloat16)
    mixed = mixed.reshape(rows, local_heads * head)
    offset = (device & (1 << query_steps) - 1) * query_cols
    own_mixed = lax.dynamic_slice_in_dim(mixed, offset, query_cols, 1)
    partial_out = jnp.dot(own_mixed, output_weight, preferred_element_type=jnp.float32)
    summed = sum_features(partial_out, "tp")
    hidden = (tokens.astype(jnp.float32) + summed).astype(jnp.bfloat16)
    hidden_full = gather_features(hidden, "tp")
    normed_two = rms_scale(hidden_full, forward_gain)
    low_held_two = jnp.dot(normed_two, factors[:, rank:], preferred_element_type=jnp.float32).astype(
        jnp.bfloat16
    )
    low_up = from_owner(low_held_two, owner, "tp")[None]
    lift_up = jnp.einsum(
        "rtk,rkc->rtc", low_up, adapter_upper[request_adapter], preferred_element_type=jnp.float32
    )
    gate = jnp.dot(normed_two, gate_weight, preferred_element_type=jnp.float32)
    upper = jnp.dot(normed_two, up_weight, preferred_element_type=jnp.float32) + lift_up.reshape(
        rows, -1
    )
    active = (jax.nn.silu(gate) * upper).astype(jnp.bfloat16)
    forward = jnp.dot(active, down_weight, preferred_element_type=jnp.float32)
    forward_part = sum_features(forward, "tp")
    return (hidden.astype(jnp.float32) + forward_part).astype(jnp.bfloat16)


VMEM = pltpu.VMEM
WHOLE = pl.BlockSpec(memory_space=pltpu.VMEM)
SCALAR = pl.BlockSpec(memory_space=pltpu.SMEM)
FAR = pl.BlockSpec(memory_space=pltpu.HBM)
ROW_DOT = (((1,), (1,)), ((), ()))
LANES = 128
CHUNK = 1024


def dot(a, b):
    return jnp.dot(a, b, preferred_element_type=jnp.float32)


def dot_rows(a, b):
    return lax.dot_general(a, b, ROW_DOT, preferred_element_type=jnp.float32)


def call(kernel, name, outs, args, weights=(), ahead=(), scratch=(), limit=6, far=()):
    outs = tuple(VMEM(o.shape, o.dtype) for o in outs)
    size = sum(w.size for w in weights + far)
    used = len(args) + len(weights) + len(far)

    def run(*refs):
        kernel(*refs[:used], *refs[used + len(ahead) :])

    return pl.pallas_call(
        run,
        out_shape=outs,
        in_specs=[WHOLE] * (len(args) + len(weights)) + [FAR] * len(far + ahead),
        out_specs=(WHOLE,) * len(outs),
        scratch_shapes=list(scratch),
        name=name,
        cost_estimate=pl.CostEstimate(
            flops=64 * size, bytes_accessed=2 * size, transcendentals=0
        ),
        compiler_params=pltpu.CompilerParams(vmem_limit_bytes=limit << 20),
    )(
        *[pltpu.with_memory_space_constraint(w, VMEM) for w in args + weights],
        *[pltpu.with_memory_space_constraint(w, pltpu.HBM) for w in far + ahead],
    )


def near(x):
    return pltpu.with_memory_space_constraint(x, VMEM)


def distant(x):
    return pltpu.with_memory_space_constraint(x, pltpu.HBM)


def spread(tokens, kept, ahead, chips):
    outs = (VMEM((chips,) + tokens.shape, tokens.dtype),)
    outs += tuple(VMEM(a.shape, a.dtype) for a in (tokens, *kept))
    used = 1 + len(kept)

    def kernel(*refs):
        ins, outs, sem = refs[:used], refs[used + len(ahead) : -1], refs[-1]
        pairs = [(ins[0], outs[0].at[chip]) for chip in range(chips)]
        pairs += [(ins[k], outs[1 + k]) for k in range(used)]
        copies = [
            pltpu.make_async_copy(src, dst, sem.at[k]) for k, (src, dst) in enumerate(pairs)
        ]
        for copy in copies:
            copy.start()
        for copy in copies:
            copy.wait()

    return pl.pallas_call(
        kernel,
        out_shape=outs,
        in_specs=[FAR] * (used + len(ahead)),
        out_specs=(WHOLE,) * len(outs),
        scratch_shapes=[pltpu.SemaphoreType.DMA((chips + used,))],
        name="spread",
        compiler_params=pltpu.CompilerParams(vmem_limit_bytes=2 << 20),
    )(*[distant(a) for a in (tokens, *kept, *ahead)])


def table_kernel(
    request_ref, place_ref, query_ref, up_ref, parent_ref, after_ref,
    query_out, up_out, owner_out, cosine_out, sine_out, reach_out, place, sem,
):
    request = request_ref[0]
    copies = [
        pltpu.make_async_copy(place_ref, place, sem.at[0]),
        pltpu.make_async_copy(query_ref.at[request], query_out, sem.at[1]),
        pltpu.make_async_copy(up_ref.at[request], up_out, sem.at[2]),
    ]
    for copy in copies:
        copy.start()
    rows, head = cosine_out.shape
    half = head // 2
    own = lax.broadcasted_iota(jnp.int32, (rows, rows), 0)
    other = lax.broadcasted_iota(jnp.int32, (rows, rows), 1)
    eye = jnp.where(own == other, 1.0, 0.0)
    links = jnp.where(parent_ref[...] == own, 1.0, 0.0)
    reach = dot_rows(eye.astype(jnp.bfloat16), jnp.maximum(links, eye).astype(jnp.bfloat16))
    for _ in range((rows - 1).bit_length()):
        square = reach.astype(jnp.bfloat16)
        reach = jnp.minimum(dot(square, square), 1.0)
    reach_out[...] = reach
    lane = lax.broadcasted_iota(jnp.int32, (rows, head), 1)
    place_in_half = jnp.where(lane < half, lane, lane - half).astype(jnp.float32)
    freq = jnp.exp(place_in_half * np.float32(-2.0 / head * np.log(ROPE_BASE)))
    angle = (jnp.sum(reach, axis=-1, keepdims=True) - 1.0) * freq
    sine = jnp.sin(angle)
    cosine_out[...] = jnp.cos(angle)
    sine_out[...] = jnp.where(lane < half, -sine, sine)
    for copy in copies:
        copy.wait()
    owner_out[...] = jnp.full(owner_out.shape, place[request], jnp.int32)


def tables(request, place, lifts, parents, after):
    rows = parents.shape[1]
    shapes = [(a.shape[1:], a.dtype) for a in lifts]
    shapes += [((8, LANES), jnp.int32)]
    shapes += [((rows, HEAD_SIZE), jnp.float32)] * 2 + [((rows, rows), jnp.float32)]
    return pl.pallas_call(
        table_kernel,
        out_shape=tuple(VMEM(*a) for a in shapes),
        in_specs=[SCALAR] + [FAR] * 3 + [WHOLE] * 2,
        out_specs=(WHOLE,) * len(shapes),
        scratch_shapes=[
            pltpu.SMEM(place.shape, jnp.int32),
            pltpu.SemaphoreType.DMA((3,)),
        ],
        name="tables",
        compiler_params=pltpu.CompilerParams(vmem_limit_bytes=2 << 20),
    )(request, *[distant(a) for a in (place, *lifts)], near(parents), near(after))


def dot_chunks(left, weight_ref):
    depth = weight_ref.shape[0]
    step = min(depth, CHUNK)
    total = dot(left[:, :step], weight_ref[:step, :])
    for at in range(step, depth, step):
        total = total + dot(left[:, at : at + step], weight_ref[at : at + step, :])
    return total


def gain_block(gain_ref, index, cols):
    count = cols // LANES
    lines = [gain_ref[index * count + j : index * count + j + 1, :] for j in range(count)]
    return jnp.concatenate([line.astype(jnp.float32) for line in lines], axis=1)


def core_index():
    return lax.axis_index("tp") & 1


def in_order(mine, theirs, flag):
    mine = mine.astype(jnp.float32)
    theirs = theirs.astype(jnp.float32)
    return jnp.where(flag, mine, theirs), jnp.where(flag, theirs, mine)


def norm_blocks(mine_ref, theirs_ref, gain_ref, scratch, cols):
    chips = mine_ref.shape[0]
    first = core_index() == 0
    squares = jnp.zeros((mine_ref.shape[1], cols), jnp.float32)
    for chip in range(chips):
        for ref in (mine_ref, theirs_ref):
            wide = ref[chip, :, :cols].astype(jnp.float32)
            squares = squares + wide * wide
    mean_sq = jnp.sum(squares, axis=-1, keepdims=True) / (2 * chips * cols)
    scale = lax.rsqrt(mean_sq + EPS)
    for chip in range(chips):
        pair = in_order(mine_ref[chip, :, :cols], theirs_ref[chip, :, :cols], first)
        for side in range(2):
            low = (2 * chip + side) * cols
            gain = gain_block(gain_ref, 2 * chip + side, cols)
            scratch[:, low : low + cols] = (pair[side] * scale * gain).astype(jnp.bfloat16)
    return scale


def project_kernel(
    mine_ref, theirs_ref, gain_ref, owner_ref, other_ref, key_ref, value_ref, factor_ref,
    normed_out, pair_out, payload_out,
):
    chips, rows, cols = mine_ref.shape
    core = core_index()
    norm_blocks(mine_ref, theirs_ref, gain_ref, normed_out, cols)
    normed = normed_out[...]
    rank = factor_ref.shape[0] // 2
    here = (owner_ref[:1, :1] & 1) == core
    low = jnp.where(
        here, dot_rows(normed, factor_ref[:rank, :]), dot_rows(normed, other_ref[:rank, :])
    )
    half = key_ref.shape[0]
    pair_out[:, :half] = dot_rows(normed, key_ref[...]).astype(jnp.bfloat16)
    pair_out[:, half:] = dot_rows(normed, value_ref[...]).astype(jnp.bfloat16)
    parts = rows // rank
    padded = jnp.concatenate([low, jnp.zeros((rows, LANES - rank), jnp.float32)], axis=1)
    padded = padded.astype(jnp.bfloat16)
    for chip in range(chips):
        at = pl.multiple_of((2 * chip + core) * cols, cols)
        own = factor_ref[rank:, pl.ds(at, cols)].astype(jnp.float32)
        other = other_ref[rank:, pl.ds(at, cols)].astype(jnp.float32)
        payload_out[chip, :, :cols] = jnp.where(here, own, other).astype(jnp.bfloat16)
        for part in range(parts):
            lanes = slice(cols + part * LANES, cols + (part + 1) * LANES)
            payload_out[chip, :, lanes] = padded[part * rank : (part + 1) * rank]


def query_kernel(normed_ref, query_ref, query_out):
    query_out[...] = dot_chunks(normed_ref[...], query_ref)


def side_product(left, weight_ref, side, out):
    chips, _, cols = out.shape
    for chip in range(chips):
        at = pl.multiple_of((2 * chip + side) * cols, cols)
        out[chip] = dot(left, weight_ref[:, pl.ds(at, cols)]).astype(out.dtype)


def attend_kernel(
    query_ref, pair_mine, pair_theirs, owner_ref, got_ref, lift_ref, cosine_ref, sine_ref,
    reach_ref, output_ref, mixed_out, theirs_out, piece_out,
):
    rows, query_cols = query_ref.shape
    chips, _, cols = theirs_out.shape
    head = HEAD_SIZE
    heads = query_cols // head
    half = head // 2
    rank = lift_ref.shape[0]
    owner = owner_ref[:1, :1]
    piece = jnp.zeros(got_ref.shape[1:], jnp.float32)
    for chip in range(chips):
        sent = got_ref[chip].astype(jnp.float32)
        piece = piece + jnp.where((owner >> 1) == chip, sent, 0.0)
    piece_out[...] = piece.astype(jnp.bfloat16)
    low = jnp.concatenate(
        [piece[:, at : at + LANES] for at in range(cols, piece.shape[1], LANES)], axis=0
    )
    lane = lax.broadcasted_iota(jnp.int32, (rows, head), 1)
    cosine = cosine_ref[...]
    sine = sine_ref[...]

    def rotate(wide):
        return (wide * cosine + pltpu.roll(wide, half, 1) * sine).astype(jnp.bfloat16)

    first = core_index() == 0
    even, odd = in_order(pair_mine[...], pair_theirs[...], first)
    key = rotate(jnp.where(lane < half, even, pltpu.roll(odd, half, 1)))
    value = jnp.where(lane < half, pltpu.roll(even, half, 1), odd).astype(jnp.bfloat16)
    query = query_ref[...] + dot(low[:, :rank].astype(jnp.bfloat16), lift_ref[...])
    query = query.astype(jnp.bfloat16).astype(jnp.float32)
    stacked = jnp.concatenate(
        [rotate(query[:, h * head : (h + 1) * head]) for h in range(heads)], axis=0
    )
    scores = dot_rows(stacked, key) * head ** (-0.5)
    weights = jnp.exp(scores) * jnp.concatenate([reach_ref[...]] * heads, axis=0)
    probs = (weights / jnp.sum(weights, axis=-1, keepdims=True)).astype(jnp.bfloat16)
    mixed = dot(probs, value).astype(jnp.bfloat16)
    mixed = jnp.concatenate([mixed[h * rows : (h + 1) * rows] for h in range(heads)], axis=1)
    mixed_out[...] = mixed
    side_product(mixed, output_ref, 1 - core_index(), theirs_out)


def rest_kernel(mixed_ref, output_ref, mine_out):
    side_product(mixed_ref[...], output_ref, core_index(), mine_out)


def hidden_kernel(
    got_ref, token_ref, gain_ref, piece_ref,
    hidden_out, payload_out,
):
    chips, rows, cols = got_ref.shape
    total = token_ref[...].astype(jnp.float32)
    added = got_ref[0].astype(jnp.float32)
    for chip in range(1, chips):
        added = added + got_ref[chip].astype(jnp.float32)
    hidden = (total + added).astype(jnp.bfloat16)
    hidden_out[...] = hidden
    factor = piece_ref[:, :cols]
    rank = factor.shape[0]
    device = lax.axis_index("tp")
    gain = gain_block(gain_ref, 0, cols)
    for index in range(1, 2 * chips):
        gain = jnp.where(device == index, gain_block(gain_ref, index, cols), gain)
    gained = hidden.astype(jnp.float32) * gain
    low = dot_rows(gained.astype(jnp.bfloat16), factor)
    padded = jnp.concatenate([low, jnp.zeros((rows, LANES - rank), jnp.float32)], axis=1)
    padded = padded.astype(jnp.bfloat16)
    for chip in range(chips):
        payload_out[chip, :, :cols] = hidden
        payload_out[chip, :, cols:] = padded


def down_copies(down_ref, held, sem, side):
    chips, _, cols = held.shape

    def copy(chip):
        part = pl.ds(pl.multiple_of((2 * chip + side) * cols, LANES), cols)
        return pltpu.make_async_copy(down_ref.at[:, part], held.at[chip], sem.at[chip])

    return copy


def forward_kernel(
    mine_ref, theirs_ref, gain_ref, lift_ref, gate_ref, up_ref, down_ref,
    active_out, theirs_out, held_out, scratch, held, sem, sem_out,
):
    chips, rows, cols = theirs_out.shape
    core = core_index()
    rank = lift_ref.shape[0]
    first = down_copies(down_ref, held, sem, 1 - core)
    second = down_copies(down_ref, held_out, sem_out, core)

    @pl.loop(0, chips)
    def _(chip):
        first(chip).start()

    @pl.loop(0, chips)
    def _(chip):
        second(chip).start()

    scale = norm_blocks(mine_ref, theirs_ref, gain_ref, scratch, cols)
    low = jnp.zeros((rows, LANES), jnp.float32)
    for chip in range(chips):
        for ref in (mine_ref, theirs_ref):
            low = low + ref[chip, :, cols:].astype(jnp.float32)
    low = (low * scale)[:, :rank].astype(jnp.bfloat16)
    normed = scratch[...]
    gate = dot_chunks(normed, gate_ref)
    upper = dot_chunks(normed, up_ref) + dot(low, lift_ref[...])
    active_out[...] = (gate * jax.nn.sigmoid(gate) * upper).astype(jnp.bfloat16)

    @pl.loop(0, chips)
    def _(chip):
        first(chip).wait()
        theirs_out[chip] = dot(active_out[...], held[chip]).astype(theirs_out.dtype)

    @pl.loop(0, chips)
    def _(chip):
        second(chip).wait()


def last_kernel(active_ref, held_ref, mine_out):
    for chip in range(mine_out.shape[0]):
        mine_out[chip] = dot(active_ref[...], held_ref[chip])


def fast_body(
    tokens,
    attention_gain,
    forward_gain,
    query_weight,
    key_matrix,
    value_matrix,
    output_weight,
    gate_weight,
    up_weight,
    down_weight,
    adapter_inputs,
    adapter_query,
    adapter_upper,
    adapter_place,
    request_adapter,
    tree_parents,
):
    rows, cols = tokens.shape
    chips = lax.axis_size("tp") // 2
    width = query_weight.shape[0]
    shape = jax.ShapeDtypeStruct
    bf16, f32 = jnp.bfloat16, jnp.float32
    wide = cols + LANES
    heavy = (gate_weight, up_weight, down_weight)
    most = heavy + (query_weight, output_weight)
    rank = adapter_query.shape[1]
    factors = adapter_inputs[0].T

    spread_tokens, kept_tokens, gain_one, gain_two, parents = spread(
        tokens,
        (attention_gain.reshape(-1, LANES), forward_gain.reshape(-1, LANES), tree_parents),
        heavy,
        chips,
    )
    mine = exchange(spread_tokens, "tp")
    mine, held = lax.optimization_barrier((mine, adapter_inputs))
    theirs = partner_2(mine, "tp", 0)
    factors_theirs = partner_2(held, "tp", 0)[0].T
    query_lift, up_lift, owner, cosine, sine, reach = tables(
        request_adapter, adapter_place, (adapter_query, adapter_upper), parents, mine
    )
    normed, pair, payload = call(
        project_kernel,
        "project",
        (
            shape((rows, width), bf16),
            shape((rows, 2 * key_matrix.shape[1]), bf16),
            shape((chips, rank, cols + rows // rank * LANES), bf16),
        ),
        (mine, theirs, gain_one, owner, factors_theirs),
        (key_matrix.T, value_matrix.T, factors),
    )
    pair_theirs = partner_2(pair, "tp", 0)
    (query,) = call(
        query_kernel,
        "query",
        (shape((rows, query_weight.shape[1]), f32),),
        (normed,),
        (query_weight,),
        heavy,
    )
    pair_theirs, query, payload = lax.optimization_barrier((pair_theirs, query, payload))
    mixed, sent, piece = call(
        attend_kernel,
        "attend",
        (
            shape((rows, query_weight.shape[1]), bf16),
            shape((chips, rows, cols), bf16),
            shape(payload.shape[1:], bf16),
        ),
        (
            query, pair, pair_theirs, owner, exchange(payload, "tp"), query_lift, cosine,
            sine, reach,
        ),
        (output_weight,),
        heavy + (query_weight,),
    )
    sent_theirs = partner_2(sent, "tp", 0)
    (kept,) = call(
        rest_kernel, "rest", (shape((chips, rows, cols), f32),), (mixed,), (output_weight,)
    )
    chip_sum = (kept + sent_theirs.astype(f32)).astype(bf16)
    hidden, payload = call(
        hidden_kernel,
        "hidden",
        (shape((rows, cols), bf16), shape((chips, rows, wide), bf16)),
        (exchange(chip_sum, "tp"), kept_tokens, gain_two, piece),
        (),
        most,
    )
    mine = exchange(payload, "tp")
    theirs = partner_2(mine, "tp", 0)
    held = shape((chips, down_weight.shape[0], cols), bf16)
    active, sent, held_mine = call(
        forward_kernel,
        "forward",
        (
            shape((rows, gate_weight.shape[1]), bf16),
            shape((chips, rows, cols), bf16),
            held,
        ),
        (mine, theirs, gain_two, up_lift),
        (gate_weight, up_weight),
        (query_weight, output_weight),
        [
            VMEM((rows, width), bf16),
            VMEM(held.shape, bf16),
            pltpu.SemaphoreType.DMA((chips,)),
            pltpu.SemaphoreType.DMA((chips,)),
        ],
        far=(down_weight,),
        limit=10,
    )
    sent_theirs = partner_2(sent, "tp", 0)
    (kept,) = call(
        last_kernel, "last", (shape((chips, rows, cols), f32),), (active, held_mine)
    )
    chip_sum = (kept + sent_theirs.astype(f32)).astype(bf16)
    added = jnp.sum(exchange(chip_sum, "tp").astype(f32), axis=0)
    return (hidden.astype(f32) + added).astype(bf16)


def body(*args):
    tokens, key_matrix, query_weight = args[0], args[4], args[3]
    fits = (
        tokens.shape[1] % LANES == 0
        and query_weight.shape[1] % HEAD_SIZE == 0
        and key_matrix.shape[1] * 2 == HEAD_SIZE
        and args[10].shape[0] == 1
        and args[14].shape[0] == 1
        and args[10].shape[2] == tokens.shape[0]
    )
    return fast_body(*args) if fits else general_body(*args)


def solution(mesh):
    return jax.shard_map(
        body,
        mesh=mesh,
        in_specs=(
            P("rep", "tp"),
            P(),
            P(),
            P(None, "tp"),
            P(None, "tp"),
            P(None, "tp"),
            P("tp", None),
            P(None, "tp"),
            P(None, "tp"),
            P("tp", None),
            P(("rep", "tp"), None, None),
            P("rep", None, "tp"),
            P("rep", None, "tp"),
            P("rep"),
            P("rep"),
            P("rep", None),
        ),
        out_specs=P("rep", "tp"),
        check_vma=False,
    )
```

```python
import jax
import jax.numpy as jnp
import numpy as np
from jax import lax
from jax.experimental import pallas as pl
from jax.experimental.pallas import tpu as pltpu
from jax.sharding import PartitionSpec as P

HEAD_SIZE = 128


EPS = 1e-05
ROPE_BASE = 500000.0


def core_groups(axis):
    count = lax.axis_size(axis)
    return [list(range(core, count, 2)) for core in range(2)]


def exchange(blocks, axis):
    return lax.all_to_all(
        blocks, axis, 0, 0, axis_index_groups=core_groups(axis), tiled=True
    )


def by_core(mine, theirs, core):
    even = jnp.where(core == 0, mine, theirs)
    odd = jnp.where(core == 0, theirs, mine)
    return jnp.stack([even, odd], axis=1)


def gather_features(part, axis):
    chips = lax.axis_size(axis) // 2
    core = lax.axis_index(axis) & 1
    mine = exchange(jnp.broadcast_to(part[None], (chips,) + part.shape), axis)
    theirs = partner_2(mine, axis, 0)
    both = by_core(mine, theirs, core).reshape((2 * chips,) + part.shape)
    return jnp.moveaxis(both, 0, 1).reshape(part.shape[0], -1)


def sum_features(partial, axis):
    count = lax.axis_size(axis)
    core = lax.axis_index(axis) & 1
    rows = partial.shape[0]
    split = partial.reshape(rows, count // 2, 2, -1)
    even = split[:, :, 0]
    odd = split[:, :, 1]
    mine = jnp.where(core == 0, even, odd)
    theirs = jnp.where(core == 0, odd, even).astype(jnp.bfloat16)
    pair = (mine + partner_2(theirs, axis, 0).astype(jnp.float32)).astype(jnp.bfloat16)
    got = exchange(jnp.moveaxis(pair, 1, 0), axis)
    return jnp.sum(got.astype(jnp.float32), axis=0)


def from_owner(mine, owner, axis):
    core = lax.axis_index(axis) & 1
    held = jnp.where(lax.axis_index(axis) == owner, mine, jnp.zeros_like(mine))
    held = held + partner_2(held, axis, 0)
    chips = lax.axis_size(axis) // 2
    got = exchange(jnp.broadcast_to(held[None], (chips,) + held.shape), axis)
    return lax.dynamic_index_in_dim(got, owner >> 1, 0, keepdims=False)


def partner_2(block, axis, distance):
    count = lax.axis_size(axis)
    route = []
    for low in range(count):
        high = low | 1 << distance
        if high != low and high < count:
            route += [(low, high), (high, low)]
    return lax.ppermute(block, axis, route)


def rms_scale(rows, gain):
    wide = rows.astype(jnp.float32)
    mean_sq = jnp.mean(wide * wide, axis=-1, keepdims=True)
    return (wide * lax.rsqrt(mean_sq + EPS) * gain.astype(jnp.float32)).astype(jnp.bfloat16)


def ancestry(parents):
    tree_width = parents.shape[-1]
    places = jnp.arange(tree_width, dtype=jnp.int32)
    links = (parents[:, :, None] == places[None, None, :]).astype(jnp.float32)
    reach = jnp.maximum(links, jnp.eye(tree_width, dtype=jnp.float32)[None])
    for step in range(int(tree_width).bit_length()):
        reach = jnp.minimum(
            jnp.einsum("rij,rjk->rik", reach, reach, precision=lax.Precision.HIGHEST), 1.0
        )
    tree_depth = jnp.sum(reach, axis=-1) - 1.0
    return (reach, tree_depth)


def apply_rotary(heads, tree_depth):
    half = heads.shape[-1] // 2
    freq = ROPE_BASE ** (-jnp.arange(half, dtype=jnp.float32) * 2.0 / heads.shape[-1])
    angle = tree_depth[:, :, None] * freq[None, None, :]
    cosine = jnp.cos(angle)[:, :, None, :]
    sine = jnp.sin(angle)[:, :, None, :]
    wide = heads.astype(jnp.float32)
    first = wide[..., :half]
    second = wide[..., half:]
    return jnp.concatenate(
        [first * cosine - second * sine, second * cosine + first * sine], axis=-1
    ).astype(jnp.bfloat16)


def join_pair(mine, theirs, flag):
    lower = jnp.concatenate([mine, theirs], axis=1)
    upper = jnp.concatenate([theirs, mine], axis=1)
    return jnp.where(flag == 1, upper, lower)


def general_body(
    tokens,
    attention_gain,
    forward_gain,
    query_weight,
    key_matrix,
    value_matrix,
    output_weight,
    gate_weight,
    up_weight,
    down_weight,
    adapter_inputs,
    adapter_query,
    adapter_upper,
    adapter_place,
    request_adapter,
    tree_parents,
):
    device = lax.axis_index("tp")
    rows = tokens.shape[0]
    request_list = request_adapter.shape[0]
    tree_width = rows // request_list
    rank = adapter_query.shape[1]
    pool_local = adapter_inputs.shape[0]
    head = HEAD_SIZE
    full_tokens = gather_features(tokens, "tp")
    normed = rms_scale(full_tokens, attention_gain)
    slots = adapter_place[request_adapter]
    owner = slots[0] // pool_local
    factors = lax.dynamic_index_in_dim(adapter_inputs, slots[0] % pool_local, 0, keepdims=False)
    low_held = jnp.dot(normed, factors[:, :rank], preferred_element_type=jnp.float32).astype(
        jnp.bfloat16
    )
    low_query = from_owner(low_held, owner, "tp")[None]
    lift = jnp.einsum(
        "rtk,rkc->rtc",
        low_query,
        adapter_query[request_adapter],
        preferred_element_type=jnp.float32,
    )
    query_local = (
        jnp.dot(normed, query_weight, preferred_element_type=jnp.float32) + lift.reshape(rows, -1)
    ).astype(jnp.bfloat16)
    key_local = jnp.dot(normed, key_matrix, preferred_element_type=jnp.float32).astype(jnp.bfloat16)
    value_local = jnp.dot(normed, value_matrix, preferred_element_type=jnp.float32).astype(
        jnp.bfloat16
    )
    query_cols = query_weight.shape[1]
    query_steps = max(0, (head // query_cols).bit_length() - 1)
    key_steps = (head // key_matrix.shape[1]).bit_length() - 1
    for bit in range(key_steps):
        flag = device >> bit & 1
        key_width = key_local.shape[1]
        with_query = bit < query_steps
        if with_query:
            query_width = query_local.shape[1]
            packed = jnp.concatenate([query_local, key_local, value_local], axis=1)
        else:
            query_width = 0
            packed = jnp.concatenate([key_local, value_local], axis=1)
        partner = partner_2(packed, "tp", bit)
        if with_query:
            query_local = join_pair(query_local, partner[:, :query_width], flag)
        key_other = partner[:, query_width : query_width + key_width]
        value_other = partner[:, query_width + key_width :]
        key_local = join_pair(key_local, key_other, flag)
        value_local = join_pair(value_local, value_other, flag)
    reach, tree_depth = ancestry(tree_parents)
    local_heads = query_local.shape[1] // head
    query_rotated = apply_rotary(
        query_local.reshape(request_list, tree_width, local_heads, head), tree_depth
    )
    key_rotated = apply_rotary(key_local.reshape(request_list, tree_width, 1, head), tree_depth)[
        :, :, 0, :
    ]
    heads_value = value_local.reshape(request_list, tree_width, head)
    scores = jnp.einsum(
        "rqhd,rkd->rhqk", query_rotated, key_rotated, preferred_element_type=jnp.float32
    ) * head ** (-0.5)
    weights = jnp.exp(scores) * reach[:, None, :, :]
    probs = (weights / jnp.sum(weights, axis=-1, keepdims=True)).astype(jnp.bfloat16)
    mixed = jnp.einsum(
        "rhqk,rkd->rqhd", probs, heads_value, preferred_element_type=jnp.float32
    ).astype(jnp.bfloat16)
    mixed = mixed.reshape(rows, local_heads * head)
    offset = (device & (1 << query_steps) - 1) * query_cols
    own_mixed = lax.dynamic_slice_in_dim(mixed, offset, query_cols, 1)
    partial_out = jnp.dot(own_mixed, output_weight, preferred_element_type=jnp.float32)
    summed = sum_features(partial_out, "tp")
    hidden = (tokens.astype(jnp.float32) + summed).astype(jnp.bfloat16)
    hidden_full = gather_features(hidden, "tp")
    normed_two = rms_scale(hidden_full, forward_gain)
    low_held_two = jnp.dot(normed_two, factors[:, rank:], preferred_element_type=jnp.float32).astype(
        jnp.bfloat16
    )
    low_up = from_owner(low_held_two, owner, "tp")[None]
    lift_up = jnp.einsum(
        "rtk,rkc->rtc", low_up, adapter_upper[request_adapter], preferred_element_type=jnp.float32
    )
    gate = jnp.dot(normed_two, gate_weight, preferred_element_type=jnp.float32)
    upper = jnp.dot(normed_two, up_weight, preferred_element_type=jnp.float32) + lift_up.reshape(
        rows, -1
    )
    active = (jax.nn.silu(gate) * upper).astype(jnp.bfloat16)
    forward = jnp.dot(active, down_weight, preferred_element_type=jnp.float32)
    forward_part = sum_features(forward, "tp")
    return (hidden.astype(jnp.float32) + forward_part).astype(jnp.bfloat16)


VMEM = pltpu.VMEM
WHOLE = pl.BlockSpec(memory_space=pltpu.VMEM)
SCALAR = pl.BlockSpec(memory_space=pltpu.SMEM)
FAR = pl.BlockSpec(memory_space=pltpu.HBM)
ROW_DOT = (((1,), (1,)), ((), ()))
LANES = 128
CHUNK = 1024


def dot(a, b):
    return jnp.dot(a, b, preferred_element_type=jnp.float32)


def dot_rows(a, b):
    return lax.dot_general(a, b, ROW_DOT, preferred_element_type=jnp.float32)


def call(kernel, name, outs, args, weights=(), ahead=(), scratch=(), limit=6, far=()):
    outs = tuple(VMEM(o.shape, o.dtype) for o in outs)
    size = sum(w.size for w in weights + far)
    used = len(args) + len(weights) + len(far)

    def run(*refs):
        kernel(*refs[:used], *refs[used + len(ahead) :])

    return pl.pallas_call(
        run,
        out_shape=outs,
        in_specs=[WHOLE] * (len(args) + len(weights)) + [FAR] * len(far + ahead),
        out_specs=(WHOLE,) * len(outs),
        scratch_shapes=list(scratch),
        name=name,
        cost_estimate=pl.CostEstimate(
            flops=64 * size, bytes_accessed=2 * size, transcendentals=0
        ),
        compiler_params=pltpu.CompilerParams(vmem_limit_bytes=limit << 20),
    )(
        *[pltpu.with_memory_space_constraint(w, VMEM) for w in args + weights],
        *[pltpu.with_memory_space_constraint(w, pltpu.HBM) for w in far + ahead],
    )


def near(x):
    return pltpu.with_memory_space_constraint(x, VMEM)


def distant(x):
    return pltpu.with_memory_space_constraint(x, pltpu.HBM)


def spread(tokens, kept, ahead, chips):
    outs = (VMEM((chips,) + tokens.shape, tokens.dtype),)
    outs += tuple(VMEM(a.shape, a.dtype) for a in (tokens, *kept))
    used = 1 + len(kept)

    def kernel(*refs):
        ins, outs, sem = refs[:used], refs[used + len(ahead) : -1], refs[-1]
        pairs = [(ins[0], outs[0].at[chip]) for chip in range(chips)]
        pairs += [(ins[k], outs[1 + k]) for k in range(used)]
        copies = [
            pltpu.make_async_copy(src, dst, sem.at[k]) for k, (src, dst) in enumerate(pairs)
        ]
        for copy in copies:
            copy.start()
        for copy in copies:
            copy.wait()

    return pl.pallas_call(
        kernel,
        out_shape=outs,
        in_specs=[FAR] * (used + len(ahead)),
        out_specs=(WHOLE,) * len(outs),
        scratch_shapes=[pltpu.SemaphoreType.DMA((chips + used,))],
        name="spread",
        compiler_params=pltpu.CompilerParams(vmem_limit_bytes=2 << 20),
    )(*[distant(a) for a in (tokens, *kept, *ahead)])


def table_kernel(
    request_ref, place_ref, query_ref, up_ref, parent_ref, after_ref,
    query_out, up_out, owner_out, cosine_out, sine_out, reach_out, place, sem,
):
    request = request_ref[0]
    copies = [
        pltpu.make_async_copy(place_ref, place, sem.at[0]),
        pltpu.make_async_copy(query_ref.at[request], query_out, sem.at[1]),
        pltpu.make_async_copy(up_ref.at[request], up_out, sem.at[2]),
    ]
    for copy in copies:
        copy.start()
    rows, head = cosine_out.shape
    half = head // 2
    own = lax.broadcasted_iota(jnp.int32, (rows, rows), 0)
    other = lax.broadcasted_iota(jnp.int32, (rows, rows), 1)
    eye = jnp.where(own == other, 1.0, 0.0)
    links = jnp.where(parent_ref[...] == own, 1.0, 0.0)
    reach = dot_rows(eye.astype(jnp.bfloat16), jnp.maximum(links, eye).astype(jnp.bfloat16))
    for _ in range((rows - 1).bit_length()):
        square = reach.astype(jnp.bfloat16)
        reach = jnp.minimum(dot(square, square), 1.0)
    reach_out[...] = reach
    lane = lax.broadcasted_iota(jnp.int32, (rows, head), 1)
    place_in_half = jnp.where(lane < half, lane, lane - half).astype(jnp.float32)
    freq = jnp.exp(place_in_half * np.float32(-2.0 / head * np.log(ROPE_BASE)))
    angle = (jnp.sum(reach, axis=-1, keepdims=True) - 1.0) * freq
    sine = jnp.sin(angle)
    cosine_out[...] = jnp.cos(angle)
    sine_out[...] = jnp.where(lane < half, -sine, sine)
    for copy in copies:
        copy.wait()
    owner_out[...] = jnp.full(owner_out.shape, place[request], jnp.int32)


def tables(request, place, lifts, parents, after):
    rows = parents.shape[1]
    shapes = [(a.shape[1:], a.dtype) for a in lifts]
    shapes += [((8, LANES), jnp.int32)]
    shapes += [((rows, HEAD_SIZE), jnp.float32)] * 2 + [((rows, rows), jnp.float32)]
    return pl.pallas_call(
        table_kernel,
        out_shape=tuple(VMEM(*a) for a in shapes),
        in_specs=[SCALAR] + [FAR] * 3 + [WHOLE] * 2,
        out_specs=(WHOLE,) * len(shapes),
        scratch_shapes=[
            pltpu.SMEM(place.shape, jnp.int32),
            pltpu.SemaphoreType.DMA((3,)),
        ],
        name="tables",
        compiler_params=pltpu.CompilerParams(vmem_limit_bytes=2 << 20),
    )(request, *[distant(a) for a in (place, *lifts)], near(parents), near(after))


def dot_chunks(left, weight_ref):
    depth = weight_ref.shape[0]
    step = min(depth, CHUNK)
    total = dot(left[:, :step], weight_ref[:step, :])
    for at in range(step, depth, step):
        total = total + dot(left[:, at : at + step], weight_ref[at : at + step, :])
    return total


def gain_block(gain_ref, index, cols):
    count = cols // LANES
    lines = [gain_ref[index * count + j : index * count + j + 1, :] for j in range(count)]
    return jnp.concatenate([line.astype(jnp.float32) for line in lines], axis=1)


def core_index():
    return lax.axis_index("tp") & 1


def in_order(mine, theirs, flag):
    mine = mine.astype(jnp.float32)
    theirs = theirs.astype(jnp.float32)
    return jnp.where(flag, mine, theirs), jnp.where(flag, theirs, mine)


def fold(low):
    rows, rank = low.shape
    padded = jnp.concatenate([low, jnp.zeros((rows, LANES - rank), jnp.float32)], axis=1)
    return (padded[:rank] + pltpu.roll(padded[rank:], LANES // 2, 1)).astype(jnp.bfloat16)


def unfold(folded):
    rank = folded.shape[0]
    low = jnp.concatenate([folded, pltpu.roll(folded, LANES // 2, 1)], axis=0)
    return low[:, :rank]


def features(ref, chip, rows, cols):
    if ref.shape[2] == cols:
        return ref[chip].astype(jnp.float32)
    lanes = ref.shape[2]
    blocks = [ref[chip, j * rows : (j + 1) * rows, :] for j in range(cols // lanes)]
    return jnp.concatenate(blocks, axis=1).astype(jnp.float32)


def norm_blocks(mine_ref, theirs_ref, gain_ref, scratch, cols):
    chips = mine_ref.shape[0]
    first = core_index() == 0
    rows = scratch.shape[0]
    squares = jnp.zeros((rows, cols), jnp.float32)
    for chip in range(chips):
        for ref in (mine_ref, theirs_ref):
            wide = features(ref, chip, rows, cols)
            squares = squares + wide * wide
    mean_sq = jnp.sum(squares, axis=-1, keepdims=True) / (2 * chips * cols)
    scale = lax.rsqrt(mean_sq + EPS)
    for chip in range(chips):
        mine = features(mine_ref, chip, rows, cols)
        pair = in_order(mine, features(theirs_ref, chip, rows, cols), first)
        for side in range(2):
            low = (2 * chip + side) * cols
            gain = gain_block(gain_ref, 2 * chip + side, cols)
            scratch[:, low : low + cols] = (pair[side] * scale * gain).astype(jnp.bfloat16)
    return scale


def project_kernel(
    mine_ref, theirs_ref, gain_ref, owner_ref, other_ref, key_ref, value_ref, factor_ref,
    normed_out, pair_out, payload_out,
):
    chips, rows, cols = mine_ref.shape
    core = core_index()
    norm_blocks(mine_ref, theirs_ref, gain_ref, normed_out, cols)
    normed = normed_out[...]
    rank = factor_ref.shape[0] // 2
    here = (owner_ref[:1, :1] & 1) == core
    low = jnp.where(
        here, dot_rows(normed, factor_ref[:rank, :]), dot_rows(normed, other_ref[:rank, :])
    )
    half = key_ref.shape[0]
    pair_out[:, :half] = dot_rows(normed, key_ref[...]).astype(jnp.bfloat16)
    pair_out[:, half:] = dot_rows(normed, value_ref[...]).astype(jnp.bfloat16)
    folded = fold(low)
    for chip in range(chips):
        at = pl.multiple_of((2 * chip + core) * cols, cols)
        own = factor_ref[rank:, pl.ds(at, cols)].astype(jnp.float32)
        other = other_ref[rank:, pl.ds(at, cols)].astype(jnp.float32)
        payload_out[chip, :, :cols] = jnp.where(here, own, other).astype(jnp.bfloat16)
        payload_out[chip, :, cols:] = folded


def query_kernel(normed_ref, query_ref, query_out):
    query_out[...] = dot_chunks(normed_ref[...], query_ref)


def side_product(left, weight_ref, side, out):
    chips, _, cols = out.shape
    for chip in range(chips):
        at = pl.multiple_of((2 * chip + side) * cols, cols)
        out[chip] = dot(left, weight_ref[:, pl.ds(at, cols)]).astype(out.dtype)


def attend_kernel(
    query_ref, pair_mine, pair_theirs, owner_ref, got_ref, lift_ref, cosine_ref, sine_ref,
    reach_ref, output_ref, mixed_out, theirs_out, piece_out,
):
    rows, query_cols = query_ref.shape
    chips, _, cols = theirs_out.shape
    head = HEAD_SIZE
    heads = query_cols // head
    half = head // 2
    owner = owner_ref[:1, :1]
    piece = jnp.zeros(got_ref.shape[1:], jnp.float32)
    for chip in range(chips):
        sent = got_ref[chip].astype(jnp.float32)
        piece = piece + jnp.where((owner >> 1) == chip, sent, 0.0)
    piece_out[...] = piece.astype(jnp.bfloat16)
    low = unfold(piece[:, cols:])
    lane = lax.broadcasted_iota(jnp.int32, (rows, head), 1)
    cosine = cosine_ref[...]
    sine = sine_ref[...]

    def rotate(wide):
        return (wide * cosine + pltpu.roll(wide, half, 1) * sine).astype(jnp.bfloat16)

    first = core_index() == 0
    even, odd = in_order(pair_mine[...], pair_theirs[...], first)
    key = rotate(jnp.where(lane < half, even, pltpu.roll(odd, half, 1)))
    value = jnp.where(lane < half, pltpu.roll(even, half, 1), odd).astype(jnp.bfloat16)
    query = query_ref[...] + dot(low.astype(jnp.bfloat16), lift_ref[...])
    query = query.astype(jnp.bfloat16).astype(jnp.float32)
    stacked = jnp.concatenate(
        [rotate(query[:, h * head : (h + 1) * head]) for h in range(heads)], axis=0
    )
    scores = dot_rows(stacked, key) * head ** (-0.5)
    weights = jnp.exp(scores) * jnp.concatenate([reach_ref[...]] * heads, axis=0)
    probs = (weights / jnp.sum(weights, axis=-1, keepdims=True)).astype(jnp.bfloat16)
    mixed = dot(probs, value).astype(jnp.bfloat16)
    mixed = jnp.concatenate([mixed[h * rows : (h + 1) * rows] for h in range(heads)], axis=1)
    mixed_out[...] = mixed
    side_product(mixed, output_ref, 1 - core_index(), theirs_out)


def rest_kernel(mixed_ref, output_ref, mine_out):
    side_product(mixed_ref[...], output_ref, core_index(), mine_out)


def hidden_kernel(
    got_ref, token_ref, gain_ref, piece_ref,
    hidden_out, payload_out,
):
    chips, rows, cols = got_ref.shape
    total = token_ref[...].astype(jnp.float32)
    added = got_ref[0].astype(jnp.float32)
    for chip in range(1, chips):
        added = added + got_ref[chip].astype(jnp.float32)
    hidden = (total + added).astype(jnp.bfloat16)
    hidden_out[...] = hidden
    factor = piece_ref[:, :cols]
    rank = factor.shape[0]
    device = lax.axis_index("tp")
    gain = gain_block(gain_ref, 0, cols)
    for index in range(1, 2 * chips):
        gain = jnp.where(device == index, gain_block(gain_ref, index, cols), gain)
    gained = hidden.astype(jnp.float32) * gain
    low = dot_rows(gained.astype(jnp.bfloat16), factor)
    folded = fold(low)
    for chip in range(chips):
        for j in range(cols // LANES):
            part = hidden[:, j * LANES : (j + 1) * LANES]
            payload_out[chip, j * rows : (j + 1) * rows, :] = part
        payload_out[chip, -rank:, :] = folded


def down_copies(down_ref, held, sem, side):
    chips, _, cols = held.shape

    def copy(chip):
        part = pl.ds(pl.multiple_of((2 * chip + side) * cols, LANES), cols)
        return pltpu.make_async_copy(down_ref.at[:, part], held.at[chip], sem.at[chip])

    return copy


def forward_kernel(
    mine_ref, theirs_ref, gain_ref, lift_ref, gate_ref, up_ref, down_ref,
    active_out, theirs_out, held_out, scratch, held, sem, sem_out,
):
    chips, rows, cols = theirs_out.shape
    core = core_index()
    rank = lift_ref.shape[0]
    first = down_copies(down_ref, held, sem, 1 - core)
    second = down_copies(down_ref, held_out, sem_out, core)

    @pl.loop(0, chips)
    def _(chip):
        first(chip).start()

    @pl.loop(0, chips)
    def _(chip):
        second(chip).start()

    scale = norm_blocks(mine_ref, theirs_ref, gain_ref, scratch, cols)
    folded = jnp.zeros((rank, LANES), jnp.float32)
    for chip in range(chips):
        for ref in (mine_ref, theirs_ref):
            folded = folded + ref[chip, -rank:, :].astype(jnp.float32)
    low = (unfold(folded) * scale).astype(jnp.bfloat16)
    normed = scratch[...]
    gate = dot_chunks(normed, gate_ref)
    upper = dot_chunks(normed, up_ref) + dot(low, lift_ref[...])
    active_out[...] = (gate * jax.nn.sigmoid(gate) * upper).astype(jnp.bfloat16)

    @pl.loop(0, chips)
    def _(chip):
        first(chip).wait()
        theirs_out[chip] = dot(active_out[...], held[chip]).astype(theirs_out.dtype)

    @pl.loop(0, chips)
    def _(chip):
        second(chip).wait()


def last_kernel(active_ref, held_ref, mine_out):
    for chip in range(mine_out.shape[0]):
        mine_out[chip] = dot(active_ref[...], held_ref[chip])


def fast_body(
    tokens,
    attention_gain,
    forward_gain,
    query_weight,
    key_matrix,
    value_matrix,
    output_weight,
    gate_weight,
    up_weight,
    down_weight,
    adapter_inputs,
    adapter_query,
    adapter_upper,
    adapter_place,
    request_adapter,
    tree_parents,
):
    rows, cols = tokens.shape
    chips = lax.axis_size("tp") // 2
    width = query_weight.shape[0]
    shape = jax.ShapeDtypeStruct
    bf16, f32 = jnp.bfloat16, jnp.float32
    tall = rows * cols // LANES + adapter_query.shape[1]
    heavy = (gate_weight, up_weight, down_weight)
    most = heavy + (query_weight, output_weight)
    rank = adapter_query.shape[1]
    factors = adapter_inputs[0].T

    spread_tokens, kept_tokens, gain_one, gain_two, parents = spread(
        tokens,
        (attention_gain.reshape(-1, LANES), forward_gain.reshape(-1, LANES), tree_parents),
        heavy,
        chips,
    )
    mine = exchange(spread_tokens, "tp")
    mine, held = lax.optimization_barrier((mine, adapter_inputs))
    theirs = partner_2(mine, "tp", 0)
    factors_theirs = partner_2(held, "tp", 0)[0].T
    query_lift, up_lift, owner, cosine, sine, reach = tables(
        request_adapter, adapter_place, (adapter_query, adapter_upper), parents, mine
    )
    normed, pair, payload = call(
        project_kernel,
        "project",
        (
            shape((rows, width), bf16),
            shape((rows, 2 * key_matrix.shape[1]), bf16),
            shape((chips, rank, cols + LANES), bf16),
        ),
        (mine, theirs, gain_one, owner, factors_theirs),
        (key_matrix.T, value_matrix.T, factors),
    )
    pair_theirs = partner_2(pair, "tp", 0)
    (query,) = call(
        query_kernel,
        "query",
        (shape((rows, query_weight.shape[1]), f32),),
        (normed,),
        (query_weight,),
        heavy,
    )
    pair_theirs, query, payload = lax.optimization_barrier((pair_theirs, query, payload))
    mixed, sent, piece = call(
        attend_kernel,
        "attend",
        (
            shape((rows, query_weight.shape[1]), bf16),
            shape((chips, rows, cols), bf16),
            shape(payload.shape[1:], bf16),
        ),
        (
            query, pair, pair_theirs, owner, exchange(payload, "tp"), query_lift, cosine,
            sine, reach,
        ),
        (output_weight,),
        heavy + (query_weight,),
    )
    sent_theirs = partner_2(sent, "tp", 0)
    (kept,) = call(
        rest_kernel, "rest", (shape((chips, rows, cols), f32),), (mixed,), (output_weight,)
    )
    chip_sum = (kept + sent_theirs.astype(f32)).astype(bf16)
    hidden, payload = call(
        hidden_kernel,
        "hidden",
        (shape((rows, cols), bf16), shape((chips, tall, LANES), bf16)),
        (exchange(chip_sum, "tp"), kept_tokens, gain_two, piece),
        (),
        most,
    )
    mine = exchange(payload, "tp")
    theirs = partner_2(mine, "tp", 0)
    held = shape((chips, down_weight.shape[0], cols), bf16)
    active, sent, held_mine = call(
        forward_kernel,
        "forward",
        (
            shape((rows, gate_weight.shape[1]), bf16),
            shape((chips, rows, cols), bf16),
            held,
        ),
        (mine, theirs, gain_two, up_lift),
        (gate_weight, up_weight),
        (query_weight, output_weight),
        [
            VMEM((rows, width), bf16),
            VMEM(held.shape, bf16),
            pltpu.SemaphoreType.DMA((chips,)),
            pltpu.SemaphoreType.DMA((chips,)),
        ],
        far=(down_weight,),
        limit=10,
    )
    sent_theirs = partner_2(sent, "tp", 0)
    (kept,) = call(
        last_kernel, "last", (shape((chips, rows, cols), f32),), (active, held_mine)
    )
    chip_sum = (kept + sent_theirs.astype(f32)).astype(bf16)
    added = jnp.sum(exchange(chip_sum, "tp").astype(f32), axis=0)
    return (hidden.astype(f32) + added).astype(bf16)


def body(*args):
    tokens, key_matrix, query_weight = args[0], args[4], args[3]
    fits = (
        tokens.shape[1] % LANES == 0
        and query_weight.shape[1] % HEAD_SIZE == 0
        and key_matrix.shape[1] * 2 == HEAD_SIZE
        and args[10].shape[0] == 1
        and args[14].shape[0] == 1
        and args[10].shape[2] == tokens.shape[0]
    )
    return fast_body(*args) if fits else general_body(*args)


def solution(mesh):
    return jax.shard_map(
        body,
        mesh=mesh,
        in_specs=(
            P("rep", "tp"),
            P(),
            P(),
            P(None, "tp"),
            P(None, "tp"),
            P(None, "tp"),
            P("tp", None),
            P(None, "tp"),
            P(None, "tp"),
            P("tp", None),
            P(("rep", "tp"), None, None),
            P("rep", None, "tp"),
            P("rep", None, "tp"),
            P("rep"),
            P("rep"),
            P("rep", None),
        ),
        out_specs=P("rep", "tp"),
        check_vma=False,
    )
```

```python
import jax
import jax.numpy as jnp
import numpy as np
from jax import lax
from jax.experimental import pallas as pl
from jax.experimental.pallas import tpu as pltpu
from jax.sharding import PartitionSpec as P

HEAD_SIZE = 128


EPS = 1e-05
ROPE_BASE = 500000.0


def core_groups(axis):
    count = lax.axis_size(axis)
    return [list(range(core, count, 2)) for core in range(2)]


def exchange(blocks, axis):
    return lax.all_to_all(
        blocks, axis, 0, 0, axis_index_groups=core_groups(axis), tiled=True
    )


def by_core(mine, theirs, core):
    even = jnp.where(core == 0, mine, theirs)
    odd = jnp.where(core == 0, theirs, mine)
    return jnp.stack([even, odd], axis=1)


def gather_features(part, axis):
    chips = lax.axis_size(axis) // 2
    core = lax.axis_index(axis) & 1
    mine = exchange(jnp.broadcast_to(part[None], (chips,) + part.shape), axis)
    theirs = partner_2(mine, axis, 0)
    both = by_core(mine, theirs, core).reshape((2 * chips,) + part.shape)
    return jnp.moveaxis(both, 0, 1).reshape(part.shape[0], -1)


def sum_features(partial, axis):
    count = lax.axis_size(axis)
    core = lax.axis_index(axis) & 1
    rows = partial.shape[0]
    split = partial.reshape(rows, count // 2, 2, -1)
    even = split[:, :, 0]
    odd = split[:, :, 1]
    mine = jnp.where(core == 0, even, odd)
    theirs = jnp.where(core == 0, odd, even).astype(jnp.bfloat16)
    pair = (mine + partner_2(theirs, axis, 0).astype(jnp.float32)).astype(jnp.bfloat16)
    got = exchange(jnp.moveaxis(pair, 1, 0), axis)
    return jnp.sum(got.astype(jnp.float32), axis=0)


def from_owner(mine, owner, axis):
    core = lax.axis_index(axis) & 1
    held = jnp.where(lax.axis_index(axis) == owner, mine, jnp.zeros_like(mine))
    held = held + partner_2(held, axis, 0)
    chips = lax.axis_size(axis) // 2
    got = exchange(jnp.broadcast_to(held[None], (chips,) + held.shape), axis)
    return lax.dynamic_index_in_dim(got, owner >> 1, 0, keepdims=False)


def partner_2(block, axis, distance):
    count = lax.axis_size(axis)
    route = []
    for low in range(count):
        high = low | 1 << distance
        if high != low and high < count:
            route += [(low, high), (high, low)]
    return lax.ppermute(block, axis, route)


def rms_scale(rows, gain):
    wide = rows.astype(jnp.float32)
    mean_sq = jnp.mean(wide * wide, axis=-1, keepdims=True)
    return (wide * lax.rsqrt(mean_sq + EPS) * gain.astype(jnp.float32)).astype(jnp.bfloat16)


def ancestry(parents):
    tree_width = parents.shape[-1]
    places = jnp.arange(tree_width, dtype=jnp.int32)
    links = (parents[:, :, None] == places[None, None, :]).astype(jnp.float32)
    reach = jnp.maximum(links, jnp.eye(tree_width, dtype=jnp.float32)[None])
    for step in range(int(tree_width).bit_length()):
        reach = jnp.minimum(
            jnp.einsum("rij,rjk->rik", reach, reach, precision=lax.Precision.HIGHEST), 1.0
        )
    tree_depth = jnp.sum(reach, axis=-1) - 1.0
    return (reach, tree_depth)


def apply_rotary(heads, tree_depth):
    half = heads.shape[-1] // 2
    freq = ROPE_BASE ** (-jnp.arange(half, dtype=jnp.float32) * 2.0 / heads.shape[-1])
    angle = tree_depth[:, :, None] * freq[None, None, :]
    cosine = jnp.cos(angle)[:, :, None, :]
    sine = jnp.sin(angle)[:, :, None, :]
    wide = heads.astype(jnp.float32)
    first = wide[..., :half]
    second = wide[..., half:]
    return jnp.concatenate(
        [first * cosine - second * sine, second * cosine + first * sine], axis=-1
    ).astype(jnp.bfloat16)


def join_pair(mine, theirs, flag):
    lower = jnp.concatenate([mine, theirs], axis=1)
    upper = jnp.concatenate([theirs, mine], axis=1)
    return jnp.where(flag == 1, upper, lower)


def general_body(
    tokens,
    attention_gain,
    forward_gain,
    query_weight,
    key_matrix,
    value_matrix,
    output_weight,
    gate_weight,
    up_weight,
    down_weight,
    adapter_inputs,
    adapter_query,
    adapter_upper,
    adapter_place,
    request_adapter,
    tree_parents,
):
    device = lax.axis_index("tp")
    rows = tokens.shape[0]
    request_list = request_adapter.shape[0]
    tree_width = rows // request_list
    rank = adapter_query.shape[1]
    pool_local = adapter_inputs.shape[0]
    head = HEAD_SIZE
    full_tokens = gather_features(tokens, "tp")
    normed = rms_scale(full_tokens, attention_gain)
    slots = adapter_place[request_adapter]
    owner = slots[0] // pool_local
    factors = lax.dynamic_index_in_dim(adapter_inputs, slots[0] % pool_local, 0, keepdims=False)
    low_held = jnp.dot(normed, factors[:, :rank], preferred_element_type=jnp.float32).astype(
        jnp.bfloat16
    )
    low_query = from_owner(low_held, owner, "tp")[None]
    lift = jnp.einsum(
        "rtk,rkc->rtc",
        low_query,
        adapter_query[request_adapter],
        preferred_element_type=jnp.float32,
    )
    query_local = (
        jnp.dot(normed, query_weight, preferred_element_type=jnp.float32) + lift.reshape(rows, -1)
    ).astype(jnp.bfloat16)
    key_local = jnp.dot(normed, key_matrix, preferred_element_type=jnp.float32).astype(jnp.bfloat16)
    value_local = jnp.dot(normed, value_matrix, preferred_element_type=jnp.float32).astype(
        jnp.bfloat16
    )
    query_cols = query_weight.shape[1]
    query_steps = max(0, (head // query_cols).bit_length() - 1)
    key_steps = (head // key_matrix.shape[1]).bit_length() - 1
    for bit in range(key_steps):
        flag = device >> bit & 1
        key_width = key_local.shape[1]
        with_query = bit < query_steps
        if with_query:
            query_width = query_local.shape[1]
            packed = jnp.concatenate([query_local, key_local, value_local], axis=1)
        else:
            query_width = 0
            packed = jnp.concatenate([key_local, value_local], axis=1)
        partner = partner_2(packed, "tp", bit)
        if with_query:
            query_local = join_pair(query_local, partner[:, :query_width], flag)
        key_other = partner[:, query_width : query_width + key_width]
        value_other = partner[:, query_width + key_width :]
        key_local = join_pair(key_local, key_other, flag)
        value_local = join_pair(value_local, value_other, flag)
    reach, tree_depth = ancestry(tree_parents)
    local_heads = query_local.shape[1] // head
    query_rotated = apply_rotary(
        query_local.reshape(request_list, tree_width, local_heads, head), tree_depth
    )
    key_rotated = apply_rotary(key_local.reshape(request_list, tree_width, 1, head), tree_depth)[
        :, :, 0, :
    ]
    heads_value = value_local.reshape(request_list, tree_width, head)
    scores = jnp.einsum(
        "rqhd,rkd->rhqk", query_rotated, key_rotated, preferred_element_type=jnp.float32
    ) * head ** (-0.5)
    weights = jnp.exp(scores) * reach[:, None, :, :]
    probs = (weights / jnp.sum(weights, axis=-1, keepdims=True)).astype(jnp.bfloat16)
    mixed = jnp.einsum(
        "rhqk,rkd->rqhd", probs, heads_value, preferred_element_type=jnp.float32
    ).astype(jnp.bfloat16)
    mixed = mixed.reshape(rows, local_heads * head)
    offset = (device & (1 << query_steps) - 1) * query_cols
    own_mixed = lax.dynamic_slice_in_dim(mixed, offset, query_cols, 1)
    partial_out = jnp.dot(own_mixed, output_weight, preferred_element_type=jnp.float32)
    summed = sum_features(partial_out, "tp")
    hidden = (tokens.astype(jnp.float32) + summed).astype(jnp.bfloat16)
    hidden_full = gather_features(hidden, "tp")
    normed_two = rms_scale(hidden_full, forward_gain)
    low_held_two = jnp.dot(normed_two, factors[:, rank:], preferred_element_type=jnp.float32).astype(
        jnp.bfloat16
    )
    low_up = from_owner(low_held_two, owner, "tp")[None]
    lift_up = jnp.einsum(
        "rtk,rkc->rtc", low_up, adapter_upper[request_adapter], preferred_element_type=jnp.float32
    )
    gate = jnp.dot(normed_two, gate_weight, preferred_element_type=jnp.float32)
    upper = jnp.dot(normed_two, up_weight, preferred_element_type=jnp.float32) + lift_up.reshape(
        rows, -1
    )
    active = (jax.nn.silu(gate) * upper).astype(jnp.bfloat16)
    forward = jnp.dot(active, down_weight, preferred_element_type=jnp.float32)
    forward_part = sum_features(forward, "tp")
    return (hidden.astype(jnp.float32) + forward_part).astype(jnp.bfloat16)


VMEM = pltpu.VMEM
WHOLE = pl.BlockSpec(memory_space=pltpu.VMEM)
SCALAR = pl.BlockSpec(memory_space=pltpu.SMEM)
FAR = pl.BlockSpec(memory_space=pltpu.HBM)
ROW_DOT = (((1,), (1,)), ((), ()))
LANES = 128
CHUNK = 1024


def dot(a, b):
    return jnp.dot(a, b, preferred_element_type=jnp.float32)


def dot_rows(a, b):
    return lax.dot_general(a, b, ROW_DOT, preferred_element_type=jnp.float32)


def call(kernel, name, outs, args, weights=(), ahead=(), scratch=(), limit=6, far=()):
    outs = tuple(VMEM(o.shape, o.dtype) for o in outs)
    size = sum(w.size for w in weights + far)
    used = len(args) + len(weights) + len(far)

    def run(*refs):
        kernel(*refs[:used], *refs[used + len(ahead) :])

    return pl.pallas_call(
        run,
        out_shape=outs,
        in_specs=[WHOLE] * (len(args) + len(weights)) + [FAR] * len(far + ahead),
        out_specs=(WHOLE,) * len(outs),
        scratch_shapes=list(scratch),
        name=name,
        cost_estimate=pl.CostEstimate(
            flops=64 * size, bytes_accessed=2 * size, transcendentals=0
        ),
        compiler_params=pltpu.CompilerParams(vmem_limit_bytes=limit << 20),
    )(
        *[pltpu.with_memory_space_constraint(w, VMEM) for w in args + weights],
        *[pltpu.with_memory_space_constraint(w, pltpu.HBM) for w in far + ahead],
    )


def near(x):
    return pltpu.with_memory_space_constraint(x, VMEM)


def distant(x):
    return pltpu.with_memory_space_constraint(x, pltpu.HBM)


def spread(tokens, kept, ahead, chips):
    outs = (VMEM((chips,) + tokens.shape, tokens.dtype),)
    outs += tuple(VMEM(a.shape, a.dtype) for a in (tokens, *kept))
    used = 1 + len(kept)

    def kernel(*refs):
        ins, outs, sem = refs[:used], refs[used + len(ahead) : -1], refs[-1]
        pairs = [(ins[0], outs[0].at[chip]) for chip in range(chips)]
        pairs += [(ins[k], outs[1 + k]) for k in range(used)]
        copies = [
            pltpu.make_async_copy(src, dst, sem.at[k]) for k, (src, dst) in enumerate(pairs)
        ]
        for copy in copies:
            copy.start()
        for copy in copies:
            copy.wait()

    return pl.pallas_call(
        kernel,
        out_shape=outs,
        in_specs=[FAR] * (used + len(ahead)),
        out_specs=(WHOLE,) * len(outs),
        scratch_shapes=[pltpu.SemaphoreType.DMA((chips + used,))],
        name="spread",
        compiler_params=pltpu.CompilerParams(vmem_limit_bytes=2 << 20),
    )(*[distant(a) for a in (tokens, *kept, *ahead)])


def table_kernel(
    request_ref, place_ref, query_ref, up_ref, parent_ref, after_ref,
    query_out, up_out, owner_out, cosine_out, sine_out, reach_out, place, sem,
):
    request = request_ref[0]
    copies = [
        pltpu.make_async_copy(place_ref, place, sem.at[0]),
        pltpu.make_async_copy(query_ref.at[request], query_out, sem.at[1]),
        pltpu.make_async_copy(up_ref.at[request], up_out, sem.at[2]),
    ]
    for copy in copies:
        copy.start()
    rows, head = cosine_out.shape
    half = head // 2
    own = lax.broadcasted_iota(jnp.int32, (rows, rows), 0)
    other = lax.broadcasted_iota(jnp.int32, (rows, rows), 1)
    eye = jnp.where(own == other, 1.0, 0.0)
    links = jnp.where(parent_ref[...] == own, 1.0, 0.0)
    reach = dot_rows(eye.astype(jnp.bfloat16), jnp.maximum(links, eye).astype(jnp.bfloat16))
    for _ in range((rows - 1).bit_length()):
        square = reach.astype(jnp.bfloat16)
        reach = jnp.minimum(dot(square, square), 1.0)
    reach_out[...] = reach
    lane = lax.broadcasted_iota(jnp.int32, (rows, head), 1)
    place_in_half = jnp.where(lane < half, lane, lane - half).astype(jnp.float32)
    freq = jnp.exp(place_in_half * np.float32(-2.0 / head * np.log(ROPE_BASE)))
    angle = (jnp.sum(reach, axis=-1, keepdims=True) - 1.0) * freq
    sine = jnp.sin(angle)
    cosine_out[...] = jnp.cos(angle)
    sine_out[...] = jnp.where(lane < half, -sine, sine)
    for copy in copies:
        copy.wait()
    owner_out[...] = jnp.full(owner_out.shape, place[request], jnp.int32)


def tables(request, place, lifts, parents, after):
    rows = parents.shape[1]
    shapes = [(a.shape[1:], a.dtype) for a in lifts]
    shapes += [((8, LANES), jnp.int32)]
    shapes += [((rows, HEAD_SIZE), jnp.float32)] * 2 + [((rows, rows), jnp.float32)]
    return pl.pallas_call(
        table_kernel,
        out_shape=tuple(VMEM(*a) for a in shapes),
        in_specs=[SCALAR] + [FAR] * 3 + [WHOLE] * 2,
        out_specs=(WHOLE,) * len(shapes),
        scratch_shapes=[
            pltpu.SMEM(place.shape, jnp.int32),
            pltpu.SemaphoreType.DMA((3,)),
        ],
        name="tables",
        compiler_params=pltpu.CompilerParams(vmem_limit_bytes=2 << 20),
    )(request, *[distant(a) for a in (place, *lifts)], near(parents), near(after))


def dot_chunks(left, weight_ref):
    depth = weight_ref.shape[0]
    step = min(depth, CHUNK)
    total = dot(left[:, :step], weight_ref[:step, :])
    for at in range(step, depth, step):
        total = total + dot(left[:, at : at + step], weight_ref[at : at + step, :])
    return total


def gain_block(gain_ref, index, cols):
    count = cols // LANES
    lines = [gain_ref[index * count + j : index * count + j + 1, :] for j in range(count)]
    return jnp.concatenate([line.astype(jnp.float32) for line in lines], axis=1)


def core_index():
    return lax.axis_index("tp") & 1


def in_order(mine, theirs, flag):
    mine = mine.astype(jnp.float32)
    theirs = theirs.astype(jnp.float32)
    return jnp.where(flag, mine, theirs), jnp.where(flag, theirs, mine)


def fold(low):
    rows, rank = low.shape
    padded = jnp.concatenate([low, jnp.zeros((rows, LANES - rank), jnp.float32)], axis=1)
    return (padded[:rank] + pltpu.roll(padded[rank:], LANES // 2, 1)).astype(jnp.bfloat16)


def unfold(folded):
    rank = folded.shape[0]
    low = jnp.concatenate([folded, pltpu.roll(folded, LANES // 2, 1)], axis=0)
    return low[:, :rank]


def features(ref, chip, rows, cols):
    if ref.shape[2] == cols:
        return ref[chip].astype(jnp.float32)
    lanes = ref.shape[2]
    blocks = [ref[chip, j * rows : (j + 1) * rows, :] for j in range(cols // lanes)]
    return jnp.concatenate(blocks, axis=1).astype(jnp.float32)


def norm_blocks(mine_ref, theirs_ref, gain_ref, scratch, cols):
    chips = mine_ref.shape[0]
    first = core_index() == 0
    rows = scratch.shape[0]
    squares = jnp.zeros((rows, cols), jnp.float32)
    for chip in range(chips):
        for ref in (mine_ref, theirs_ref):
            wide = features(ref, chip, rows, cols)
            squares = squares + wide * wide
    mean_sq = jnp.sum(squares, axis=-1, keepdims=True) / (2 * chips * cols)
    scale = lax.rsqrt(mean_sq + EPS)
    for chip in range(chips):
        mine = features(mine_ref, chip, rows, cols)
        pair = in_order(mine, features(theirs_ref, chip, rows, cols), first)
        for side in range(2):
            low = (2 * chip + side) * cols
            gain = gain_block(gain_ref, 2 * chip + side, cols)
            scratch[:, low : low + cols] = (pair[side] * scale * gain).astype(jnp.bfloat16)
    return scale


def project_kernel(
    mine_ref, theirs_ref, gain_ref, owner_ref, other_ref, key_ref, value_ref, factor_ref,
    normed_out, pair_out, payload_out,
):
    chips, rows, cols = mine_ref.shape
    core = core_index()
    norm_blocks(mine_ref, theirs_ref, gain_ref, normed_out, cols)
    normed = normed_out[...]
    rank = factor_ref.shape[0] // 2
    here = (owner_ref[:1, :1] & 1) == core
    low = jnp.where(
        here, dot_rows(normed, factor_ref[:rank, :]), dot_rows(normed, other_ref[:rank, :])
    )
    half = key_ref.shape[0]
    pair_out[:, :half] = dot_rows(normed, key_ref[...]).astype(jnp.bfloat16)
    pair_out[:, half:] = dot_rows(normed, value_ref[...]).astype(jnp.bfloat16)
    folded = fold(low)
    for chip in range(chips):
        at = pl.multiple_of((2 * chip + core) * cols, cols)
        own = factor_ref[rank:, pl.ds(at, cols)].astype(jnp.float32)
        other = other_ref[rank:, pl.ds(at, cols)].astype(jnp.float32)
        payload_out[chip, :, :cols] = jnp.where(here, own, other).astype(jnp.bfloat16)
        payload_out[chip, :, cols:] = folded


def query_kernel(normed_ref, query_ref, query_out):
    query_out[...] = dot_chunks(normed_ref[...], query_ref)


def side_product(left, weight_ref, side, out):
    chips, _, cols = out.shape
    for chip in range(chips):
        at = pl.multiple_of((2 * chip + side) * cols, cols)
        out[chip] = dot(left, weight_ref[:, pl.ds(at, cols)]).astype(out.dtype)


def attend_kernel(
    query_ref, pair_mine, pair_theirs, owner_ref, got_ref, lift_ref, cosine_ref, sine_ref,
    reach_ref, output_ref, mixed_out, theirs_out, piece_out,
):
    rows, query_cols = query_ref.shape
    chips, _, cols = theirs_out.shape
    head = HEAD_SIZE
    heads = query_cols // head
    half = head // 2
    owner = owner_ref[:1, :1]
    piece = jnp.zeros(got_ref.shape[1:], jnp.float32)
    for chip in range(chips):
        sent = got_ref[chip].astype(jnp.float32)
        piece = piece + jnp.where((owner >> 1) == chip, sent, 0.0)
    piece_out[...] = piece.astype(jnp.bfloat16)
    low = unfold(piece[:, cols:])
    lane = lax.broadcasted_iota(jnp.int32, (rows, head), 1)
    cosine = cosine_ref[...]
    sine = sine_ref[...]

    def rotate(wide):
        return (wide * cosine + pltpu.roll(wide, half, 1) * sine).astype(jnp.bfloat16)

    first = core_index() == 0
    even, odd = in_order(pair_mine[...], pair_theirs[...], first)
    key = rotate(jnp.where(lane < half, even, pltpu.roll(odd, half, 1)))
    value = jnp.where(lane < half, pltpu.roll(even, half, 1), odd).astype(jnp.bfloat16)
    query = query_ref[...] + dot(low.astype(jnp.bfloat16), lift_ref[...])
    query = query.astype(jnp.bfloat16).astype(jnp.float32)
    stacked = jnp.concatenate(
        [rotate(query[:, h * head : (h + 1) * head]) for h in range(heads)], axis=0
    )
    scores = dot_rows(stacked, key) * head ** (-0.5)
    weights = jnp.exp(scores) * jnp.concatenate([reach_ref[...]] * heads, axis=0)
    probs = (weights / jnp.sum(weights, axis=-1, keepdims=True)).astype(jnp.bfloat16)
    mixed = dot(probs, value).astype(jnp.bfloat16)
    mixed = jnp.concatenate([mixed[h * rows : (h + 1) * rows] for h in range(heads)], axis=1)
    mixed_out[...] = mixed
    side_product(mixed, output_ref, 1 - core_index(), theirs_out)


def rest_kernel(mixed_ref, output_ref, mine_out):
    side_product(mixed_ref[...], output_ref, core_index(), mine_out)


def hidden_kernel(
    got_ref, token_ref, gain_ref, piece_ref,
    hidden_out, payload_out,
):
    chips, rows, cols = got_ref.shape
    total = token_ref[...].astype(jnp.float32)
    added = got_ref[0].astype(jnp.float32)
    for chip in range(1, chips):
        added = added + got_ref[chip].astype(jnp.float32)
    hidden = (total + added).astype(jnp.bfloat16)
    hidden_out[...] = hidden
    factor = piece_ref[:, :cols]
    rank = factor.shape[0]
    device = lax.axis_index("tp")
    gain = gain_block(gain_ref, 0, cols)
    for index in range(1, 2 * chips):
        gain = jnp.where(device == index, gain_block(gain_ref, index, cols), gain)
    gained = hidden.astype(jnp.float32) * gain
    low = dot_rows(gained.astype(jnp.bfloat16), factor)
    folded = fold(low)
    for chip in range(chips):
        for j in range(cols // LANES):
            part = hidden[:, j * LANES : (j + 1) * LANES]
            payload_out[chip, j * rows : (j + 1) * rows, :] = part
        payload_out[chip, -rank:, :] = folded


def down_copies(down_ref, held, sem, side, start=0):
    cols = held.shape[2]

    def copy(k):
        part = pl.ds(pl.multiple_of((2 * (k + start) + side) * cols, LANES), cols)
        return pltpu.make_async_copy(down_ref.at[:, part], held.at[k], sem.at[k])

    return copy


def half_products(block_ref, gain_ref, gate_ref, up_ref, side, rows, cols):
    gate = up = None
    for chip in range(block_ref.shape[0]):
        gain = jnp.where(
            side == 0, gain_block(gain_ref, 2 * chip, cols), gain_block(gain_ref, 2 * chip + 1, cols)
        )
        left = (features(block_ref, chip, rows, cols) * gain).astype(jnp.bfloat16)
        part = pl.ds(pl.multiple_of((2 * chip + side) * cols, cols), cols)
        gate_part = dot(left, gate_ref[part, :])
        up_part = dot(left, up_ref[part, :])
        gate = gate_part if gate is None else gate + gate_part
        up = up_part if up is None else up + up_part
    return gate, up


def near_kernel(
    mine_ref, gain_ref, gate_ref, up_ref, down_ref, gate_out, up_out, held_out, sem
):
    core = core_index()
    count, _, cols = held_out.shape
    copy = down_copies(down_ref, held_out, sem, 1 - core)

    @pl.loop(0, count)
    def _(k):
        copy(k).start()

    gate, up = half_products(
        mine_ref, gain_ref, gate_ref, up_ref, core, gate_out.shape[0], cols
    )
    gate_out[...] = gate
    up_out[...] = up

    @pl.loop(0, count)
    def _(k):
        copy(k).wait()


def forward_kernel(
    mine_ref, theirs_ref, gain_ref, lift_ref, gate_part, up_part, early_ref, gate_ref, up_ref,
    down_ref, active_out, theirs_out, held_out, held, sem, sem_out,
):
    chips, rows, cols = theirs_out.shape
    core = core_index()
    rank = lift_ref.shape[0]
    early = early_ref.shape[0]
    first = down_copies(down_ref, held, sem, 1 - core, early)
    second = down_copies(down_ref, held_out, sem_out, core)

    @pl.loop(0, chips - early)
    def _(k):
        first(k).start()

    @pl.loop(0, chips)
    def _(k):
        second(k).start()

    gate, up = half_products(theirs_ref, gain_ref, gate_ref, up_ref, 1 - core, rows, cols)
    squares = jnp.zeros((rows, cols), jnp.float32)
    folded = jnp.zeros((rank, LANES), jnp.float32)
    for chip in range(chips):
        for ref in (mine_ref, theirs_ref):
            wide = features(ref, chip, rows, cols)
            squares = squares + wide * wide
            folded = folded + ref[chip, -rank:, :].astype(jnp.float32)
    mean_sq = jnp.sum(squares, axis=-1, keepdims=True) / (2 * chips * cols)
    scale = lax.rsqrt(mean_sq + EPS)
    low = (unfold(folded) * scale).astype(jnp.bfloat16)
    gate = (gate + gate_part[...]) * scale
    upper = (up + up_part[...]) * scale + dot(low, lift_ref[...])
    active_out[...] = (gate * jax.nn.sigmoid(gate) * upper).astype(jnp.bfloat16)

    @pl.loop(0, early)
    def _(k):
        theirs_out[k] = dot(active_out[...], early_ref[k]).astype(theirs_out.dtype)

    @pl.loop(0, chips - early)
    def _(k):
        first(k).wait()
        theirs_out[k + early] = dot(active_out[...], held[k]).astype(theirs_out.dtype)

    @pl.loop(0, chips)
    def _(k):
        second(k).wait()


def last_kernel(active_ref, held_ref, mine_out):
    for chip in range(mine_out.shape[0]):
        mine_out[chip] = dot(active_ref[...], held_ref[chip])


def fast_body(
    tokens,
    attention_gain,
    forward_gain,
    query_weight,
    key_matrix,
    value_matrix,
    output_weight,
    gate_weight,
    up_weight,
    down_weight,
    adapter_inputs,
    adapter_query,
    adapter_upper,
    adapter_place,
    request_adapter,
    tree_parents,
):
    rows, cols = tokens.shape
    chips = lax.axis_size("tp") // 2
    width = query_weight.shape[0]
    shape = jax.ShapeDtypeStruct
    bf16, f32 = jnp.bfloat16, jnp.float32
    tall = rows * cols // LANES + adapter_query.shape[1]
    heavy = (gate_weight, up_weight, down_weight)
    most = heavy + (query_weight, output_weight)
    rank = adapter_query.shape[1]
    factors = adapter_inputs[0].T

    spread_tokens, kept_tokens, gain_one, gain_two, parents = spread(
        tokens,
        (attention_gain.reshape(-1, LANES), forward_gain.reshape(-1, LANES), tree_parents),
        heavy,
        chips,
    )
    mine = exchange(spread_tokens, "tp")
    mine, held = lax.optimization_barrier((mine, adapter_inputs))
    theirs = partner_2(mine, "tp", 0)
    factors_theirs = partner_2(held, "tp", 0)[0].T
    query_lift, up_lift, owner, cosine, sine, reach = tables(
        request_adapter, adapter_place, (adapter_query, adapter_upper), parents, mine
    )
    normed, pair, payload = call(
        project_kernel,
        "project",
        (
            shape((rows, width), bf16),
            shape((rows, 2 * key_matrix.shape[1]), bf16),
            shape((chips, rank, cols + LANES), bf16),
        ),
        (mine, theirs, gain_one, owner, factors_theirs),
        (key_matrix.T, value_matrix.T, factors),
    )
    pair_theirs = partner_2(pair, "tp", 0)
    (query,) = call(
        query_kernel,
        "query",
        (shape((rows, query_weight.shape[1]), f32),),
        (normed,),
        (query_weight,),
        heavy,
    )
    pair_theirs, query, payload = lax.optimization_barrier((pair_theirs, query, payload))
    mixed, sent, piece = call(
        attend_kernel,
        "attend",
        (
            shape((rows, query_weight.shape[1]), bf16),
            shape((chips, rows, cols), bf16),
            shape(payload.shape[1:], bf16),
        ),
        (
            query, pair, pair_theirs, owner, exchange(payload, "tp"), query_lift, cosine,
            sine, reach,
        ),
        (output_weight,),
        heavy + (query_weight,),
    )
    sent_theirs = partner_2(sent, "tp", 0)
    (kept,) = call(
        rest_kernel, "rest", (shape((chips, rows, cols), f32),), (mixed,), (output_weight,)
    )
    chip_sum = (kept + sent_theirs.astype(f32)).astype(bf16)
    hidden, payload = call(
        hidden_kernel,
        "hidden",
        (shape((rows, cols), bf16), shape((chips, tall, LANES), bf16)),
        (exchange(chip_sum, "tp"), kept_tokens, gain_two, piece),
        (),
        most,
    )
    mine = exchange(payload, "tp")
    theirs = partner_2(mine, "tp", 0)
    held = shape((chips, down_weight.shape[0], cols), bf16)
    half = chips // 2
    part = shape((rows, gate_weight.shape[1]), f32)
    gate_part, up_part, early = call(
        near_kernel,
        "near",
        (part, part, shape((half, *held.shape[1:]), bf16)),
        (mine, gain_two),
        (gate_weight, up_weight),
        (),
        [pltpu.SemaphoreType.DMA((half,))],
        far=(down_weight,),
        limit=8,
    )
    active, sent, held_mine = call(
        forward_kernel,
        "forward",
        (shape(part.shape, bf16), shape((chips, rows, cols), bf16), held),
        (mine, theirs, gain_two, up_lift, gate_part, up_part, early),
        (gate_weight, up_weight),
        (),
        [
            VMEM((chips - half, *held.shape[1:]), bf16),
            pltpu.SemaphoreType.DMA((chips - half,)),
            pltpu.SemaphoreType.DMA((chips,)),
        ],
        far=(down_weight,),
        limit=8,
    )
    sent_theirs = partner_2(sent, "tp", 0)
    (kept,) = call(
        last_kernel, "last", (shape((chips, rows, cols), f32),), (active, held_mine)
    )
    chip_sum = (kept + sent_theirs.astype(f32)).astype(bf16)
    added = jnp.sum(exchange(chip_sum, "tp").astype(f32), axis=0)
    return (hidden.astype(f32) + added).astype(bf16)


def body(*args):
    tokens, key_matrix, query_weight = args[0], args[4], args[3]
    fits = (
        tokens.shape[1] % LANES == 0
        and query_weight.shape[1] % HEAD_SIZE == 0
        and key_matrix.shape[1] * 2 == HEAD_SIZE
        and args[10].shape[0] == 1
        and args[14].shape[0] == 1
        and args[10].shape[2] == tokens.shape[0]
    )
    return fast_body(*args) if fits else general_body(*args)


def solution(mesh):
    return jax.shard_map(
        body,
        mesh=mesh,
        in_specs=(
            P("rep", "tp"),
            P(),
            P(),
            P(None, "tp"),
            P(None, "tp"),
            P(None, "tp"),
            P("tp", None),
            P(None, "tp"),
            P(None, "tp"),
            P("tp", None),
            P(("rep", "tp"), None, None),
            P("rep", None, "tp"),
            P("rep", None, "tp"),
            P("rep"),
            P("rep"),
            P("rep", None),
        ),
        out_specs=P("rep", "tp"),
        check_vma=False,
    )
```

```python
import jax
import jax.numpy as jnp
import numpy as np
from jax import lax
from jax.experimental import pallas as pl
from jax.experimental.pallas import tpu as pltpu
from jax.sharding import PartitionSpec as P

HEAD_SIZE = 128


EPS = 1e-05
ROPE_BASE = 500000.0


def core_groups(axis):
    count = lax.axis_size(axis)
    return [list(range(core, count, 2)) for core in range(2)]


def exchange(blocks, axis):
    return lax.all_to_all(
        blocks, axis, 0, 0, axis_index_groups=core_groups(axis), tiled=True
    )


def by_core(mine, theirs, core):
    even = jnp.where(core == 0, mine, theirs)
    odd = jnp.where(core == 0, theirs, mine)
    return jnp.stack([even, odd], axis=1)


def gather_features(part, axis):
    chips = lax.axis_size(axis) // 2
    core = lax.axis_index(axis) & 1
    mine = exchange(jnp.broadcast_to(part[None], (chips,) + part.shape), axis)
    theirs = partner_2(mine, axis, 0)
    both = by_core(mine, theirs, core).reshape((2 * chips,) + part.shape)
    return jnp.moveaxis(both, 0, 1).reshape(part.shape[0], -1)


def sum_features(partial, axis):
    count = lax.axis_size(axis)
    core = lax.axis_index(axis) & 1
    rows = partial.shape[0]
    split = partial.reshape(rows, count // 2, 2, -1)
    even = split[:, :, 0]
    odd = split[:, :, 1]
    mine = jnp.where(core == 0, even, odd)
    theirs = jnp.where(core == 0, odd, even).astype(jnp.bfloat16)
    pair = (mine + partner_2(theirs, axis, 0).astype(jnp.float32)).astype(jnp.bfloat16)
    got = exchange(jnp.moveaxis(pair, 1, 0), axis)
    return jnp.sum(got.astype(jnp.float32), axis=0)


def from_owner(mine, owner, axis):
    core = lax.axis_index(axis) & 1
    held = jnp.where(lax.axis_index(axis) == owner, mine, jnp.zeros_like(mine))
    held = held + partner_2(held, axis, 0)
    chips = lax.axis_size(axis) // 2
    got = exchange(jnp.broadcast_to(held[None], (chips,) + held.shape), axis)
    return lax.dynamic_index_in_dim(got, owner >> 1, 0, keepdims=False)


def partner_2(block, axis, distance):
    count = lax.axis_size(axis)
    route = []
    for low in range(count):
        high = low | 1 << distance
        if high != low and high < count:
            route += [(low, high), (high, low)]
    return lax.ppermute(block, axis, route)


def rms_scale(rows, gain):
    wide = rows.astype(jnp.float32)
    mean_sq = jnp.mean(wide * wide, axis=-1, keepdims=True)
    return (wide * lax.rsqrt(mean_sq + EPS) * gain.astype(jnp.float32)).astype(jnp.bfloat16)


def ancestry(parents):
    tree_width = parents.shape[-1]
    places = jnp.arange(tree_width, dtype=jnp.int32)
    links = (parents[:, :, None] == places[None, None, :]).astype(jnp.float32)
    reach = jnp.maximum(links, jnp.eye(tree_width, dtype=jnp.float32)[None])
    for step in range(int(tree_width).bit_length()):
        reach = jnp.minimum(
            jnp.einsum("rij,rjk->rik", reach, reach, precision=lax.Precision.HIGHEST), 1.0
        )
    tree_depth = jnp.sum(reach, axis=-1) - 1.0
    return (reach, tree_depth)


def apply_rotary(heads, tree_depth):
    half = heads.shape[-1] // 2
    freq = ROPE_BASE ** (-jnp.arange(half, dtype=jnp.float32) * 2.0 / heads.shape[-1])
    angle = tree_depth[:, :, None] * freq[None, None, :]
    cosine = jnp.cos(angle)[:, :, None, :]
    sine = jnp.sin(angle)[:, :, None, :]
    wide = heads.astype(jnp.float32)
    first = wide[..., :half]
    second = wide[..., half:]
    return jnp.concatenate(
        [first * cosine - second * sine, second * cosine + first * sine], axis=-1
    ).astype(jnp.bfloat16)


def join_pair(mine, theirs, flag):
    lower = jnp.concatenate([mine, theirs], axis=1)
    upper = jnp.concatenate([theirs, mine], axis=1)
    return jnp.where(flag == 1, upper, lower)


def general_body(
    tokens,
    attention_gain,
    forward_gain,
    query_weight,
    key_matrix,
    value_matrix,
    output_weight,
    gate_weight,
    up_weight,
    down_weight,
    adapter_inputs,
    adapter_query,
    adapter_upper,
    adapter_place,
    request_adapter,
    tree_parents,
):
    device = lax.axis_index("tp")
    rows = tokens.shape[0]
    request_list = request_adapter.shape[0]
    tree_width = rows // request_list
    rank = adapter_query.shape[1]
    pool_local = adapter_inputs.shape[0]
    head = HEAD_SIZE
    full_tokens = gather_features(tokens, "tp")
    normed = rms_scale(full_tokens, attention_gain)
    slots = adapter_place[request_adapter]
    owner = slots[0] // pool_local
    factors = lax.dynamic_index_in_dim(adapter_inputs, slots[0] % pool_local, 0, keepdims=False)
    low_held = jnp.dot(normed, factors[:, :rank], preferred_element_type=jnp.float32).astype(
        jnp.bfloat16
    )
    low_query = from_owner(low_held, owner, "tp")[None]
    lift = jnp.einsum(
        "rtk,rkc->rtc",
        low_query,
        adapter_query[request_adapter],
        preferred_element_type=jnp.float32,
    )
    query_local = (
        jnp.dot(normed, query_weight, preferred_element_type=jnp.float32) + lift.reshape(rows, -1)
    ).astype(jnp.bfloat16)
    key_local = jnp.dot(normed, key_matrix, preferred_element_type=jnp.float32).astype(jnp.bfloat16)
    value_local = jnp.dot(normed, value_matrix, preferred_element_type=jnp.float32).astype(
        jnp.bfloat16
    )
    query_cols = query_weight.shape[1]
    query_steps = max(0, (head // query_cols).bit_length() - 1)
    key_steps = (head // key_matrix.shape[1]).bit_length() - 1
    for bit in range(key_steps):
        flag = device >> bit & 1
        key_width = key_local.shape[1]
        with_query = bit < query_steps
        if with_query:
            query_width = query_local.shape[1]
            packed = jnp.concatenate([query_local, key_local, value_local], axis=1)
        else:
            query_width = 0
            packed = jnp.concatenate([key_local, value_local], axis=1)
        partner = partner_2(packed, "tp", bit)
        if with_query:
            query_local = join_pair(query_local, partner[:, :query_width], flag)
        key_other = partner[:, query_width : query_width + key_width]
        value_other = partner[:, query_width + key_width :]
        key_local = join_pair(key_local, key_other, flag)
        value_local = join_pair(value_local, value_other, flag)
    reach, tree_depth = ancestry(tree_parents)
    local_heads = query_local.shape[1] // head
    query_rotated = apply_rotary(
        query_local.reshape(request_list, tree_width, local_heads, head), tree_depth
    )
    key_rotated = apply_rotary(key_local.reshape(request_list, tree_width, 1, head), tree_depth)[
        :, :, 0, :
    ]
    heads_value = value_local.reshape(request_list, tree_width, head)
    scores = jnp.einsum(
        "rqhd,rkd->rhqk", query_rotated, key_rotated, preferred_element_type=jnp.float32
    ) * head ** (-0.5)
    weights = jnp.exp(scores) * reach[:, None, :, :]
    probs = (weights / jnp.sum(weights, axis=-1, keepdims=True)).astype(jnp.bfloat16)
    mixed = jnp.einsum(
        "rhqk,rkd->rqhd", probs, heads_value, preferred_element_type=jnp.float32
    ).astype(jnp.bfloat16)
    mixed = mixed.reshape(rows, local_heads * head)
    offset = (device & (1 << query_steps) - 1) * query_cols
    own_mixed = lax.dynamic_slice_in_dim(mixed, offset, query_cols, 1)
    partial_out = jnp.dot(own_mixed, output_weight, preferred_element_type=jnp.float32)
    summed = sum_features(partial_out, "tp")
    hidden = (tokens.astype(jnp.float32) + summed).astype(jnp.bfloat16)
    hidden_full = gather_features(hidden, "tp")
    normed_two = rms_scale(hidden_full, forward_gain)
    low_held_two = jnp.dot(normed_two, factors[:, rank:], preferred_element_type=jnp.float32).astype(
        jnp.bfloat16
    )
    low_up = from_owner(low_held_two, owner, "tp")[None]
    lift_up = jnp.einsum(
        "rtk,rkc->rtc", low_up, adapter_upper[request_adapter], preferred_element_type=jnp.float32
    )
    gate = jnp.dot(normed_two, gate_weight, preferred_element_type=jnp.float32)
    upper = jnp.dot(normed_two, up_weight, preferred_element_type=jnp.float32) + lift_up.reshape(
        rows, -1
    )
    active = (jax.nn.silu(gate) * upper).astype(jnp.bfloat16)
    forward = jnp.dot(active, down_weight, preferred_element_type=jnp.float32)
    forward_part = sum_features(forward, "tp")
    return (hidden.astype(jnp.float32) + forward_part).astype(jnp.bfloat16)


VMEM = pltpu.VMEM
WHOLE = pl.BlockSpec(memory_space=pltpu.VMEM)
SCALAR = pl.BlockSpec(memory_space=pltpu.SMEM)
FAR = pl.BlockSpec(memory_space=pltpu.HBM)
ROW_DOT = (((1,), (1,)), ((), ()))
LANES = 128
CHUNK = 1024


def dot(a, b):
    return jnp.dot(a, b, preferred_element_type=jnp.float32)


def dot_rows(a, b):
    return lax.dot_general(a, b, ROW_DOT, preferred_element_type=jnp.float32)


def call(kernel, name, outs, args, weights=(), ahead=(), scratch=(), limit=6, far=()):
    outs = tuple(VMEM(o.shape, o.dtype) for o in outs)
    size = sum(w.size for w in weights + far)
    used = len(args) + len(weights) + len(far)

    def run(*refs):
        kernel(*refs[:used], *refs[used + len(ahead) :])

    return pl.pallas_call(
        run,
        out_shape=outs,
        in_specs=[WHOLE] * (len(args) + len(weights)) + [FAR] * len(far + ahead),
        out_specs=(WHOLE,) * len(outs),
        scratch_shapes=list(scratch),
        name=name,
        cost_estimate=pl.CostEstimate(
            flops=64 * size, bytes_accessed=2 * size, transcendentals=0
        ),
        compiler_params=pltpu.CompilerParams(vmem_limit_bytes=limit << 20),
    )(
        *[pltpu.with_memory_space_constraint(w, VMEM) for w in args + weights],
        *[pltpu.with_memory_space_constraint(w, pltpu.HBM) for w in far + ahead],
    )


def near(x):
    return pltpu.with_memory_space_constraint(x, VMEM)


def distant(x):
    return pltpu.with_memory_space_constraint(x, pltpu.HBM)


def spread(tokens, kept, ahead, chips):
    outs = (VMEM((chips,) + tokens.shape, tokens.dtype),)
    outs += tuple(VMEM(a.shape, a.dtype) for a in (tokens, *kept))
    used = 1 + len(kept)

    def kernel(*refs):
        ins, outs, sem = refs[:used], refs[used + len(ahead) : -1], refs[-1]
        pairs = [(ins[0], outs[0].at[chip]) for chip in range(chips)]
        pairs += [(ins[k], outs[1 + k]) for k in range(used)]
        copies = [
            pltpu.make_async_copy(src, dst, sem.at[k]) for k, (src, dst) in enumerate(pairs)
        ]
        for copy in copies:
            copy.start()
        for copy in copies:
            copy.wait()

    return pl.pallas_call(
        kernel,
        out_shape=outs,
        in_specs=[FAR] * (used + len(ahead)),
        out_specs=(WHOLE,) * len(outs),
        scratch_shapes=[pltpu.SemaphoreType.DMA((chips + used,))],
        name="spread",
        compiler_params=pltpu.CompilerParams(vmem_limit_bytes=2 << 20),
    )(*[distant(a) for a in (tokens, *kept, *ahead)])


def table_kernel(
    request_ref, place_ref, query_ref, up_ref, parent_ref, after_ref,
    query_out, up_out, owner_out, cosine_out, sine_out, reach_out, place, sem,
):
    request = request_ref[0]
    copies = [
        pltpu.make_async_copy(place_ref, place, sem.at[0]),
        pltpu.make_async_copy(query_ref.at[request], query_out, sem.at[1]),
        pltpu.make_async_copy(up_ref.at[request], up_out, sem.at[2]),
    ]
    for copy in copies:
        copy.start()
    rows, head = cosine_out.shape
    half = head // 2
    own = lax.broadcasted_iota(jnp.int32, (rows, rows), 0)
    other = lax.broadcasted_iota(jnp.int32, (rows, rows), 1)
    eye = jnp.where(own == other, 1.0, 0.0)
    links = jnp.where(parent_ref[...] == own, 1.0, 0.0)
    reach = dot_rows(eye.astype(jnp.bfloat16), jnp.maximum(links, eye).astype(jnp.bfloat16))
    for _ in range((rows - 1).bit_length()):
        square = reach.astype(jnp.bfloat16)
        reach = jnp.minimum(dot(square, square), 1.0)
    reach_out[...] = reach
    lane = lax.broadcasted_iota(jnp.int32, (rows, head), 1)
    place_in_half = jnp.where(lane < half, lane, lane - half).astype(jnp.float32)
    freq = jnp.exp(place_in_half * np.float32(-2.0 / head * np.log(ROPE_BASE)))
    angle = (jnp.sum(reach, axis=-1, keepdims=True) - 1.0) * freq
    sine = jnp.sin(angle)
    cosine_out[...] = jnp.cos(angle)
    sine_out[...] = jnp.where(lane < half, -sine, sine)
    for copy in copies:
        copy.wait()
    owner_out[...] = jnp.full(owner_out.shape, place[request], jnp.int32)


def tables(request, place, lifts, parents, after):
    rows = parents.shape[1]
    shapes = [(a.shape[1:], a.dtype) for a in lifts]
    shapes += [((8, LANES), jnp.int32)]
    shapes += [((rows, HEAD_SIZE), jnp.float32)] * 2 + [((rows, rows), jnp.float32)]
    return pl.pallas_call(
        table_kernel,
        out_shape=tuple(VMEM(*a) for a in shapes),
        in_specs=[SCALAR] + [FAR] * 3 + [WHOLE] * 2,
        out_specs=(WHOLE,) * len(shapes),
        scratch_shapes=[
            pltpu.SMEM(place.shape, jnp.int32),
            pltpu.SemaphoreType.DMA((3,)),
        ],
        name="tables",
        compiler_params=pltpu.CompilerParams(vmem_limit_bytes=2 << 20),
    )(request, *[distant(a) for a in (place, *lifts)], near(parents), near(after))


def dot_chunks(left, weight_ref):
    depth = weight_ref.shape[0]
    step = min(depth, CHUNK)
    total = dot(left[:, :step], weight_ref[:step, :])
    for at in range(step, depth, step):
        total = total + dot(left[:, at : at + step], weight_ref[at : at + step, :])
    return total


def gain_block(gain_ref, index, cols):
    count = cols // LANES
    lines = [gain_ref[index * count + j : index * count + j + 1, :] for j in range(count)]
    return jnp.concatenate([line.astype(jnp.float32) for line in lines], axis=1)


def core_index():
    return lax.axis_index("tp") & 1


def in_order(mine, theirs, flag):
    mine = mine.astype(jnp.float32)
    theirs = theirs.astype(jnp.float32)
    return jnp.where(flag, mine, theirs), jnp.where(flag, theirs, mine)


def fold(low):
    rows, rank = low.shape
    padded = jnp.concatenate([low, jnp.zeros((rows, LANES - rank), jnp.float32)], axis=1)
    return (padded[:rank] + pltpu.roll(padded[rank:], LANES // 2, 1)).astype(jnp.bfloat16)


def unfold(folded):
    rank = folded.shape[0]
    low = jnp.concatenate([folded, pltpu.roll(folded, LANES // 2, 1)], axis=0)
    return low[:, :rank]


def features(ref, chip, rows, cols):
    if ref.shape[2] == cols:
        return ref[chip].astype(jnp.float32)
    lanes = ref.shape[2]
    blocks = [ref[chip, j * rows : (j + 1) * rows, :] for j in range(cols // lanes)]
    return jnp.concatenate(blocks, axis=1).astype(jnp.float32)


def norm_blocks(mine_ref, theirs_ref, gain_ref, scratch, cols):
    chips = mine_ref.shape[0]
    first = core_index() == 0
    rows = scratch.shape[0]
    squares = jnp.zeros((rows, cols), jnp.float32)
    for chip in range(chips):
        for ref in (mine_ref, theirs_ref):
            wide = features(ref, chip, rows, cols)
            squares = squares + wide * wide
    mean_sq = jnp.sum(squares, axis=-1, keepdims=True) / (2 * chips * cols)
    scale = lax.rsqrt(mean_sq + EPS)
    for chip in range(chips):
        mine = features(mine_ref, chip, rows, cols)
        pair = in_order(mine, features(theirs_ref, chip, rows, cols), first)
        for side in range(2):
            low = (2 * chip + side) * cols
            gain = gain_block(gain_ref, 2 * chip + side, cols)
            scratch[:, low : low + cols] = (pair[side] * scale * gain).astype(jnp.bfloat16)
    return scale


def project_kernel(
    mine_ref, theirs_ref, gain_ref, owner_ref, other_ref, key_ref, value_ref, factor_ref,
    normed_out, pair_out, payload_out,
):
    chips, rows, cols = mine_ref.shape
    core = core_index()
    norm_blocks(mine_ref, theirs_ref, gain_ref, normed_out, cols)
    normed = normed_out[...]
    rank = factor_ref.shape[0] // 2
    here = (owner_ref[:1, :1] & 1) == core
    low = jnp.where(
        here, dot_rows(normed, factor_ref[:rank, :]), dot_rows(normed, other_ref[:rank, :])
    )
    half = key_ref.shape[0]
    pair_out[:, :half] = dot_rows(normed, key_ref[...]).astype(jnp.bfloat16)
    pair_out[:, half:] = dot_rows(normed, value_ref[...]).astype(jnp.bfloat16)
    folded = fold(low)
    for chip in range(chips):
        at = pl.multiple_of((2 * chip + core) * cols, cols)
        own = factor_ref[rank:, pl.ds(at, cols)].astype(jnp.float32)
        other = other_ref[rank:, pl.ds(at, cols)].astype(jnp.float32)
        payload_out[chip, :, :cols] = jnp.where(here, own, other).astype(jnp.bfloat16)
        payload_out[chip, :, cols:] = folded


def query_kernel(normed_ref, query_ref, query_out):
    query_out[...] = dot_chunks(normed_ref[...], query_ref)


def side_product(left, weight_ref, side, out):
    chips, _, cols = out.shape
    for chip in range(chips):
        at = pl.multiple_of((2 * chip + side) * cols, cols)
        out[chip] = dot(left, weight_ref[:, pl.ds(at, cols)]).astype(out.dtype)


def attend_kernel(
    query_ref, pair_mine, pair_theirs, owner_ref, got_ref, lift_ref, cosine_ref, sine_ref,
    reach_ref, output_ref, mixed_out, theirs_out, piece_out,
):
    rows, query_cols = query_ref.shape
    chips, _, cols = theirs_out.shape
    head = HEAD_SIZE
    heads = query_cols // head
    half = head // 2
    owner = owner_ref[:1, :1]
    piece = jnp.zeros(got_ref.shape[1:], jnp.float32)
    for chip in range(chips):
        sent = got_ref[chip].astype(jnp.float32)
        piece = piece + jnp.where((owner >> 1) == chip, sent, 0.0)
    piece_out[...] = piece.astype(jnp.bfloat16)
    low = unfold(piece[:, cols:])
    lane = lax.broadcasted_iota(jnp.int32, (rows, head), 1)
    cosine = cosine_ref[...]
    sine = sine_ref[...]

    def rotate(wide):
        return (wide * cosine + pltpu.roll(wide, half, 1) * sine).astype(jnp.bfloat16)

    first = core_index() == 0
    even, odd = in_order(pair_mine[...], pair_theirs[...], first)
    key = rotate(jnp.where(lane < half, even, pltpu.roll(odd, half, 1)))
    value = jnp.where(lane < half, pltpu.roll(even, half, 1), odd).astype(jnp.bfloat16)
    query = query_ref[...] + dot(low.astype(jnp.bfloat16), lift_ref[...])
    query = query.astype(jnp.bfloat16).astype(jnp.float32)
    stacked = jnp.concatenate(
        [rotate(query[:, h * head : (h + 1) * head]) for h in range(heads)], axis=0
    )
    scores = dot_rows(stacked, key) * head ** (-0.5)
    weights = jnp.exp(scores) * jnp.concatenate([reach_ref[...]] * heads, axis=0)
    probs = (weights / jnp.sum(weights, axis=-1, keepdims=True)).astype(jnp.bfloat16)
    mixed = dot(probs, value).astype(jnp.bfloat16)
    mixed = jnp.concatenate([mixed[h * rows : (h + 1) * rows] for h in range(heads)], axis=1)
    mixed_out[...] = mixed
    side_product(mixed, output_ref, 1 - core_index(), theirs_out)


def rest_kernel(mixed_ref, output_ref, mine_out):
    side_product(mixed_ref[...], output_ref, core_index(), mine_out)


def hidden_kernel(
    got_ref, token_ref, gain_ref, piece_ref,
    hidden_out, payload_out,
):
    chips, rows, cols = got_ref.shape
    total = token_ref[...].astype(jnp.float32)
    added = got_ref[0].astype(jnp.float32)
    for chip in range(1, chips):
        added = added + got_ref[chip].astype(jnp.float32)
    hidden = (total + added).astype(jnp.bfloat16)
    hidden_out[...] = hidden
    factor = piece_ref[:, :cols]
    rank = factor.shape[0]
    device = lax.axis_index("tp")
    gain = gain_block(gain_ref, 0, cols)
    for index in range(1, 2 * chips):
        gain = jnp.where(device == index, gain_block(gain_ref, index, cols), gain)
    gained = hidden.astype(jnp.float32) * gain
    low = dot_rows(gained.astype(jnp.bfloat16), factor)
    folded = fold(low)
    for chip in range(chips):
        for j in range(cols // LANES):
            part = hidden[:, j * LANES : (j + 1) * LANES]
            payload_out[chip, j * rows : (j + 1) * rows, :] = part
        payload_out[chip, -rank:, :] = folded


def down_copies(down_ref, held, sem, side, start=0):
    cols = held.shape[2]

    def copy(k):
        part = pl.ds(pl.multiple_of((2 * (k + start) + side) * cols, LANES), cols)
        return pltpu.make_async_copy(down_ref.at[:, part], held.at[k], sem.at[k])

    return copy


def half_products(block_ref, gain_ref, gate_ref, up_ref, side, rows, cols):
    gate = up = None
    for chip in range(block_ref.shape[0]):
        gain = jnp.where(
            side == 0, gain_block(gain_ref, 2 * chip, cols), gain_block(gain_ref, 2 * chip + 1, cols)
        )
        left = (features(block_ref, chip, rows, cols) * gain).astype(jnp.bfloat16)
        part = pl.ds(pl.multiple_of((2 * chip + side) * cols, cols), cols)
        gate_part = dot(left, gate_ref[part, :])
        up_part = dot(left, up_ref[part, :])
        gate = gate_part if gate is None else gate + gate_part
        up = up_part if up is None else up + up_part
    return gate, up


def near_kernel(
    mine_ref, gain_ref, gate_ref, up_ref, down_ref, gate_out, up_out, held_out, sem
):
    core = core_index()
    count, _, cols = held_out.shape
    copy = down_copies(down_ref, held_out, sem, 1 - core)

    @pl.loop(0, count)
    def _(k):
        copy(k).start()

    gate, up = half_products(
        mine_ref, gain_ref, gate_ref, up_ref, core, gate_out.shape[0], cols
    )
    gate_out[...] = gate
    up_out[...] = up

    @pl.loop(0, count)
    def _(k):
        copy(k).wait()


def forward_kernel(
    mine_ref, theirs_ref, gain_ref, lift_ref, gate_part, up_part, early_ref, gate_ref, up_ref,
    down_ref, active_out, theirs_out, held_out, held, sem, sem_out,
):
    chips, rows, cols = theirs_out.shape
    core = core_index()
    rank = lift_ref.shape[0]
    early = early_ref.shape[0]
    first = down_copies(down_ref, held, sem, 1 - core, early)
    second = down_copies(down_ref, held_out, sem_out, core)

    @pl.loop(0, chips - early)
    def _(k):
        first(k).start()

    @pl.loop(0, chips)
    def _(k):
        second(k).start()

    gate, up = half_products(theirs_ref, gain_ref, gate_ref, up_ref, 1 - core, rows, cols)
    squares = jnp.zeros((rows, cols), jnp.float32)
    folded = jnp.zeros((rank, LANES), jnp.float32)
    for chip in range(chips):
        for ref in (mine_ref, theirs_ref):
            wide = features(ref, chip, rows, cols)
            squares = squares + wide * wide
            folded = folded + ref[chip, -rank:, :].astype(jnp.float32)
    mean_sq = jnp.sum(squares, axis=-1, keepdims=True) / (2 * chips * cols)
    scale = lax.rsqrt(mean_sq + EPS)
    low = (unfold(folded) * scale).astype(jnp.bfloat16)
    gate = (gate + gate_part[...]) * scale
    upper = (up + up_part[...]) * scale + dot(low, lift_ref[...])
    active_out[...] = (gate * jax.nn.sigmoid(gate) * upper).astype(jnp.bfloat16)

    for k in range(early):
        theirs_out[k] = dot(active_out[...], early_ref[k]).astype(theirs_out.dtype)

    @pl.loop(0, chips - early)
    def _(k):
        first(k).wait()

    for k in range(chips - early):
        theirs_out[k + early] = dot(active_out[...], held[k]).astype(theirs_out.dtype)

    @pl.loop(0, chips)
    def _(k):
        second(k).wait()


def last_kernel(active_ref, held_ref, mine_out):
    for chip in range(mine_out.shape[0]):
        mine_out[chip] = dot(active_ref[...], held_ref[chip])


def fast_body(
    tokens,
    attention_gain,
    forward_gain,
    query_weight,
    key_matrix,
    value_matrix,
    output_weight,
    gate_weight,
    up_weight,
    down_weight,
    adapter_inputs,
    adapter_query,
    adapter_upper,
    adapter_place,
    request_adapter,
    tree_parents,
):
    rows, cols = tokens.shape
    chips = lax.axis_size("tp") // 2
    width = query_weight.shape[0]
    shape = jax.ShapeDtypeStruct
    bf16, f32 = jnp.bfloat16, jnp.float32
    tall = rows * cols // LANES + adapter_query.shape[1]
    heavy = (gate_weight, up_weight, down_weight)
    most = heavy + (query_weight, output_weight)
    rank = adapter_query.shape[1]
    factors = adapter_inputs[0].T

    spread_tokens, kept_tokens, gain_one, gain_two, parents = spread(
        tokens,
        (attention_gain.reshape(-1, LANES), forward_gain.reshape(-1, LANES), tree_parents),
        heavy,
        chips,
    )
    mine = exchange(spread_tokens, "tp")
    mine, held = lax.optimization_barrier((mine, adapter_inputs))
    theirs = partner_2(mine, "tp", 0)
    factors_theirs = partner_2(held, "tp", 0)[0].T
    query_lift, up_lift, owner, cosine, sine, reach = tables(
        request_adapter, adapter_place, (adapter_query, adapter_upper), parents, mine
    )
    normed, pair, payload = call(
        project_kernel,
        "project",
        (
            shape((rows, width), bf16),
            shape((rows, 2 * key_matrix.shape[1]), bf16),
            shape((chips, rank, cols + LANES), bf16),
        ),
        (mine, theirs, gain_one, owner, factors_theirs),
        (key_matrix.T, value_matrix.T, factors),
    )
    pair_theirs = partner_2(pair, "tp", 0)
    (query,) = call(
        query_kernel,
        "query",
        (shape((rows, query_weight.shape[1]), f32),),
        (normed,),
        (query_weight,),
        heavy,
    )
    pair_theirs, query, payload = lax.optimization_barrier((pair_theirs, query, payload))
    mixed, sent, piece = call(
        attend_kernel,
        "attend",
        (
            shape((rows, query_weight.shape[1]), bf16),
            shape((chips, rows, cols), bf16),
            shape(payload.shape[1:], bf16),
        ),
        (
            query, pair, pair_theirs, owner, exchange(payload, "tp"), query_lift, cosine,
            sine, reach,
        ),
        (output_weight,),
        heavy + (query_weight,),
    )
    sent_theirs = partner_2(sent, "tp", 0)
    (kept,) = call(
        rest_kernel, "rest", (shape((chips, rows, cols), f32),), (mixed,), (output_weight,)
    )
    chip_sum = (kept + sent_theirs.astype(f32)).astype(bf16)
    hidden, payload = call(
        hidden_kernel,
        "hidden",
        (shape((rows, cols), bf16), shape((chips, tall, LANES), bf16)),
        (exchange(chip_sum, "tp"), kept_tokens, gain_two, piece),
        (),
        most,
    )
    mine = exchange(payload, "tp")
    theirs = partner_2(mine, "tp", 0)
    held = shape((chips, down_weight.shape[0], cols), bf16)
    half = chips // 2
    part = shape((rows, gate_weight.shape[1]), f32)
    gate_part, up_part, early = call(
        near_kernel,
        "near",
        (part, part, shape((half, *held.shape[1:]), bf16)),
        (mine, gain_two),
        (gate_weight, up_weight),
        (),
        [pltpu.SemaphoreType.DMA((half,))],
        far=(down_weight,),
        limit=8,
    )
    active, sent, held_mine = call(
        forward_kernel,
        "forward",
        (shape(part.shape, bf16), shape((chips, rows, cols), bf16), held),
        (mine, theirs, gain_two, up_lift, gate_part, up_part, early),
        (gate_weight, up_weight),
        (),
        [
            VMEM((chips - half, *held.shape[1:]), bf16),
            pltpu.SemaphoreType.DMA((chips - half,)),
            pltpu.SemaphoreType.DMA((chips,)),
        ],
        far=(down_weight,),
        limit=8,
    )
    sent_theirs = partner_2(sent, "tp", 0)
    (kept,) = call(
        last_kernel, "last", (shape((chips, rows, cols), f32),), (active, held_mine)
    )
    chip_sum = (kept + sent_theirs.astype(f32)).astype(bf16)
    added = jnp.sum(exchange(chip_sum, "tp").astype(f32), axis=0)
    return (hidden.astype(f32) + added).astype(bf16)


def body(*args):
    tokens, key_matrix, query_weight = args[0], args[4], args[3]
    fits = (
        tokens.shape[1] % LANES == 0
        and query_weight.shape[1] % HEAD_SIZE == 0
        and key_matrix.shape[1] * 2 == HEAD_SIZE
        and args[10].shape[0] == 1
        and args[14].shape[0] == 1
        and args[10].shape[2] == tokens.shape[0]
    )
    return fast_body(*args) if fits else general_body(*args)


def solution(mesh):
    return jax.shard_map(
        body,
        mesh=mesh,
        in_specs=(
            P("rep", "tp"),
            P(),
            P(),
            P(None, "tp"),
            P(None, "tp"),
            P(None, "tp"),
            P("tp", None),
            P(None, "tp"),
            P(None, "tp"),
            P("tp", None),
            P(("rep", "tp"), None, None),
            P("rep", None, "tp"),
            P("rep", None, "tp"),
            P("rep"),
            P("rep"),
            P("rep", None),
        ),
        out_specs=P("rep", "tp"),
        check_vma=False,
    )
```

```python
import jax
import jax.numpy as jnp
import numpy as np
from jax import lax
from jax.experimental import pallas as pl
from jax.experimental.pallas import tpu as pltpu
from jax.sharding import PartitionSpec as P

HEAD_SIZE = 128


EPS = 1e-05
ROPE_BASE = 500000.0


def core_groups(axis):
    count = lax.axis_size(axis)
    return [list(range(core, count, 2)) for core in range(2)]


def exchange(blocks, axis):
    return lax.all_to_all(
        blocks, axis, 0, 0, axis_index_groups=core_groups(axis), tiled=True
    )


def by_core(mine, theirs, core):
    even = jnp.where(core == 0, mine, theirs)
    odd = jnp.where(core == 0, theirs, mine)
    return jnp.stack([even, odd], axis=1)


def gather_features(part, axis):
    chips = lax.axis_size(axis) // 2
    core = lax.axis_index(axis) & 1
    mine = exchange(jnp.broadcast_to(part[None], (chips,) + part.shape), axis)
    theirs = partner_2(mine, axis, 0)
    both = by_core(mine, theirs, core).reshape((2 * chips,) + part.shape)
    return jnp.moveaxis(both, 0, 1).reshape(part.shape[0], -1)


def sum_features(partial, axis):
    count = lax.axis_size(axis)
    core = lax.axis_index(axis) & 1
    rows = partial.shape[0]
    split = partial.reshape(rows, count // 2, 2, -1)
    even = split[:, :, 0]
    odd = split[:, :, 1]
    mine = jnp.where(core == 0, even, odd)
    theirs = jnp.where(core == 0, odd, even).astype(jnp.bfloat16)
    pair = (mine + partner_2(theirs, axis, 0).astype(jnp.float32)).astype(jnp.bfloat16)
    got = exchange(jnp.moveaxis(pair, 1, 0), axis)
    return jnp.sum(got.astype(jnp.float32), axis=0)


def from_owner(mine, owner, axis):
    core = lax.axis_index(axis) & 1
    held = jnp.where(lax.axis_index(axis) == owner, mine, jnp.zeros_like(mine))
    held = held + partner_2(held, axis, 0)
    chips = lax.axis_size(axis) // 2
    got = exchange(jnp.broadcast_to(held[None], (chips,) + held.shape), axis)
    return lax.dynamic_index_in_dim(got, owner >> 1, 0, keepdims=False)


def partner_2(block, axis, distance):
    count = lax.axis_size(axis)
    route = []
    for low in range(count):
        high = low | 1 << distance
        if high != low and high < count:
            route += [(low, high), (high, low)]
    return lax.ppermute(block, axis, route)


def rms_scale(rows, gain):
    wide = rows.astype(jnp.float32)
    mean_sq = jnp.mean(wide * wide, axis=-1, keepdims=True)
    return (wide * lax.rsqrt(mean_sq + EPS) * gain.astype(jnp.float32)).astype(jnp.bfloat16)


def ancestry(parents):
    tree_width = parents.shape[-1]
    places = jnp.arange(tree_width, dtype=jnp.int32)
    links = (parents[:, :, None] == places[None, None, :]).astype(jnp.float32)
    reach = jnp.maximum(links, jnp.eye(tree_width, dtype=jnp.float32)[None])
    for step in range(int(tree_width).bit_length()):
        reach = jnp.minimum(
            jnp.einsum("rij,rjk->rik", reach, reach, precision=lax.Precision.HIGHEST), 1.0
        )
    tree_depth = jnp.sum(reach, axis=-1) - 1.0
    return (reach, tree_depth)


def apply_rotary(heads, tree_depth):
    half = heads.shape[-1] // 2
    freq = ROPE_BASE ** (-jnp.arange(half, dtype=jnp.float32) * 2.0 / heads.shape[-1])
    angle = tree_depth[:, :, None] * freq[None, None, :]
    cosine = jnp.cos(angle)[:, :, None, :]
    sine = jnp.sin(angle)[:, :, None, :]
    wide = heads.astype(jnp.float32)
    first = wide[..., :half]
    second = wide[..., half:]
    return jnp.concatenate(
        [first * cosine - second * sine, second * cosine + first * sine], axis=-1
    ).astype(jnp.bfloat16)


def join_pair(mine, theirs, flag):
    lower = jnp.concatenate([mine, theirs], axis=1)
    upper = jnp.concatenate([theirs, mine], axis=1)
    return jnp.where(flag == 1, upper, lower)


def general_body(
    tokens,
    attention_gain,
    forward_gain,
    query_weight,
    key_matrix,
    value_matrix,
    output_weight,
    gate_weight,
    up_weight,
    down_weight,
    adapter_inputs,
    adapter_query,
    adapter_upper,
    adapter_place,
    request_adapter,
    tree_parents,
):
    device = lax.axis_index("tp")
    rows = tokens.shape[0]
    request_list = request_adapter.shape[0]
    tree_width = rows // request_list
    rank = adapter_query.shape[1]
    pool_local = adapter_inputs.shape[0]
    head = HEAD_SIZE
    full_tokens = gather_features(tokens, "tp")
    normed = rms_scale(full_tokens, attention_gain)
    slots = adapter_place[request_adapter]
    owner = slots[0] // pool_local
    factors = lax.dynamic_index_in_dim(adapter_inputs, slots[0] % pool_local, 0, keepdims=False)
    low_held = jnp.dot(normed, factors[:, :rank], preferred_element_type=jnp.float32).astype(
        jnp.bfloat16
    )
    low_query = from_owner(low_held, owner, "tp")[None]
    lift = jnp.einsum(
        "rtk,rkc->rtc",
        low_query,
        adapter_query[request_adapter],
        preferred_element_type=jnp.float32,
    )
    query_local = (
        jnp.dot(normed, query_weight, preferred_element_type=jnp.float32) + lift.reshape(rows, -1)
    ).astype(jnp.bfloat16)
    key_local = jnp.dot(normed, key_matrix, preferred_element_type=jnp.float32).astype(jnp.bfloat16)
    value_local = jnp.dot(normed, value_matrix, preferred_element_type=jnp.float32).astype(
        jnp.bfloat16
    )
    query_cols = query_weight.shape[1]
    query_steps = max(0, (head // query_cols).bit_length() - 1)
    key_steps = (head // key_matrix.shape[1]).bit_length() - 1
    for bit in range(key_steps):
        flag = device >> bit & 1
        key_width = key_local.shape[1]
        with_query = bit < query_steps
        if with_query:
            query_width = query_local.shape[1]
            packed = jnp.concatenate([query_local, key_local, value_local], axis=1)
        else:
            query_width = 0
            packed = jnp.concatenate([key_local, value_local], axis=1)
        partner = partner_2(packed, "tp", bit)
        if with_query:
            query_local = join_pair(query_local, partner[:, :query_width], flag)
        key_other = partner[:, query_width : query_width + key_width]
        value_other = partner[:, query_width + key_width :]
        key_local = join_pair(key_local, key_other, flag)
        value_local = join_pair(value_local, value_other, flag)
    reach, tree_depth = ancestry(tree_parents)
    local_heads = query_local.shape[1] // head
    query_rotated = apply_rotary(
        query_local.reshape(request_list, tree_width, local_heads, head), tree_depth
    )
    key_rotated = apply_rotary(key_local.reshape(request_list, tree_width, 1, head), tree_depth)[
        :, :, 0, :
    ]
    heads_value = value_local.reshape(request_list, tree_width, head)
    scores = jnp.einsum(
        "rqhd,rkd->rhqk", query_rotated, key_rotated, preferred_element_type=jnp.float32
    ) * head ** (-0.5)
    weights = jnp.exp(scores) * reach[:, None, :, :]
    probs = (weights / jnp.sum(weights, axis=-1, keepdims=True)).astype(jnp.bfloat16)
    mixed = jnp.einsum(
        "rhqk,rkd->rqhd", probs, heads_value, preferred_element_type=jnp.float32
    ).astype(jnp.bfloat16)
    mixed = mixed.reshape(rows, local_heads * head)
    offset = (device & (1 << query_steps) - 1) * query_cols
    own_mixed = lax.dynamic_slice_in_dim(mixed, offset, query_cols, 1)
    partial_out = jnp.dot(own_mixed, output_weight, preferred_element_type=jnp.float32)
    summed = sum_features(partial_out, "tp")
    hidden = (tokens.astype(jnp.float32) + summed).astype(jnp.bfloat16)
    hidden_full = gather_features(hidden, "tp")
    normed_two = rms_scale(hidden_full, forward_gain)
    low_held_two = jnp.dot(normed_two, factors[:, rank:], preferred_element_type=jnp.float32).astype(
        jnp.bfloat16
    )
    low_up = from_owner(low_held_two, owner, "tp")[None]
    lift_up = jnp.einsum(
        "rtk,rkc->rtc", low_up, adapter_upper[request_adapter], preferred_element_type=jnp.float32
    )
    gate = jnp.dot(normed_two, gate_weight, preferred_element_type=jnp.float32)
    upper = jnp.dot(normed_two, up_weight, preferred_element_type=jnp.float32) + lift_up.reshape(
        rows, -1
    )
    active = (jax.nn.silu(gate) * upper).astype(jnp.bfloat16)
    forward = jnp.dot(active, down_weight, preferred_element_type=jnp.float32)
    forward_part = sum_features(forward, "tp")
    return (hidden.astype(jnp.float32) + forward_part).astype(jnp.bfloat16)


VMEM = pltpu.VMEM
WHOLE = pl.BlockSpec(memory_space=pltpu.VMEM)
SCALAR = pl.BlockSpec(memory_space=pltpu.SMEM)
FAR = pl.BlockSpec(memory_space=pltpu.HBM)
ROW_DOT = (((1,), (1,)), ((), ()))
LANES = 128
CHUNK = 1024


def dot(a, b):
    return jnp.dot(a, b, preferred_element_type=jnp.float32)


def dot_rows(a, b):
    return lax.dot_general(a, b, ROW_DOT, preferred_element_type=jnp.float32)


def call(kernel, name, outs, args, weights=(), ahead=(), scratch=(), limit=6, far=()):
    outs = tuple(VMEM(o.shape, o.dtype) for o in outs)
    size = sum(w.size for w in weights + far)
    used = len(args) + len(weights) + len(far)

    def run(*refs):
        kernel(*refs[:used], *refs[used + len(ahead) :])

    return pl.pallas_call(
        run,
        out_shape=outs,
        in_specs=[WHOLE] * (len(args) + len(weights)) + [FAR] * len(far + ahead),
        out_specs=(WHOLE,) * len(outs),
        scratch_shapes=list(scratch),
        name=name,
        cost_estimate=pl.CostEstimate(
            flops=64 * size, bytes_accessed=2 * size, transcendentals=0
        ),
        compiler_params=pltpu.CompilerParams(vmem_limit_bytes=limit << 20),
    )(
        *[pltpu.with_memory_space_constraint(w, VMEM) for w in args + weights],
        *[pltpu.with_memory_space_constraint(w, pltpu.HBM) for w in far + ahead],
    )


def near(x):
    return pltpu.with_memory_space_constraint(x, VMEM)


def distant(x):
    return pltpu.with_memory_space_constraint(x, pltpu.HBM)


def spread(tokens, kept, ahead, chips):
    outs = (VMEM((chips,) + tokens.shape, tokens.dtype),)
    outs += tuple(VMEM(a.shape, a.dtype) for a in (tokens, *kept))
    used = 1 + len(kept)

    def kernel(*refs):
        ins, outs, sem = refs[:used], refs[used + len(ahead) : -1], refs[-1]
        pairs = [(ins[0], outs[0].at[chip]) for chip in range(chips)]
        pairs += [(ins[k], outs[1 + k]) for k in range(used)]
        copies = [
            pltpu.make_async_copy(src, dst, sem.at[k]) for k, (src, dst) in enumerate(pairs)
        ]
        for copy in copies:
            copy.start()
        for copy in copies:
            copy.wait()

    return pl.pallas_call(
        kernel,
        out_shape=outs,
        in_specs=[FAR] * (used + len(ahead)),
        out_specs=(WHOLE,) * len(outs),
        scratch_shapes=[pltpu.SemaphoreType.DMA((chips + used,))],
        name="spread",
        compiler_params=pltpu.CompilerParams(vmem_limit_bytes=2 << 20),
    )(*[distant(a) for a in (tokens, *kept, *ahead)])


def table_kernel(
    request_ref, place_ref, query_ref, up_ref, parent_ref, after_ref,
    query_out, up_out, owner_out, cosine_out, sine_out, reach_out, place, sem,
):
    request = request_ref[0]
    copies = [
        pltpu.make_async_copy(place_ref, place, sem.at[0]),
        pltpu.make_async_copy(query_ref.at[request], query_out, sem.at[1]),
        pltpu.make_async_copy(up_ref.at[request], up_out, sem.at[2]),
    ]
    for copy in copies:
        copy.start()
    rows, head = cosine_out.shape
    half = head // 2
    own = lax.broadcasted_iota(jnp.int32, (rows, rows), 0)
    other = lax.broadcasted_iota(jnp.int32, (rows, rows), 1)
    eye = jnp.where(own == other, 1.0, 0.0)
    links = jnp.where(parent_ref[...] == own, 1.0, 0.0)
    reach = dot_rows(eye.astype(jnp.bfloat16), jnp.maximum(links, eye).astype(jnp.bfloat16))
    for _ in range((rows - 1).bit_length()):
        square = reach.astype(jnp.bfloat16)
        reach = jnp.minimum(dot(square, square), 1.0)
    reach_out[...] = reach
    lane = lax.broadcasted_iota(jnp.int32, (rows, head), 1)
    place_in_half = jnp.where(lane < half, lane, lane - half).astype(jnp.float32)
    freq = jnp.exp(place_in_half * np.float32(-2.0 / head * np.log(ROPE_BASE)))
    angle = (jnp.sum(reach, axis=-1, keepdims=True) - 1.0) * freq
    sine = jnp.sin(angle)
    cosine_out[...] = jnp.cos(angle)
    sine_out[...] = jnp.where(lane < half, -sine, sine)
    for copy in copies:
        copy.wait()
    owner_out[...] = jnp.full(owner_out.shape, place[request], jnp.int32)


def tables(request, place, lifts, parents, after):
    rows = parents.shape[1]
    shapes = [(a.shape[1:], a.dtype) for a in lifts]
    shapes += [((8, LANES), jnp.int32)]
    shapes += [((rows, HEAD_SIZE), jnp.float32)] * 2 + [((rows, rows), jnp.float32)]
    return pl.pallas_call(
        table_kernel,
        out_shape=tuple(VMEM(*a) for a in shapes),
        in_specs=[SCALAR] + [FAR] * 3 + [WHOLE] * 2,
        out_specs=(WHOLE,) * len(shapes),
        scratch_shapes=[
            pltpu.SMEM(place.shape, jnp.int32),
            pltpu.SemaphoreType.DMA((3,)),
        ],
        name="tables",
        compiler_params=pltpu.CompilerParams(vmem_limit_bytes=2 << 20),
    )(request, *[distant(a) for a in (place, *lifts)], near(parents), near(after))


def dot_chunks(left, weight_ref):
    depth = weight_ref.shape[0]
    step = min(depth, CHUNK)
    total = dot(left[:, :step], weight_ref[:step, :])
    for at in range(step, depth, step):
        total = total + dot(left[:, at : at + step], weight_ref[at : at + step, :])
    return total


def gain_block(gain_ref, index, cols):
    count = cols // LANES
    lines = [gain_ref[index * count + j : index * count + j + 1, :] for j in range(count)]
    return jnp.concatenate([line.astype(jnp.float32) for line in lines], axis=1)


def core_index():
    return lax.axis_index("tp") & 1


def in_order(mine, theirs, flag):
    mine = mine.astype(jnp.float32)
    theirs = theirs.astype(jnp.float32)
    return jnp.where(flag, mine, theirs), jnp.where(flag, theirs, mine)


def fold(low):
    rows, rank = low.shape
    padded = jnp.concatenate([low, jnp.zeros((rows, LANES - rank), jnp.float32)], axis=1)
    return (padded[:rank] + pltpu.roll(padded[rank:], LANES // 2, 1)).astype(jnp.bfloat16)


def unfold(folded):
    rank = folded.shape[0]
    low = jnp.concatenate([folded, pltpu.roll(folded, LANES // 2, 1)], axis=0)
    return low[:, :rank]


def features(ref, chip, rows, cols):
    if ref.shape[2] == cols:
        return ref[chip].astype(jnp.float32)
    lanes = ref.shape[2]
    blocks = [ref[chip, j * rows : (j + 1) * rows, :] for j in range(cols // lanes)]
    return jnp.concatenate(blocks, axis=1).astype(jnp.float32)


def norm_blocks(mine_ref, theirs_ref, gain_ref, scratch, cols):
    chips = mine_ref.shape[0]
    first = core_index() == 0
    rows = scratch.shape[0]
    squares = jnp.zeros((rows, cols), jnp.float32)
    for chip in range(chips):
        for ref in (mine_ref, theirs_ref):
            wide = features(ref, chip, rows, cols)
            squares = squares + wide * wide
    mean_sq = jnp.sum(squares, axis=-1, keepdims=True) / (2 * chips * cols)
    scale = lax.rsqrt(mean_sq + EPS)
    for chip in range(chips):
        mine = features(mine_ref, chip, rows, cols)
        pair = in_order(mine, features(theirs_ref, chip, rows, cols), first)
        for side in range(2):
            low = (2 * chip + side) * cols
            gain = gain_block(gain_ref, 2 * chip + side, cols)
            scratch[:, low : low + cols] = (pair[side] * scale * gain).astype(jnp.bfloat16)
    return scale


def project_kernel(
    mine_ref, theirs_ref, gain_ref, owner_ref, other_ref, key_ref, value_ref, factor_ref,
    normed_out, pair_out, payload_out,
):
    chips, rows, cols = mine_ref.shape
    core = core_index()
    norm_blocks(mine_ref, theirs_ref, gain_ref, normed_out, cols)
    normed = normed_out[...]
    rank = factor_ref.shape[0] // 2
    here = (owner_ref[:1, :1] & 1) == core
    low = jnp.where(
        here, dot_rows(normed, factor_ref[:rank, :]), dot_rows(normed, other_ref[:rank, :])
    )
    half = key_ref.shape[0]
    turned = [dot_rows(ref[...], normed) for ref in (key_ref, value_ref)]
    pair_out[...] = jnp.concatenate(turned, axis=0).T.astype(jnp.bfloat16)
    folded = fold(low)
    for chip in range(chips):
        at = pl.multiple_of((2 * chip + core) * cols, cols)
        own = factor_ref[rank:, pl.ds(at, cols)].astype(jnp.float32)
        other = other_ref[rank:, pl.ds(at, cols)].astype(jnp.float32)
        payload_out[chip, :, :cols] = jnp.where(here, own, other).astype(jnp.bfloat16)
        payload_out[chip, :, cols:] = folded


def query_kernel(normed_ref, query_ref, query_out):
    query_out[...] = dot_chunks(normed_ref[...], query_ref)


def side_product(left, weight_ref, side, out):
    chips, _, cols = out.shape
    for chip in range(chips):
        at = pl.multiple_of((2 * chip + side) * cols, cols)
        out[chip] = dot(left, weight_ref[:, pl.ds(at, cols)]).astype(out.dtype)


def owner_part(owner, got_ref, lanes):
    part = jnp.zeros((got_ref.shape[1], lanes.stop - lanes.start), jnp.float32)
    for chip in range(got_ref.shape[0]):
        sent = got_ref[chip, :, lanes].astype(jnp.float32)
        part = part + jnp.where((owner >> 1) == chip, sent, 0.0)
    return part


def attend_kernel(
    query_ref, pair_mine, pair_theirs, owner_ref, got_ref, lift_ref, cosine_ref, sine_ref,
    reach_ref, output_ref, mixed_out, theirs_out,
):
    rows, query_cols = query_ref.shape
    chips, _, cols = theirs_out.shape
    head = HEAD_SIZE
    heads = query_cols // head
    half = head // 2
    owner = owner_ref[:1, :1]
    low = unfold(owner_part(owner, got_ref, slice(cols, cols + LANES)))
    lane = lax.broadcasted_iota(jnp.int32, (rows, head), 1)
    cosine = cosine_ref[...]
    sine = sine_ref[...]

    def rotate(wide):
        return (wide * cosine + pltpu.roll(wide, half, 1) * sine).astype(jnp.bfloat16)

    first = core_index() == 0
    even, odd = in_order(pair_mine[...], pair_theirs[...], first)
    key = rotate(jnp.where(lane < half, even, pltpu.roll(odd, half, 1)))
    value = jnp.where(lane < half, pltpu.roll(even, half, 1), odd).astype(jnp.bfloat16)
    query = query_ref[...] + dot(low.astype(jnp.bfloat16), lift_ref[...])
    query = query.astype(jnp.bfloat16).astype(jnp.float32)
    stacked = jnp.concatenate(
        [rotate(query[:, h * head : (h + 1) * head]) for h in range(heads)], axis=0
    )
    scores = dot_rows(stacked, key) * head ** (-0.5)
    weights = jnp.exp(scores) * jnp.concatenate([reach_ref[...]] * heads, axis=0)
    probs = (weights / jnp.sum(weights, axis=-1, keepdims=True)).astype(jnp.bfloat16)
    mixed = dot(probs, value).astype(jnp.bfloat16)
    mixed = jnp.concatenate([mixed[h * rows : (h + 1) * rows] for h in range(heads)], axis=1)
    mixed_out[...] = mixed
    side_product(mixed, output_ref, 1 - core_index(), theirs_out)


def rest_kernel(mixed_ref, owner_ref, got_ref, output_ref, mine_out, piece_out):
    part = owner_part(owner_ref[:1, :1], got_ref, slice(0, piece_out.shape[1]))
    piece_out[...] = part.astype(jnp.bfloat16)
    side_product(mixed_ref[...], output_ref, core_index(), mine_out)


def hidden_kernel(
    got_ref, token_ref, gain_ref, piece_ref,
    hidden_out, payload_out,
):
    chips, rows, cols = got_ref.shape
    total = token_ref[...].astype(jnp.float32)
    added = got_ref[0].astype(jnp.float32)
    for chip in range(1, chips):
        added = added + got_ref[chip].astype(jnp.float32)
    hidden = (total + added).astype(jnp.bfloat16)
    hidden_out[...] = hidden
    factor = piece_ref[:, :cols]
    rank = factor.shape[0]
    device = lax.axis_index("tp")
    gain = gain_block(gain_ref, 0, cols)
    for index in range(1, 2 * chips):
        gain = jnp.where(device == index, gain_block(gain_ref, index, cols), gain)
    gained = hidden.astype(jnp.float32) * gain
    low = dot_rows(gained.astype(jnp.bfloat16), factor)
    folded = fold(low)
    for chip in range(chips):
        for j in range(cols // LANES):
            part = hidden[:, j * LANES : (j + 1) * LANES]
            payload_out[chip, j * rows : (j + 1) * rows, :] = part
        payload_out[chip, -rank:, :] = folded


def down_copies(down_ref, held, sem, side, start=0):
    cols = held.shape[2]

    def copy(k):
        part = pl.ds(pl.multiple_of((2 * (k + start) + side) * cols, LANES), cols)
        return pltpu.make_async_copy(down_ref.at[:, part], held.at[k], sem.at[k])

    return copy


def half_products(block_ref, gain_ref, gate_ref, up_ref, side, rows, cols):
    gate = up = None
    for chip in range(block_ref.shape[0]):
        gain = jnp.where(
            side == 0, gain_block(gain_ref, 2 * chip, cols), gain_block(gain_ref, 2 * chip + 1, cols)
        )
        left = (features(block_ref, chip, rows, cols) * gain).astype(jnp.bfloat16)
        part = pl.ds(pl.multiple_of((2 * chip + side) * cols, cols), cols)
        gate_part = dot(left, gate_ref[part, :])
        up_part = dot(left, up_ref[part, :])
        gate = gate_part if gate is None else gate + gate_part
        up = up_part if up is None else up + up_part
    return gate, up


def near_kernel(
    mine_ref, gain_ref, gate_ref, up_ref, down_ref, gate_out, up_out, held_out, sem
):
    core = core_index()
    count, _, cols = held_out.shape
    copy = down_copies(down_ref, held_out, sem, 1 - core)

    @pl.loop(0, count)
    def _(k):
        copy(k).start()

    gate, up = half_products(
        mine_ref, gain_ref, gate_ref, up_ref, core, gate_out.shape[0], cols
    )
    gate_out[...] = gate
    up_out[...] = up

    @pl.loop(0, count)
    def _(k):
        copy(k).wait()


def forward_kernel(
    mine_ref, theirs_ref, gain_ref, lift_ref, gate_part, up_part, early_ref, gate_ref, up_ref,
    down_ref, active_out, theirs_out, held_out, held, sem, sem_out,
):
    chips, rows, cols = theirs_out.shape
    core = core_index()
    rank = lift_ref.shape[0]
    early = early_ref.shape[0]
    first = down_copies(down_ref, held, sem, 1 - core, early)
    second = down_copies(down_ref, held_out, sem_out, core)

    @pl.loop(0, chips - early)
    def _(k):
        first(k).start()

    @pl.loop(0, chips)
    def _(k):
        second(k).start()

    gate, up = half_products(theirs_ref, gain_ref, gate_ref, up_ref, 1 - core, rows, cols)
    squares = jnp.zeros((rows, cols), jnp.float32)
    folded = jnp.zeros((rank, LANES), jnp.float32)
    for chip in range(chips):
        for ref in (mine_ref, theirs_ref):
            wide = features(ref, chip, rows, cols)
            squares = squares + wide * wide
            folded = folded + ref[chip, -rank:, :].astype(jnp.float32)
    mean_sq = jnp.sum(squares, axis=-1, keepdims=True) / (2 * chips * cols)
    scale = lax.rsqrt(mean_sq + EPS)
    low = (unfold(folded) * scale).astype(jnp.bfloat16)
    gate = (gate + gate_part[...]) * scale
    upper = (up + up_part[...]) * scale + dot(low, lift_ref[...])
    active_out[...] = (gate * jax.nn.sigmoid(gate) * upper).astype(jnp.bfloat16)

    for k in range(early):
        theirs_out[k] = dot(active_out[...], early_ref[k]).astype(theirs_out.dtype)

    @pl.loop(0, chips - early)
    def _(k):
        first(k).wait()

    for k in range(chips - early):
        theirs_out[k + early] = dot(active_out[...], held[k]).astype(theirs_out.dtype)

    @pl.loop(0, chips)
    def _(k):
        second(k).wait()


def last_kernel(active_ref, held_ref, mine_out):
    for chip in range(mine_out.shape[0]):
        mine_out[chip] = dot(active_ref[...], held_ref[chip])


def fast_body(
    tokens,
    attention_gain,
    forward_gain,
    query_weight,
    key_matrix,
    value_matrix,
    output_weight,
    gate_weight,
    up_weight,
    down_weight,
    adapter_inputs,
    adapter_query,
    adapter_upper,
    adapter_place,
    request_adapter,
    tree_parents,
):
    rows, cols = tokens.shape
    chips = lax.axis_size("tp") // 2
    width = query_weight.shape[0]
    shape = jax.ShapeDtypeStruct
    bf16, f32 = jnp.bfloat16, jnp.float32
    tall = rows * cols // LANES + adapter_query.shape[1]
    heavy = (gate_weight, up_weight, down_weight)
    most = heavy + (query_weight, output_weight)
    rank = adapter_query.shape[1]
    factors = adapter_inputs[0].T

    spread_tokens, kept_tokens, gain_one, gain_two, parents = spread(
        tokens,
        (attention_gain.reshape(-1, LANES), forward_gain.reshape(-1, LANES), tree_parents),
        heavy,
        chips,
    )
    mine = exchange(spread_tokens, "tp")
    mine, held = lax.optimization_barrier((mine, adapter_inputs))
    theirs = partner_2(mine, "tp", 0)
    factors_theirs = partner_2(held, "tp", 0)[0].T
    query_lift, up_lift, owner, cosine, sine, reach = tables(
        request_adapter, adapter_place, (adapter_query, adapter_upper), parents, mine
    )
    normed, pair, payload = call(
        project_kernel,
        "project",
        (
            shape((rows, width), bf16),
            shape((rows, 2 * key_matrix.shape[1]), bf16),
            shape((chips, rank, cols + LANES), bf16),
        ),
        (mine, theirs, gain_one, owner, factors_theirs),
        (key_matrix.T, value_matrix.T, factors),
    )
    pair_theirs = partner_2(pair, "tp", 0)
    (query,) = call(
        query_kernel,
        "query",
        (shape((rows, query_weight.shape[1]), f32),),
        (normed,),
        (query_weight,),
        heavy,
    )
    pair_theirs, query, payload = lax.optimization_barrier((pair_theirs, query, payload))
    got = exchange(payload, "tp")
    mixed, sent = call(
        attend_kernel,
        "attend",
        (
            shape((rows, query_weight.shape[1]), bf16),
            shape((chips, rows, cols), bf16),
        ),
        (
            query, pair, pair_theirs, owner, got, query_lift, cosine,
            sine, reach,
        ),
        (output_weight,),
        heavy + (query_weight,),
    )
    sent_theirs = partner_2(sent, "tp", 0)
    kept, piece = call(
        rest_kernel,
        "rest",
        (shape((chips, rows, cols), f32), shape((rank, cols), bf16)),
        (mixed, owner, got),
        (output_weight,),
    )
    chip_sum = (kept + sent_theirs.astype(f32)).astype(bf16)
    hidden, payload = call(
        hidden_kernel,
        "hidden",
        (shape((rows, cols), bf16), shape((chips, tall, LANES), bf16)),
        (exchange(chip_sum, "tp"), kept_tokens, gain_two, piece),
        (),
        most,
    )
    mine = exchange(payload, "tp")
    theirs = partner_2(mine, "tp", 0)
    held = shape((chips, down_weight.shape[0], cols), bf16)
    half = chips // 2
    part = shape((rows, gate_weight.shape[1]), f32)
    gate_part, up_part, early = call(
        near_kernel,
        "near",
        (part, part, shape((half, *held.shape[1:]), bf16)),
        (mine, gain_two),
        (gate_weight, up_weight),
        (),
        [pltpu.SemaphoreType.DMA((half,))],
        far=(down_weight,),
        limit=8,
    )
    active, sent, held_mine = call(
        forward_kernel,
        "forward",
        (shape(part.shape, bf16), shape((chips, rows, cols), bf16), held),
        (mine, theirs, gain_two, up_lift, gate_part, up_part, early),
        (gate_weight, up_weight),
        (),
        [
            VMEM((chips - half, *held.shape[1:]), bf16),
            pltpu.SemaphoreType.DMA((chips - half,)),
            pltpu.SemaphoreType.DMA((chips,)),
        ],
        far=(down_weight,),
        limit=8,
    )
    sent_theirs = partner_2(sent, "tp", 0)
    (kept,) = call(
        last_kernel, "last", (shape((chips, rows, cols), f32),), (active, held_mine)
    )
    chip_sum = (kept + sent_theirs.astype(f32)).astype(bf16)
    added = jnp.sum(exchange(chip_sum, "tp").astype(f32), axis=0)
    return (hidden.astype(f32) + added).astype(bf16)


def body(*args):
    tokens, key_matrix, query_weight = args[0], args[4], args[3]
    fits = (
        tokens.shape[1] % LANES == 0
        and query_weight.shape[1] % HEAD_SIZE == 0
        and key_matrix.shape[1] * 2 == HEAD_SIZE
        and args[10].shape[0] == 1
        and args[14].shape[0] == 1
        and args[10].shape[2] == tokens.shape[0]
    )
    return fast_body(*args) if fits else general_body(*args)


def solution(mesh):
    return jax.shard_map(
        body,
        mesh=mesh,
        in_specs=(
            P("rep", "tp"),
            P(),
            P(),
            P(None, "tp"),
            P(None, "tp"),
            P(None, "tp"),
            P("tp", None),
            P(None, "tp"),
            P(None, "tp"),
            P("tp", None),
            P(("rep", "tp"), None, None),
            P("rep", None, "tp"),
            P("rep", None, "tp"),
            P("rep"),
            P("rep"),
            P("rep", None),
        ),
        out_specs=P("rep", "tp"),
        check_vma=False,
    )
```
